32 devices in a mesh: win: 8 (over z, core), seq: 4 (over y, x).
Axes of the slice: x: 2, y: 2, z: 4, core: 2. Of those that a mesh axis runs over, the one named last changes fastest.
Arguments:
- inputs: bfloat16 [8, 1536, 1536], P('win', 'seq'), may hold values from -6 to 6
- cotangent: bfloat16 [8, 1536, 1536], P('win', 'seq'), may hold values from -6 to 6
- ln1_scale: bfloat16 [1536], P(('win', 'seq')), may hold values from 0.5 to 1.5
- ln1_offset: bfloat16 [1536], P(('win', 'seq')), may hold values from -4 to 4
- w_query: bfloat16 [1536, 512], P(('win', 'seq')), may hold values from -0.15625 to 0.15625
- w_key: bfloat16 [1536, 512], P(('win', 'seq')), may hold values from -0.15625 to 0.15625
- w_value: bfloat16 [1536, 1536], P(('win', 'seq')), may hold values from -0.15625 to 0.15625
- w_rel: bfloat16 [192, 512], P(None, ('win', 'seq')), may hold values from -0.4375 to 0.4375
- content_bias: bfloat16 [512], P(('win', 'seq')), may hold values from -0.875 to 0.875
- position_bias: bfloat16 [512], P(('win', 'seq')), may hold values from -0.875 to 0.875
- w_out: bfloat16 [1536, 1536], P(('win', 'seq')), may hold values from -1.75 to 1.75
- b_out: bfloat16 [1536], P(('win', 'seq')), may hold values from -4 to 4
- ln2_scale: bfloat16 [1536], P(('win', 'seq')), may hold values from 0.5 to 1.5
- ln2_offset: bfloat16 [1536], P(('win', 'seq')), may hold values from -4 to 4
- w_in: bfloat16 [1536, 3072], P(('win', 'seq')), may hold values from -0.15625 to 0.15625
- b_in: bfloat16 [3072], P(('win', 'seq')), may hold values from -4 to 4
- w_mlp_out: bfloat16 [3072, 1536], P(('win', 'seq')), may hold values from -0.109375 to 0.109375
- b_mlp_out: bfloat16 [1536], P(('win', 'seq')), may hold values from -4 to 4
Outputs:
- layer_out: bfloat16 [8, 1536, 1536], P('win', 'seq')
- grad_inputs: float32 [8, 1536, 1536], P('win', 'seq')
- grad_ln1_scale: float32 [1536], P(('win', 'seq'))
- grad_ln1_offset: float32 [1536], P(('win', 'seq'))
- grad_w_query: float32 [1536, 512], P(('win', 'seq'))
- grad_w_key: float32 [1536, 512], P(('win', 'seq'))
- grad_w_value: float32 [1536, 1536], P(('win', 'seq'))
- grad_w_rel: float32 [192, 512], P(None, ('win', 'seq'))
- grad_content_bias: float32 [512], P(('win', 'seq'))
- grad_position_bias: float32 [512], P(('win', 'seq'))
- grad_w_out: float32 [1536, 1536], P(('win', 'seq'))
- grad_b_out: float32 [1536], P(('win', 'seq'))
- grad_ln2_scale: float32 [1536], P(('win', 'seq'))
- grad_ln2_offset: float32 [1536], P(('win', 'seq'))
- grad_w_in: float32 [1536, 3072], P(('win', 'seq'))
- grad_b_in: float32 [3072], P(('win', 'seq'))
- grad_w_mlp_out: float32 [3072, 1536], P(('win', 'seq'))
- grad_b_mlp_out: float32 [1536], P(('win', 'seq'))
The draws below stay inside these ranges and needn't reach their ends.
All inputs are finite; a program needn't handle non-finite values.
Results may differ from the reference program's by a relative error of at most 0.03.
Values may be sent and summed in bfloat16 or wider, within the bound.
A program may use at most 256 MiB of HBM per device.

```python
import math
from functools import partial
import jax
import jax.numpy as jnp
from jax import lax

D = 1536
HEADS = 8
KD = 64
FF = 3072
F = 192
WLEN = 1536
HK = 512
WINDOWS = 8


def block_scale(rng, dims, pieces, low, high):
    loudness, own = 1.0, jax.random.fold_in(rng, 6)
    for dim, blocks in pieces:
        heights = jnp.exp(jax.random.uniform(jax.random.fold_in(own, dim), (blocks,), jnp.float32, low / len(pieces), high / len(pieces)))
        loudness = loudness * jnp.repeat(heights, dims[dim] // blocks).reshape([-1 if axis == dim else 1 for axis in range(len(dims))])
    return loudness


def scatter_about(key, shape, deviation, bound, split=(), held_as=jnp.bfloat16):
    values = deviation * jax.random.normal(key, shape, jnp.float32)
    if split:
        values = values * block_scale(key, shape, split, -0.22, 0.18)
    return jnp.clip(values, -bound, bound).astype(held_as)


def setup_inputs(seed: int = 0) -> dict:
    splits = jax.random.split(jax.random.key(seed), 19)
    return {
        "inputs": scatter_about(splits[0], (WINDOWS, WLEN, D), 1.0, 6.0, ((0, 8), (1, 4))),
        "cotangent": scatter_about(splits[1], (WINDOWS, WLEN, D), 1.0, 6.0, ((0, 8), (1, 4))),
        "ln1_scale": jnp.clip(1.0 + 0.1 * jax.random.normal(splits[2], (D,), jnp.float32), 0.5, 1.5).astype(jnp.bfloat16),
        "ln1_offset": scatter_about(splits[3], (D,), 0.3, 4.0, ((0, 32),)),
        "w_query": scatter_about(splits[4], (D, HK), D ** -0.5, 0.15625, ((0, 32),)),
        "w_key": scatter_about(splits[5], (D, HK), D ** -0.5, 0.15625, ((0, 32),)),
        "w_value": scatter_about(splits[6], (D, D), D ** -0.5, 0.15625, ((0, 32),)),
        "w_rel": scatter_about(splits[7], (F, HK), F ** -0.5, 0.4375, ((1, 32),)),
        "content_bias": scatter_about(splits[8], (HK,), 0.06, 0.875, ((0, 32),)),
        "position_bias": scatter_about(splits[9], (HK,), 0.06, 0.875, ((0, 32),)),
        "w_out": scatter_about(splits[10], (D, D), (max(D // 128, 1)) ** -0.5, 1.75, ((0, 32),)),
        "b_out": scatter_about(splits[11], (D,), 0.3, 4.0, ((0, 32),)),
        "ln2_scale": jnp.clip(1.0 + 0.1 * jax.random.normal(splits[12], (D,), jnp.float32), 0.5, 1.5).astype(jnp.bfloat16),
        "ln2_offset": scatter_about(splits[13], (D,), 0.3, 4.0, ((0, 32),)),
        "w_in": scatter_about(splits[14], (D, FF), D ** -0.5, 0.15625, ((0, 32),)),
        "b_in": scatter_about(splits[15], (FF,), 0.3, 4.0, ((0, 32),)),
        "w_mlp_out": scatter_about(splits[16], (FF, D), FF ** -0.5, 0.109375, ((0, 32),)),
        "b_mlp_out": scatter_about(splits[17], (D,), 0.3, 4.0, ((0, 32),)),
    }


@jax.custom_vjp
def low(v):
    return lax.optimization_barrier(v.astype(jnp.bfloat16)).astype(jnp.float32)

@jax.custom_vjp
def low_back(v):
    return v

def low_keep(v):
    return (low(v), None)

def low_pass(kept, grad):
    return (grad,)

def back_keep(v):
    return (v, None)

def back_low(kept, grad):
    return (low(grad),)
low.defvjp(low_keep, low_pass)
low_back.defvjp(back_keep, back_low)

def accurate(former, latter):
    return jnp.dot(former, latter, precision=lax.Precision.HIGHEST)

def rel_features(length, feature_count):
    per_basis = feature_count // 6
    offsets = jnp.arange(-length + 1, length).astype(jnp.float32)
    magnitude = jnp.abs(offsets)[:, None]
    half_life = 2.0 ** jnp.linspace(3.0, math.log2(length), per_basis)
    decaying = jnp.exp(-math.log(2.0) / half_life * magnitude)
    widths = 2.0 ** jnp.arange(1, per_basis + 1).astype(jnp.float32) - 1.0
    central = (widths > magnitude).astype(jnp.float32)
    stddev = length / (2.0 * per_basis)
    centers = jnp.linspace(length / per_basis, float(length), per_basis)
    shape_param = (centers / stddev) ** 2
    inverse_scale = centers / stddev ** 2
    peak_at = (shape_param - 1.0) / inverse_scale
    log_prob = (shape_param - 1.0) * (jnp.log(jnp.maximum(magnitude, 0.5)) - jnp.log(peak_at)) - inverse_scale * (magnitude - peak_at)
    density = jnp.exp(log_prob) + 1e-08
    gamma_pdf = density / lax.optimization_barrier(jnp.max(density, axis=0, keepdims=True))
    basis_set = jnp.concatenate([decaying, central, gamma_pdf], axis=1)
    return jnp.concatenate([basis_set, jnp.sign(offsets)[:, None] * basis_set], axis=1)

def layer_norm(values, norm_gain, norm_shift):
    centered = values - lax.optimization_barrier(jnp.mean(values, axis=-1, keepdims=True))
    variance = lax.optimization_barrier(jnp.mean(centered * centered, axis=-1, keepdims=True))
    return centered * lax.rsqrt(variance + 1e-05) * norm_gain + norm_shift

def shift_rows(relative, row_count, col_count):
    row_width = row_count + col_count - 1
    leading = relative.shape[:-2]
    flattened = relative.reshape(leading + (row_count * row_width,))
    trimmed = flattened[..., row_count - 1:row_count - 1 + row_count * (row_width - 1)]
    return trimmed.reshape(leading + (row_count, row_width - 1))[..., :col_count]

def window_layer(params, table, window):
    ln1_scale, ln1_offset, w_query, w_key, w_value, content_bias, position_bias, w_out, b_out, ln2_scale, ln2_offset, w_in, b_in, w_mlp_out, b_mlp_out = params
    length = window.shape[0]
    normed = low(layer_norm(window, ln1_scale, ln1_offset))
    query = low_back(accurate(normed, w_query)) * KD ** (-0.5)
    keys = low_back(low(accurate(normed, w_key))).reshape(length, HEADS, KD)
    values = low_back(low(accurate(normed, w_value))).reshape(length, HEADS, -1)
    query_content = low(query + content_bias).reshape(length, HEADS, KD)
    query_position = low(query + position_bias).reshape(length, HEADS, KD)
    content = jnp.einsum('ihk,jhk->hij', query_content, keys, precision=lax.Precision.HIGHEST)
    relative = jnp.einsum('ihk,chk->hic', query_position, table, precision=lax.Precision.HIGHEST)
    scores = low_back(content + shift_rows(relative, length, length))
    attention = low(jax.nn.softmax(scores, axis=-1))
    mixed = jnp.einsum('hij,jhd->ihd', attention, values, precision=lax.Precision.HIGHEST).reshape(length, -1)
    attended = low_back(low(mixed))
    branch = low_back(accurate(attended, w_out) + b_out)
    hidden_in = window + branch
    normed_two = low(layer_norm(hidden_in, ln2_scale, ln2_offset))
    pre_act = low_back(accurate(normed_two, w_in) + b_in)
    return hidden_in + accurate(low(jax.nn.gelu(pre_act)), w_mlp_out) + b_mlp_out

def reference(inputs, cotangent, ln1_scale, ln1_offset, w_query, w_key, w_value, w_rel, content_bias, position_bias, w_out, b_out, ln2_scale, ln2_offset, w_in, b_in, w_mlp_out, b_mlp_out):
    params = tuple((weight.astype(jnp.float32) for weight in (ln1_scale, ln1_offset, w_query, w_key, w_value, w_rel, content_bias, position_bias, w_out, b_out, ln2_scale, ln2_offset, w_in, b_in, w_mlp_out, b_mlp_out)))
    features = low(rel_features(WLEN, F))

    def forward(source, weights):
        table = low(accurate(features, weights[5])).reshape(2 * WLEN - 1, HEADS, KD)
        others = weights[:5] + weights[6:]
        layer = jax.checkpoint(partial(window_layer, others, table))
        return lax.map(layer, source)
    result, pullback = jax.vjp(forward, inputs.astype(jnp.float32), params)
    grad_inputs, grads = pullback(cotangent.astype(jnp.float32))
    return (result.astype(jnp.bfloat16), grad_inputs, grads[0], grads[1], grads[2], grads[3], grads[4], grads[5], grads[6], grads[7], grads[8], grads[9], grads[10], grads[11], grads[12], grads[13], grads[14], grads[15])
```

```python
import functools
import math

import jax
import jax.numpy as jnp
from jax import lax
from jax.experimental import pallas as pl
from jax.experimental.pallas import tpu as pltpu
from jax.sharding import PartitionSpec as P

HEADS = 8
KD = 64
F = 192
WLEN = 1536
CORES = 2
BLOCK_Q = 256
bfloat = jnp.bfloat16
single = jnp.float32


def rel_features(length, feature_count):
    per_basis = feature_count // 6
    offsets = jnp.arange(-length + 1, length).astype(jnp.float32)
    magnitude = jnp.abs(offsets)[:, None]
    half_life = 2.0 ** jnp.linspace(3.0, math.log2(length), per_basis)
    decaying = jnp.exp(-math.log(2.0) / half_life * magnitude)
    widths = 2.0 ** jnp.arange(1, per_basis + 1).astype(jnp.float32) - 1.0
    central = (widths > magnitude).astype(jnp.float32)
    stddev = length / (2.0 * per_basis)
    centers = jnp.linspace(length / per_basis, float(length), per_basis)
    shape_param = (centers / stddev) ** 2
    inverse_scale = centers / stddev**2
    peak_at = (shape_param - 1.0) / inverse_scale
    log_prob = (shape_param - 1.0) * (
        jnp.log(jnp.maximum(magnitude, 0.5)) - jnp.log(peak_at)
    ) - inverse_scale * (magnitude - peak_at)
    density = jnp.exp(log_prob) + 1e-08
    gamma_pdf = density / jnp.max(density, axis=0, keepdims=True)
    basis_set = jnp.concatenate([decaying, central, gamma_pdf], axis=1)
    return jnp.concatenate([basis_set, jnp.sign(offsets)[:, None] * basis_set], axis=1)


def layer_norm(values, norm_gain, norm_shift):
    centered = values - jnp.mean(values, axis=-1, keepdims=True)
    variance = jnp.mean(centered * centered, axis=-1, keepdims=True)
    return centered * lax.rsqrt(variance + 1e-05) * norm_gain + norm_shift


def fwd_kernel(L, bq, hp, vd, x_ref, tab_ref, att_ref, out_ref):
    qi = pl.program_id(0)
    hk = hp * KD
    i0 = pl.multiple_of(qi * bq, bq)
    a = pl.multiple_of(L - bq - i0, bq)
    W = L + bq
    outs = []
    for h in range(hp):
        qc = x_ref[pl.ds(i0, bq), pl.ds(h * KD, KD)]
        qp = x_ref[pl.ds(i0, bq), pl.ds(hk + h * KD, KD)]
        k = x_ref[:, pl.ds(2 * hk + h * KD, KD)]
        v = x_ref[:, pl.ds(3 * hk + h * vd, vd)]
        raw = jnp.dot(qp, tab_ref[pl.ds(h * KD, KD), pl.ds(a, W)], preferred_element_type=jnp.float32)
        rel = pltpu.roll(raw, W - bq + 1, 1, stride=1, stride_axis=0)[:, :L]
        s = rel + lax.dot_general(qc, k, (((1,), (1,)), ((), ())), preferred_element_type=jnp.float32)
        m = jnp.max(s, axis=-1, keepdims=True)
        e = jnp.exp(s - m)
        inv = 1.0 / jnp.sum(e, axis=-1, keepdims=True)
        att = (e * inv).astype(jnp.bfloat16)
        att_ref[h] = att
        outs.append(jnp.dot(att, v, preferred_element_type=jnp.float32).astype(jnp.bfloat16))
    out_ref[...] = jnp.concatenate(outs, axis=1) if hp > 1 else outs[0]

def attention_forward(x, tab, hp, vd, bq):
    L = x.shape[0]
    return pl.pallas_call(
        functools.partial(fwd_kernel, L, bq, hp, vd),
        grid=(L // bq,),
        in_specs=[pl.BlockSpec(x.shape, lambda i: (0, 0)), pl.BlockSpec(tab.shape, lambda i: (0, 0))],
        out_specs=[pl.BlockSpec((hp, bq, L), lambda i: (0, i, 0)), pl.BlockSpec((bq, hp * vd), lambda i: (i, 0))],
        out_shape=[jax.ShapeDtypeStruct((hp, L, L), jnp.bfloat16), jax.ShapeDtypeStruct((L, hp * vd), jnp.bfloat16)],
        compiler_params=pltpu.CompilerParams(vmem_limit_bytes=56 * 2**20),
    )(x, tab)

def bwd_kernel(L, bq, hp, vd, x_ref, tab_ref, att_ref, gm_ref, dq_ref, dkv_ref, dtab_ref, bias_ref, dkT, dvT):
    qi = pl.program_id(0)
    hk = hp * KD
    i0 = pl.multiple_of(qi * bq, bq)
    a = pl.multiple_of(L - bq - i0, bq)
    W = L + bq

    @pl.when(qi == 0)
    def _():
        dkT[...] = jnp.zeros_like(dkT)
        dvT[...] = jnp.zeros_like(dvT)
        dtab_ref[...] = jnp.zeros_like(dtab_ref)
        bias_ref[...] = jnp.zeros_like(bias_ref)

    row = lax.broadcasted_iota(jnp.int32, (bq, bq), 0)
    col = lax.broadcasted_iota(jnp.int32, (bq, bq), 1)
    flip = jnp.where(row + col == bq - 1, 1.0, 0.0).astype(jnp.bfloat16)

    def flipped(v):
        return jnp.dot(flip, v, preferred_element_type=jnp.float32)

    dqs, bc, bp = [], [], []
    for h in range(hp):
        qc = flipped(x_ref[pl.ds(i0, bq), pl.ds(h * KD, KD)]).astype(jnp.bfloat16)
        qp = flipped(x_ref[pl.ds(i0, bq), pl.ds(hk + h * KD, KD)]).astype(jnp.bfloat16)
        k = x_ref[:, pl.ds(2 * hk + h * KD, KD)]
        v = x_ref[:, pl.ds(3 * hk + h * vd, vd)]
        gm = gm_ref[:, pl.ds(h * vd, vd)]
        att = att_ref[h]
        dvT[pl.ds(h * vd, vd), :] += lax.dot_general(gm, att, (((0,), (0,)), ((), ())), preferred_element_type=jnp.float32)
        gmr = flipped(gm).astype(jnp.bfloat16)
        dp = lax.dot_general(gmr, v, (((1,), (1,)), ((), ())), preferred_element_type=jnp.float32)
        af = flipped(att)
        t = af * dp
        delta = jnp.sum(t, axis=-1, keepdims=True)
        ds = (t - af * delta).astype(jnp.bfloat16)
        dkT[pl.ds(h * KD, KD), :] += lax.dot_general(qc, ds, (((0,), (0,)), ((), ())), preferred_element_type=jnp.float32)
        gc = jnp.dot(ds, k, preferred_element_type=jnp.float32)
        wide = jnp.concatenate([ds.astype(jnp.float32), jnp.zeros((bq, bq), jnp.float32)], axis=1)
        rel = pltpu.roll(wide, 0, 1, stride=1, stride_axis=0).astype(jnp.bfloat16)
        tab = tab_ref[pl.ds(h * KD, KD), pl.ds(a, W)]
        gp = lax.dot_general(rel, tab, (((1,), (1,)), ((), ())), preferred_element_type=jnp.float32)
        dtab_ref[pl.ds(h * KD, KD), pl.ds(a, W)] += lax.dot_general(qp, rel, (((0,), (0,)), ((), ())), preferred_element_type=jnp.float32)
        dqs.append(flipped(((gc + gp) * KD ** -0.5).astype(jnp.bfloat16)).astype(jnp.bfloat16))
        bc.append(jnp.sum(gc, axis=0, keepdims=True))
        bp.append(jnp.sum(gp, axis=0, keepdims=True))
    dq_ref[...] = jnp.concatenate(dqs, axis=1) if hp > 1 else dqs[0]
    bias_ref[0:1, :] += jnp.concatenate(bc, axis=1) if hp > 1 else bc[0]
    bias_ref[1:2, :] += jnp.concatenate(bp, axis=1) if hp > 1 else bp[0]

    @pl.when(qi == pl.num_programs(0) - 1)
    def _():
        dkv_ref[:, :hk] = dkT[...].T.astype(jnp.bfloat16)
        dkv_ref[:, hk:] = dvT[...].T.astype(jnp.bfloat16)

def attention_backward(x, tab, att, gm, hp, vd, bq):
    L = x.shape[0]
    hk = hp * KD
    return pl.pallas_call(
        functools.partial(bwd_kernel, L, bq, hp, vd),
        grid=(L // bq,),
        in_specs=[pl.BlockSpec(x.shape, lambda i: (0, 0)), pl.BlockSpec(tab.shape, lambda i: (0, 0)),
                  pl.BlockSpec((hp, bq, L), lambda i: (0, i, 0)), pl.BlockSpec((bq, hp * vd), lambda i: (i, 0))],
        out_specs=[pl.BlockSpec((bq, hk), lambda i: (i, 0)), pl.BlockSpec((L, hk + hp * vd), lambda i: (0, 0)),
                   pl.BlockSpec(tab.shape, lambda i: (0, 0)), pl.BlockSpec((8, hk), lambda i: (0, 0))],
        out_shape=[jax.ShapeDtypeStruct((L, hk), jnp.bfloat16), jax.ShapeDtypeStruct((L, hk + hp * vd), jnp.bfloat16),
                   jax.ShapeDtypeStruct(tab.shape, jnp.float32), jax.ShapeDtypeStruct((8, hk), jnp.float32)],
        scratch_shapes=[pltpu.VMEM((hk, L), jnp.float32), pltpu.VMEM((hp * vd, L), jnp.float32)],
        compiler_params=pltpu.CompilerParams(vmem_limit_bytes=56 * 2**20),
    )(x, tab, att, gm)


def pick(stacked, index, axis):
    return lax.dynamic_index_in_dim(stacked, index, axis, keepdims=False)


def place(stacked, piece, index, axis):
    return lax.dynamic_update_slice_in_dim(stacked, jnp.expand_dims(piece, axis), index, axis)


def swap_cores(value):
    size = lax.axis_size("win")
    return lax.ppermute(value, "win", [(i, i ^ 1) for i in range(size)])


def swap_seq(value, distance):
    size = lax.axis_size("seq")
    return lax.ppermute(value, "seq", [(i, i ^ distance) for i in range(size)])


def move_chips(value, direction, first):
    size = lax.axis_size("win")
    chips = size // CORES
    if direction > 0:
        pairs = [(i, i + CORES) for i in range(size - CORES) if i // CORES >= first]
    else:
        pairs = [(i, i - CORES) for i in range(CORES, size) if i // CORES < chips - first]
    return lax.ppermute(value, "win", pairs)


def gather_chips(shard):
    chips = lax.axis_size("win") // CORES
    here = lax.axis_index("win") // CORES
    out = place(jnp.zeros((chips,) + shard.shape, shard.dtype), shard, here, 0)
    above, below = [shard], [shard]
    for step in range(1, chips):
        below.append(move_chips(below[-1], 1, step - 1))
        above.append(move_chips(above[-1], -1, step - 1))
    for step in range(1, chips):
        piece = jnp.where(here + step < chips, above[step], below[chips - step])
        out = place(out, piece, (here + step) % chips, 0)
    return out


def gather_seq(value, axis, rising):
    size = lax.axis_size("seq")
    here = lax.axis_index("seq")
    bits = [1 << b for b in range(size.bit_length() - 1)]
    shape = value.shape
    lead, tail = shape[:axis], shape[axis:]
    value = value.reshape(lead + (1,) * len(bits) + tail)
    for bit in bits if rising else bits[::-1]:
        at = axis + len(bits) - bit.bit_length()
        other = swap_seq(value, bit)
        own_low = (here & bit) == 0
        value = jnp.concatenate(
            [jnp.where(own_low, value, other), jnp.where(own_low, other, value)], axis=at
        )
    return value.reshape(lead + (size,) + tail)


def gather_cores(value, axis):
    other = swap_cores(value)
    first = lax.axis_index("win") % CORES == 0
    return jnp.stack([jnp.where(first, value, other), jnp.where(first, other, value)], axis=axis)


def gather(shard, rising):
    value = gather_chips(shard)
    value = gather_seq(value, 1, rising)
    return gather_cores(value, 1)


def total(first, *others):
    result = first.astype(single)
    for other in others:
        result = result + other.astype(single)
    return result


def scatter_cores(value, axis):
    core = lax.axis_index("win") % CORES
    arrived = swap_cores(pick(value, 1 - core, axis))
    return total(pick(value, core, axis), arrived).astype(value.dtype)


def scatter_seq(value, axis, rising):
    size = lax.axis_size("seq")
    here = lax.axis_index("seq")
    bits = [1 << b for b in range(size.bit_length() - 1)]
    shape = value.shape
    lead, tail = shape[:axis], shape[axis + 1 :]
    value = value.reshape(lead + (2,) * len(bits) + tail)
    for bit in bits[::-1] if rising else bits:
        at = axis + len(bits) - bit.bit_length()
        mine = (here & bit) // bit
        arrived = swap_seq(lax.dynamic_slice_in_dim(value, 1 - mine, 1, at), bit)
        value = total(lax.dynamic_slice_in_dim(value, mine, 1, at), arrived).astype(value.dtype)
    return value.reshape(lead + tail)


def scatter_chips(value):
    chips = lax.axis_size("win") // CORES
    here = lax.axis_index("win") // CORES
    from_below = from_above = None
    for step in range(chips - 1, 0, -1):
        up = pick(value, jnp.minimum(here + step, chips - 1), 0)
        down = pick(value, jnp.maximum(here - step, 0), 0)
        if from_below is not None:
            up = total(up, from_below).astype(value.dtype)
            down = total(down, from_above).astype(value.dtype)
        from_below = move_chips(up, 1, 0)
        from_above = move_chips(down, -1, 0)
    return total(pick(value, here, 0), from_below, from_above)


def scatter(value, rising):
    value = scatter_cores(value, 1)
    value = scatter_seq(value, 1, rising)
    return scatter_chips(value)


def exchange(blocks):
    size = lax.axis_size("seq")
    here = lax.axis_index("seq")
    out = place(jnp.zeros(blocks.shape, blocks.dtype), pick(blocks, here, 0), here, 0)
    for distance in range(1, size):
        peer = here ^ distance
        out = place(out, swap_seq(pick(blocks, peer, 0), distance), peer, 0)
    return out


def shards(
    inputs,
    cotangent,
    ln1_scale,
    ln1_offset,
    w_query,
    w_key,
    w_value,
    w_rel,
    content_bias,
    position_bias,
    w_out,
    b_out,
    ln2_scale,
    ln2_offset,
    w_in,
    b_in,
    w_mlp_out,
    b_mlp_out,
):
    win_size, seq_size = lax.axis_size("win"), lax.axis_size("seq")
    devices = win_size * seq_size
    grid = (win_size // CORES, CORES, seq_size)
    seq = lax.axis_index("seq")
    window_count, row_count, width = inputs.shape
    tokens = window_count * row_count
    hk = HEADS * KD
    vd = width // HEADS
    hp = HEADS // seq_size
    hidden = w_in.shape[1]
    scale_factor = KD ** (-0.5)

    vectors = (
        ln1_scale,
        ln1_offset,
        content_bias,
        position_bias,
        b_out,
        ln2_scale,
        ln2_offset,
        b_in,
        b_mlp_out,
    )
    packed = jnp.concatenate(vectors + (w_rel.T.reshape(-1),))
    packed_size = packed.shape[0]
    lines = -(-packed_size // 512) * 4
    packed = jnp.pad(packed, (0, lines * 128 - packed_size)).reshape(lines, 128)
    packed = gather(packed, True).reshape(devices, lines * 128)
    whole_vectors = []
    at = 0
    for vector in vectors:
        length = vector.shape[0]
        whole_vectors.append(packed[:, at : at + length].reshape(devices * length).astype(single))
        at += length
    whole_rel = packed[:, at:packed_size].reshape(hk, F)
    (
        ln1_gain,
        ln1_shift,
        bias_content,
        bias_position,
        bias_out,
        ln2_gain,
        ln2_shift,
        bias_in,
        bias_mlp,
    ) = whole_vectors

    whole_qk = gather(jnp.concatenate([w_query, w_key], axis=1), True).reshape(width, 2 * hk)
    whole_v = gather(w_value, False).reshape(width, width)
    whole_out = gather(w_out, True).reshape(width, width)
    whole_in = gather(w_in, False).reshape(width, hidden)
    whole_mlp = gather(w_mlp_out, True).reshape(hidden, width)

    features = jnp.pad(rel_features(WLEN, F).astype(bfloat), ((0, 1), (0, 0)))
    own_rel = lax.dynamic_slice_in_dim(whole_rel, seq * hp * KD, hp * KD, 0)
    table = jnp.einsum("cf,tf->ct", own_rel, features, preferred_element_type=single).astype(bfloat)

    source = inputs.reshape(tokens, width).astype(single)
    normed_one_f, norm_one_back = jax.vjp(layer_norm, source, ln1_gain, ln1_shift)
    normed_one = normed_one_f.astype(bfloat)
    proj_qk = jnp.dot(normed_one, whole_qk, preferred_element_type=single)
    query = proj_qk[:, :hk] * scale_factor
    proj_v = jnp.dot(normed_one, whole_v, preferred_element_type=single)
    parts = (
        (query + bias_content).astype(bfloat),
        (query + bias_position).astype(bfloat),
        proj_qk[:, hk:].astype(bfloat),
        proj_v.astype(bfloat),
    )
    outgoing = jnp.concatenate([part.reshape(tokens, seq_size, -1) for part in parts], axis=2)
    heads_in = exchange(jnp.transpose(outgoing, (1, 0, 2))).reshape(seq_size * tokens, -1)
    attention, mixed = attention_forward(heads_in, table, hp, vd, BLOCK_Q)
    attended = exchange(mixed.reshape(seq_size, tokens, hp * vd))
    attended = jnp.transpose(attended, (1, 0, 2)).reshape(tokens, width)

    hidden_in = source + jnp.dot(attended, whole_out, preferred_element_type=single) + bias_out
    normed_two_f, norm_two_back = jax.vjp(layer_norm, hidden_in, ln2_gain, ln2_shift)
    normed_two = normed_two_f.astype(bfloat)
    pre_act = jnp.dot(normed_two, whole_in, preferred_element_type=single) + bias_in
    gelu_out, gelu_back = jax.vjp(jax.nn.gelu, pre_act)
    activation = gelu_out.astype(bfloat)
    result = hidden_in + jnp.dot(activation, whole_mlp, preferred_element_type=single) + bias_mlp
    layer_out = result.astype(bfloat).reshape(inputs.shape)

    def weight_grad(left, right, rising):
        grad = jnp.einsum("td,te->de", left, right, preferred_element_type=single).astype(bfloat)
        rows, cols = grad.shape
        return scatter(grad.reshape(grid + (rows // devices, cols)), rising)

    cot_rows = cotangent.reshape(tokens, width)
    grad_mlp = weight_grad(activation, cot_rows, True)
    grad_bias_mlp = jnp.sum(cot_rows.astype(single), axis=0)
    grad_act = jnp.einsum("td,fd->tf", cot_rows, whole_mlp, preferred_element_type=single)
    grad_pre = gelu_back(grad_act)[0].astype(bfloat)
    grad_in = weight_grad(normed_two, grad_pre, False)
    grad_bias_in = jnp.sum(grad_pre.astype(single), axis=0)
    grad_normed_two = jnp.einsum("tf,df->td", grad_pre, whole_in, preferred_element_type=single)
    hidden_term, grad_ln2_gain, grad_ln2_shift = norm_two_back(grad_normed_two)
    grad_hidden = cot_rows.astype(single) + hidden_term
    grad_branch = grad_hidden.astype(bfloat)
    grad_out = weight_grad(attended, grad_branch, True)
    grad_bias_out = jnp.sum(grad_branch.astype(single), axis=0)
    grad_mixed = jnp.einsum(
        "te,de->td", grad_branch, whole_out, preferred_element_type=single
    ).astype(bfloat)
    grad_mixed = jnp.transpose(grad_mixed.reshape(tokens, seq_size, hp * vd), (1, 0, 2))
    grad_heads = exchange(grad_mixed).reshape(seq_size * tokens, hp * vd)
    grad_q, grad_kv, grad_table, grad_bias = attention_backward(
        heads_in, table, attention, grad_heads, hp, vd, BLOCK_Q
    )
    own = hp * KD
    returned = exchange(
        jnp.concatenate([grad_q, grad_kv], axis=1).reshape(seq_size, tokens, 2 * own + hp * vd)
    )
    returned = jnp.transpose(returned, (1, 0, 2))
    grad_qk_rows = jnp.concatenate(
        [
            returned[:, :, :own].reshape(tokens, hk),
            returned[:, :, own : 2 * own].reshape(tokens, hk),
        ],
        axis=1,
    )
    grad_v_rows = returned[:, :, 2 * own :].reshape(tokens, width)
    grad_qk = weight_grad(normed_one, grad_qk_rows, True)
    grad_v = weight_grad(normed_one, grad_v_rows, False)
    grad_normed_one = jnp.einsum(
        "tk,dk->td", grad_qk_rows, whole_qk, preferred_element_type=single
    ) + jnp.einsum("tk,dk->td", grad_v_rows, whole_v, preferred_element_type=single)
    source_term, grad_ln1_gain, grad_ln1_shift = norm_one_back(grad_normed_one)
    grad_inputs = (grad_hidden + source_term).reshape(inputs.shape)

    grad_rel = jnp.dot(grad_table, features.astype(single), precision=lax.Precision.HIGHEST)
    whole_grad_rel = lax.dynamic_update_slice_in_dim(
        jnp.zeros((hk, F), single), grad_rel, seq * own, 0
    )

    def spread(own_heads):
        return lax.dynamic_update_slice_in_dim(jnp.zeros((hk,), single), own_heads, seq * own, 0)

    vector_grads = (
        grad_ln1_gain,
        grad_ln1_shift,
        spread(grad_bias[0]),
        spread(grad_bias[1]),
        grad_bias_out,
        grad_ln2_gain,
        grad_ln2_shift,
        grad_bias_in,
        grad_bias_mlp,
    )
    small = jnp.concatenate(
        [v.reshape(devices, -1) for v in vector_grads + (whole_grad_rel,)], axis=1
    )
    small = jnp.pad(small, ((0, 0), (0, lines * 128 - packed_size)))
    small = scatter(small.reshape(grid + (lines, 128)), True).reshape(-1)[:packed_size]
    small_grads = []
    at = 0
    for vector in vectors:
        length = vector.shape[0]
        small_grads.append(small[at : at + length])
        at += length
    g = small_grads
    own_grad_rel = small[at:].reshape(-1, F).T
    return (
        layer_out,
        grad_inputs,
        g[0],
        g[1],
        grad_qk[:, :hk],
        grad_qk[:, hk:],
        grad_v,
        own_grad_rel,
        g[2],
        g[3],
        grad_out,
        g[4],
        g[5],
        g[6],
        grad_in,
        g[7],
        grad_mlp,
        g[8],
    )


def solution(mesh):
    in_specs = (
        P("win", "seq", None),
        P("win", "seq", None),
        P(("win", "seq")),
        P(("win", "seq")),
        P(("win", "seq"), None),
        P(("win", "seq"), None),
        P(("win", "seq"), None),
        P(None, ("win", "seq")),
        P(("win", "seq")),
        P(("win", "seq")),
        P(("win", "seq"), None),
        P(("win", "seq")),
        P(("win", "seq")),
        P(("win", "seq")),
        P(("win", "seq"), None),
        P(("win", "seq")),
        P(("win", "seq"), None),
        P(("win", "seq")),
    )
    out_specs = (
        P("win", "seq", None),
        P("win", "seq", None),
        P(("win", "seq")),
        P(("win", "seq")),
        P(("win", "seq"), None),
        P(("win", "seq"), None),
        P(("win", "seq"), None),
        P(None, ("win", "seq")),
        P(("win", "seq")),
        P(("win", "seq")),
        P(("win", "seq"), None),
        P(("win", "seq")),
        P(("win", "seq")),
        P(("win", "seq")),
        P(("win", "seq"), None),
        P(("win", "seq")),
        P(("win", "seq"), None),
        P(("win", "seq")),
    )
    return jax.shard_map(shards, mesh=mesh, in_specs=in_specs, out_specs=out_specs, check_vma=False)
```

```python
import functools
import math

import jax
import jax.numpy as jnp
from jax import lax
from jax.experimental import pallas as pl
from jax.experimental.pallas import tpu as pltpu
from jax.sharding import PartitionSpec as P

HEADS = 8
KD = 64
F = 192
WLEN = 1536
CORES = 2
BLOCK_Q = 256
bfloat = jnp.bfloat16
single = jnp.float32


def rel_features(length, feature_count):
    per_basis = feature_count // 6
    offsets = jnp.arange(-length + 1, length).astype(jnp.float32)
    magnitude = jnp.abs(offsets)[:, None]
    half_life = 2.0 ** jnp.linspace(3.0, math.log2(length), per_basis)
    decaying = jnp.exp(-math.log(2.0) / half_life * magnitude)
    widths = 2.0 ** jnp.arange(1, per_basis + 1).astype(jnp.float32) - 1.0
    central = (widths > magnitude).astype(jnp.float32)
    stddev = length / (2.0 * per_basis)
    centers = jnp.linspace(length / per_basis, float(length), per_basis)
    shape_param = (centers / stddev) ** 2
    inverse_scale = centers / stddev**2
    peak_at = (shape_param - 1.0) / inverse_scale
    log_prob = (shape_param - 1.0) * (
        jnp.log(jnp.maximum(magnitude, 0.5)) - jnp.log(peak_at)
    ) - inverse_scale * (magnitude - peak_at)
    density = jnp.exp(log_prob) + 1e-08
    gamma_pdf = density / jnp.max(density, axis=0, keepdims=True)
    basis_set = jnp.concatenate([decaying, central, gamma_pdf], axis=1)
    return jnp.concatenate([basis_set, jnp.sign(offsets)[:, None] * basis_set], axis=1)


def layer_norm(values, norm_gain, norm_shift):
    centered = values - jnp.mean(values, axis=-1, keepdims=True)
    variance = jnp.mean(centered * centered, axis=-1, keepdims=True)
    return centered * lax.rsqrt(variance + 1e-05) * norm_gain + norm_shift


def fwd_kernel(L, bq, hp, vd, x_ref, tab_ref, att_ref, out_ref):
    qi = pl.program_id(0)
    hk = hp * KD
    i0 = pl.multiple_of(qi * bq, bq)
    a = pl.multiple_of(L - bq - i0, bq)
    W = L + bq
    outs = []
    for h in range(hp):
        qc = x_ref[pl.ds(i0, bq), pl.ds(h * KD, KD)]
        qp = x_ref[pl.ds(i0, bq), pl.ds(hk + h * KD, KD)]
        k = x_ref[:, pl.ds(2 * hk + h * KD, KD)]
        v = x_ref[:, pl.ds(3 * hk + h * vd, vd)]
        raw = jnp.dot(qp, tab_ref[pl.ds(h * KD, KD), pl.ds(a, W)], preferred_element_type=jnp.float32)
        rel = pltpu.roll(raw, W - bq + 1, 1, stride=1, stride_axis=0)[:, :L]
        s = rel + lax.dot_general(qc, k, (((1,), (1,)), ((), ())), preferred_element_type=jnp.float32)
        m = jnp.max(s, axis=-1, keepdims=True)
        e = jnp.exp(s - m)
        inv = 1.0 / jnp.sum(e, axis=-1, keepdims=True)
        att = (e * inv).astype(jnp.bfloat16)
        att_ref[h] = att
        outs.append(jnp.dot(att, v, preferred_element_type=jnp.float32).astype(jnp.bfloat16))
    out_ref[...] = jnp.concatenate(outs, axis=1) if hp > 1 else outs[0]

def attention_forward(x, tab, hp, vd, bq):
    L = x.shape[0]
    return pl.pallas_call(
        functools.partial(fwd_kernel, L, bq, hp, vd),
        grid=(L // bq,),
        in_specs=[pl.BlockSpec(x.shape, lambda i: (0, 0)), pl.BlockSpec(tab.shape, lambda i: (0, 0))],
        out_specs=[pl.BlockSpec((hp, bq, L), lambda i: (0, i, 0)), pl.BlockSpec((bq, hp * vd), lambda i: (i, 0))],
        out_shape=[jax.ShapeDtypeStruct((hp, L, L), jnp.bfloat16), jax.ShapeDtypeStruct((L, hp * vd), jnp.bfloat16)],
        compiler_params=pltpu.CompilerParams(vmem_limit_bytes=56 * 2**20),
    )(x, tab)

def bwd_kernel(L, bq, hp, vd, x_ref, tab_ref, att_ref, gm_ref, dq_ref, dkv_ref, dtab_ref, bias_ref, dkT, dvT):
    qi = pl.program_id(0)
    hk = hp * KD
    i0 = pl.multiple_of(qi * bq, bq)
    a = pl.multiple_of(L - bq - i0, bq)
    W = L + bq

    @pl.when(qi == 0)
    def _():
        dkT[...] = jnp.zeros_like(dkT)
        dvT[...] = jnp.zeros_like(dvT)
        dtab_ref[...] = jnp.zeros_like(dtab_ref)
        bias_ref[...] = jnp.zeros_like(bias_ref)

    row = lax.broadcasted_iota(jnp.int32, (bq, bq), 0)
    col = lax.broadcasted_iota(jnp.int32, (bq, bq), 1)
    flip = jnp.where(row + col == bq - 1, 1.0, 0.0).astype(jnp.bfloat16)

    def flipped(v):
        return jnp.dot(flip, v, preferred_element_type=jnp.float32)

    dqs, bc, bp = [], [], []
    for h in range(hp):
        qc = flipped(x_ref[pl.ds(i0, bq), pl.ds(h * KD, KD)]).astype(jnp.bfloat16)
        qp = flipped(x_ref[pl.ds(i0, bq), pl.ds(hk + h * KD, KD)]).astype(jnp.bfloat16)
        k = x_ref[:, pl.ds(2 * hk + h * KD, KD)]
        v = x_ref[:, pl.ds(3 * hk + h * vd, vd)]
        gm = gm_ref[:, pl.ds(h * vd, vd)]
        att = att_ref[h]
        dvT[pl.ds(h * vd, vd), :] += lax.dot_general(gm, att, (((0,), (0,)), ((), ())), preferred_element_type=jnp.float32)
        gmr = flipped(gm).astype(jnp.bfloat16)
        dp = lax.dot_general(gmr, v, (((1,), (1,)), ((), ())), preferred_element_type=jnp.float32)
        af = flipped(att)
        t = af * dp
        delta = jnp.sum(t, axis=-1, keepdims=True)
        ds = (t - af * delta).astype(jnp.bfloat16)
        dkT[pl.ds(h * KD, KD), :] += lax.dot_general(qc, ds, (((0,), (0,)), ((), ())), preferred_element_type=jnp.float32)
        gc = jnp.dot(ds, k, preferred_element_type=jnp.float32)
        wide = jnp.concatenate([ds.astype(jnp.float32), jnp.zeros((bq, bq), jnp.float32)], axis=1)
        rel = pltpu.roll(wide, 0, 1, stride=1, stride_axis=0).astype(jnp.bfloat16)
        tab = tab_ref[pl.ds(h * KD, KD), pl.ds(a, W)]
        gp = lax.dot_general(rel, tab, (((1,), (1,)), ((), ())), preferred_element_type=jnp.float32)
        dtab_ref[pl.ds(h * KD, KD), pl.ds(a, W)] += lax.dot_general(qp, rel, (((0,), (0,)), ((), ())), preferred_element_type=jnp.float32)
        dqs.append(flipped(((gc + gp) * KD ** -0.5).astype(jnp.bfloat16)).astype(jnp.bfloat16))
        bc.append(jnp.sum(gc, axis=0, keepdims=True))
        bp.append(jnp.sum(gp, axis=0, keepdims=True))
    dq_ref[...] = jnp.concatenate(dqs, axis=1) if hp > 1 else dqs[0]
    bias_ref[0:1, :] += jnp.concatenate(bc, axis=1) if hp > 1 else bc[0]
    bias_ref[1:2, :] += jnp.concatenate(bp, axis=1) if hp > 1 else bp[0]

    @pl.when(qi == pl.num_programs(0) - 1)
    def _():
        dkv_ref[:, :hk] = dkT[...].T.astype(jnp.bfloat16)
        dkv_ref[:, hk:] = dvT[...].T.astype(jnp.bfloat16)

def attention_backward(x, tab, att, gm, hp, vd, bq):
    L = x.shape[0]
    hk = hp * KD
    return pl.pallas_call(
        functools.partial(bwd_kernel, L, bq, hp, vd),
        grid=(L // bq,),
        in_specs=[pl.BlockSpec(x.shape, lambda i: (0, 0)), pl.BlockSpec(tab.shape, lambda i: (0, 0)),
                  pl.BlockSpec((hp, bq, L), lambda i: (0, i, 0)), pl.BlockSpec((bq, hp * vd), lambda i: (i, 0))],
        out_specs=[pl.BlockSpec((bq, hk), lambda i: (i, 0)), pl.BlockSpec((L, hk + hp * vd), lambda i: (0, 0)),
                   pl.BlockSpec(tab.shape, lambda i: (0, 0)), pl.BlockSpec((8, hk), lambda i: (0, 0))],
        out_shape=[jax.ShapeDtypeStruct((L, hk), jnp.bfloat16), jax.ShapeDtypeStruct((L, hk + hp * vd), jnp.bfloat16),
                   jax.ShapeDtypeStruct(tab.shape, jnp.float32), jax.ShapeDtypeStruct((8, hk), jnp.float32)],
        scratch_shapes=[pltpu.VMEM((hk, L), jnp.float32), pltpu.VMEM((hp * vd, L), jnp.float32)],
        compiler_params=pltpu.CompilerParams(vmem_limit_bytes=56 * 2**20),
    )(x, tab, att, gm)


def pick(stacked, index, axis):
    return lax.dynamic_index_in_dim(stacked, index, axis, keepdims=False)


def place(stacked, piece, index, axis):
    return lax.dynamic_update_slice_in_dim(stacked, jnp.expand_dims(piece, axis), index, axis)


def swap_seq(value, distance):
    size = lax.axis_size("seq")
    return lax.ppermute(value, "seq", [(i, i ^ distance) for i in range(size)])


def partners():
    win, seq = lax.axis_index("win"), lax.axis_index("seq")
    chips = lax.axis_size("win") // CORES
    bits = lax.axis_size("seq").bit_length() - 1
    return win, seq, win // CORES, win % CORES, chips, bits


def start_together():
    win, seq, here, core, chips, bits = partners()
    barrier = pltpu.get_barrier_semaphore()

    def greet(to_win, to_seq):
        pl.semaphore_signal(
            barrier, inc=1, device_id=(to_win, to_seq), device_id_type=pl.DeviceIdType.MESH
        )

    greet(win ^ 1, seq)
    for bit in range(bits):
        greet(win, seq ^ (1 << bit))

    @pl.when(here > 0)
    def _():
        greet(win - CORES, seq)

    @pl.when(here < chips - 1)
    def _():
        greet(win + CORES, seq)

    ends = jnp.where(here > 0, 1, 0) + jnp.where(here < chips - 1, 1, 0)
    pl.semaphore_wait(barrier, 1 + bits + ends)


def gather_kernel(plan, count, spacing, *refs):
    shards, outs = refs[:count], refs[count : 2 * count]
    send_sem, recv_sem, local_sem = refs[2 * count :]
    win, seq, here, core, chips, bits = partners()
    own_bits = tuple((seq >> bit) & 1 for bit in reversed(range(bits)))
    own_seq = {bit: (seq >> bit) & 1 for bit in range(bits)}

    def region(chunk, chip, done, lead=0, span=None):
        which, col, cols, _ = chunk
        start, size = (col + lead, cols) if span is None else (col + lead, span)
        index = tuple(slice(None) if bit in done else own_seq[bit] for bit in reversed(range(bits)))
        return outs[which].at[(chip, core) + index + (slice(None), pl.ds(start, size))]

    def copy(ref, number, kind, to_win, to_seq):
        return pltpu.make_async_remote_copy(
            src_ref=ref,
            dst_ref=ref,
            send_sem=send_sem.at[number, kind],
            recv_sem=recv_sem.at[number, kind],
            device_id=(to_win, to_seq),
            device_id_type=pl.DeviceIdType.MESH,
        )

    chip_steps = chips - 1
    every_bit = frozenset(range(bits))

    def guarded(condition, action):
        pl.when(condition)(action)

    def chip_stage(chunk, number, step, done):
        up_shard, down_shard = here - step, here + step
        up = copy(region(chunk, jnp.maximum(up_shard, 0), done), number, step, win + CORES, seq)
        down = copy(
            region(chunk, jnp.minimum(down_shard, chips - 1), done),
            number,
            chip_steps + step,
            win - CORES,
            seq,
        )
        sends_up = (up_shard >= 0) & (here < chips - 1)
        sends_down = (down_shard < chips) & (here > 0)
        gets_up = here >= step + 1
        gets_down = here + step + 1 < chips

        def start():
            guarded(sends_up, up.start)
            guarded(sends_down, down.start)

        def arrive():
            guarded(gets_up, up.wait_recv)
            guarded(gets_down, down.wait_recv)

        def finish():
            guarded(sends_up, up.wait_send)
            guarded(sends_down, down.wait_send)

        return start, arrive, finish

    def bit_stage(chunk, number, step, chip):
        half = chunk[2] // 2
        copies = []
        for part in range(2):
            order = list(range(bits)) if part == 0 else list(reversed(range(bits)))
            ref = region(chunk, chip, frozenset(order[:step]), part * half, half)
            kind = 2 * chip_steps + part * bits + step
            copies.append(copy(ref, number, kind, win, seq ^ (1 << order[step])))

        def start():
            for item in copies:
                item.start()

        def arrive():
            for item in copies:
                item.wait_recv()

        def finish():
            for item in copies:
                item.wait_send()

        return start, arrive, finish

    def core_stage(chunk, number):
        kind = 2 * chip_steps + 2 * bits
        item = copy(region(chunk, slice(None), every_bit), number, kind, win ^ 1, seq)
        return item.start, item.wait_recv, item.wait_send

    def stages(chunk, number):
        if chunk[3]:
            line = [chip_stage(chunk, number, step, frozenset()) for step in range(chip_steps)]
            cube = [bit_stage(chunk, number, step, slice(None)) for step in range(bits)]
            return line + cube + [core_stage(chunk, number)]
        cube = [bit_stage(chunk, number, step, here) for step in range(bits)]
        line = [chip_stage(chunk, number, step, every_bit) for step in range(chip_steps)]
        return cube + line + [core_stage(chunk, number)]

    locals_ = []
    for which in range(count):
        target = outs[which].at[(here, core) + own_bits]
        locals_.append(pltpu.make_async_copy(shards[which], target, local_sem.at[which]))
    for item in locals_:
        item.start()
    start_together()
    for item in locals_:
        item.wait()
    work = [stages(chunk, number) for number, chunk in enumerate(plan)]
    depth = chip_steps + bits + 1
    for turn in range(len(plan) + spacing * depth):
        for number in range(len(plan)):
            at, off = divmod(turn - number, spacing)
            if off == 0 and 0 < at <= depth:
                work[number][at - 1][1]()
            if off == 0 and 0 <= at < depth:
                work[number][at][0]()
    for items in work:
        for item in items:
            item[2]()


def gather_all(shards, widths, lines_first, spacing, collective_id):
    chips = lax.axis_size("win") // CORES
    bits = lax.axis_size("seq").bit_length() - 1
    plan = []
    for which, (shard, width) in enumerate(zip(shards, widths)):
        for col in range(0, shard.shape[1], width):
            plan.append((which, col, width, lines_first(len(plan))))
    kinds = 2 * (chips - 1) + 2 * bits + 1
    return pl.pallas_call(
        functools.partial(gather_kernel, tuple(plan), len(shards), spacing),
        in_specs=[pl.BlockSpec(memory_space=pl.ANY)] * len(shards),
        out_specs=[pl.BlockSpec(memory_space=pl.ANY)] * len(shards),
        out_shape=[
            jax.ShapeDtypeStruct((chips, CORES) + (2,) * bits + s.shape, s.dtype) for s in shards
        ],
        scratch_shapes=[
            pltpu.SemaphoreType.DMA((len(plan), kinds)),
            pltpu.SemaphoreType.DMA((len(plan), kinds)),
            pltpu.SemaphoreType.DMA((len(shards),)),
        ],
        compiler_params=pltpu.CompilerParams(collective_id=collective_id, has_side_effects=True),
    )(*shards)


def scatter_kernel(plan, arrays, spacing, *refs):
    count = len(arrays)
    grads, outs, rest = refs[:count], refs[count : 2 * count], refs[2 * count :]
    win, seq, here, core, chips, bits = partners()
    chip_steps = chips - 1
    kept, from_core, rest = rest[:count], rest[count : 2 * count], rest[2 * count :]
    from_bits, rest = rest[: count * bits], rest[count * bits :]
    from_chips, rest = rest[:count], rest[count:]
    send_sem, recv_sem, local_sem = rest
    own_seq = {bit: (seq >> bit) & 1 for bit in range(bits)}

    def add(target, source):
        target[...] = (target[...].astype(single) + source[...].astype(single)).astype(bfloat)

    def slabs(chunk, chip, bit_index, lead=0, span=None):
        which, slot, _ = chunk
        index = tuple(bit_index.get(bit, slice(None)) for bit in reversed(range(bits)))
        width = arrays[which][1]
        columns = pl.ds(lead, width if span is None else span)
        return kept[which].at[(slot, chip) + index + (slice(None), columns)]

    def copy(src, dst, number, kind, to_win, to_seq):
        return pltpu.make_async_remote_copy(
            src_ref=src,
            dst_ref=dst,
            send_sem=send_sem.at[number, kind],
            recv_sem=recv_sem.at[number, kind],
            device_id=(to_win, to_seq),
            device_id_type=pl.DeviceIdType.MESH,
        )

    def core_stage(chunk, number):
        which, slot, _ = chunk
        width = arrays[which][1]
        columns = (slice(None),) * bits + (slice(None), pl.ds(slot * width, width))
        kind = 2 * chip_steps + 2 * bits
        item = copy(
            grads[which].at[(slice(None), 1 - core) + columns],
            from_core[which].at[slot],
            number,
            kind,
            win ^ 1,
            seq,
        )
        own = pltpu.make_async_copy(
            grads[which].at[(slice(None), core) + columns],
            kept[which].at[slot],
            local_sem.at[number],
        )

        def start():
            item.start()
            own.start()

        def arrive():
            own.wait()
            item.wait_recv()
            add(kept[which].at[slot], from_core[which].at[slot])

        return start, arrive, item.wait_send

    def bit_stage(chunk, number, step, chip):
        which, slot, _ = chunk
        half = arrays[which][1] // 2
        items = []
        for part in range(2):
            order = list(range(bits)) if part else list(reversed(range(bits)))
            bit = order[step]
            done = {b: own_seq[b] for b in order[:step]}
            kind = 2 * chip_steps + part * bits + step
            buffer = from_bits[which * bits + step]
            target = buffer.at[(slot, part) if isinstance(chip, slice) else (slot, part, 0)]
            leaving = slabs(chunk, chip, done | {bit: 1 - own_seq[bit]}, part * half, half)
            staying = slabs(chunk, chip, done | {bit: own_seq[bit]}, part * half, half)
            sent = copy(leaving, target, number, kind, win, seq ^ (1 << bit))
            items.append((sent, staying, target))

        def start():
            for sent, _, _ in items:
                sent.start()

        def arrive():
            for sent, staying, target in items:
                sent.wait_recv()
                add(staying, target)

        def finish():
            for sent, _, _ in items:
                sent.wait_send()

        return start, arrive, finish

    def chip_stage(chunk, number, step, bit_index):
        which, slot, lines_last = chunk
        part = (0,) * bits if lines_last else ()
        up_to, down_to = here + step, here - step
        up_slot = from_chips[which].at[(slot, step - 1) + part]
        down_slot = from_chips[which].at[(slot, chip_steps + step - 1) + part]
        up = copy(
            slabs(chunk, jnp.minimum(up_to, chips - 1), bit_index),
            up_slot,
            number,
            step - 1,
            win + CORES,
            seq,
        )
        down = copy(
            slabs(chunk, jnp.maximum(down_to, 0), bit_index),
            down_slot,
            number,
            chip_steps + step - 1,
            win - CORES,
            seq,
        )
        sends_up, sends_down = up_to < chips, down_to >= 0
        gets_up = (here >= 1) & (here - 1 + step < chips)
        gets_down = (here + 1 < chips) & (here + 1 - step >= 0)

        def start():
            pl.when(sends_up)(up.start)
            pl.when(sends_down)(down.start)

        def arrive():
            @pl.when(gets_up)
            def _():
                up.wait_recv()
                add(slabs(chunk, jnp.minimum(here + step - 1, chips - 1), bit_index), up_slot)

            @pl.when(gets_down)
            def _():
                down.wait_recv()
                add(slabs(chunk, jnp.maximum(here - step + 1, 0), bit_index), down_slot)

        def finish():
            pl.when(sends_up)(up.wait_send)
            pl.when(sends_down)(down.wait_send)

        return start, arrive, finish

    def stages(chunk, number):
        steps = range(chip_steps, 0, -1)
        if chunk[2]:
            cube = [bit_stage(chunk, number, step, slice(None)) for step in range(bits)]
            line = [chip_stage(chunk, number, step, own_seq) for step in steps]
            return [core_stage(chunk, number)] + cube + line
        line = [chip_stage(chunk, number, step, {}) for step in steps]
        cube = [bit_stage(chunk, number, step, here) for step in range(bits)]
        return [core_stage(chunk, number)] + line + cube

    start_together()
    work = [stages(chunk, number) for number, chunk in enumerate(plan)]
    depth = chip_steps + bits + 1
    for turn in range(len(plan) + spacing * depth):
        for number, chunk in enumerate(plan):
            at, off = divmod(turn - number, spacing)
            if off == 0 and 0 < at <= depth:
                work[number][at - 1][1]()
                if at == depth:
                    which, slot, _ = chunk
                    width = arrays[which][1]
                    outs[which][:, pl.ds(slot * width, width)] = slabs(chunk, here, own_seq)[
                        ...
                    ].astype(single)
            if off == 0 and 0 <= at < depth:
                work[number][at][0]()
    for items in work:
        for item in items:
            item[2]()


def scatter_all(grads, widths, lines_last, spacing, collective_id):
    chips = lax.axis_size("win") // CORES
    bits = lax.axis_size("seq").bit_length() - 1
    plan, arrays = [], []
    kept, from_core, from_bits, from_chips = [], [], [], []
    for which, (grad, width) in enumerate(zip(grads, widths)):
        rows, cols = grad.shape[-2:]
        slots = cols // width
        lasts = [lines_last(len(plan) + slot) for slot in range(slots)]
        plan += [(which, slot, last) for slot, last in enumerate(lasts)]
        arrays.append((rows, width))
        cube = (2,) * bits
        kept.append(pltpu.VMEM((slots, chips) + cube + (rows, width), bfloat))
        from_core.append(pltpu.VMEM((slots, chips) + cube + (rows, width), bfloat))
        for step in range(bits):
            left = (2,) * (bits - 1 - step)
            from_bits.append(
                pltpu.VMEM((slots, 2, chips) + left + (rows, width // 2), bfloat)
            )
        lone = (1,) * bits if all(lasts) else cube
        from_chips.append(pltpu.VMEM((slots, 2 * (chips - 1)) + lone + (rows, width), bfloat))
    kinds = 2 * (chips - 1) + 2 * bits + 1
    return pl.pallas_call(
        functools.partial(scatter_kernel, tuple(plan), tuple(arrays), spacing),
        in_specs=[pl.BlockSpec(memory_space=pl.ANY)] * len(grads),
        out_specs=[pl.BlockSpec(memory_space=pltpu.VMEM)] * len(grads),
        out_shape=[jax.ShapeDtypeStruct(g.shape[-2:], single) for g in grads],
        scratch_shapes=kept
        + from_core
        + from_bits
        + from_chips
        + [
            pltpu.SemaphoreType.DMA((len(plan), kinds)),
            pltpu.SemaphoreType.DMA((len(plan), kinds)),
            pltpu.SemaphoreType.DMA((len(plan),)),
        ],
        compiler_params=pltpu.CompilerParams(
            collective_id=collective_id, has_side_effects=True, vmem_limit_bytes=60 * 2**20
        ),
    )(*grads)


def exchange(blocks):
    size = lax.axis_size("seq")
    here = lax.axis_index("seq")
    out = place(jnp.zeros(blocks.shape, blocks.dtype), pick(blocks, here, 0), here, 0)
    for distance in range(1, size):
        peer = here ^ distance
        out = place(out, swap_seq(pick(blocks, peer, 0), distance), peer, 0)
    return out


def shards(
    inputs,
    cotangent,
    ln1_scale,
    ln1_offset,
    w_query,
    w_key,
    w_value,
    w_rel,
    content_bias,
    position_bias,
    w_out,
    b_out,
    ln2_scale,
    ln2_offset,
    w_in,
    b_in,
    w_mlp_out,
    b_mlp_out,
):
    win_size, seq_size = lax.axis_size("win"), lax.axis_size("seq")
    devices = win_size * seq_size
    seq = lax.axis_index("seq")
    window_count, row_count, width = inputs.shape
    tokens = window_count * row_count
    hk = HEADS * KD
    vd = width // HEADS
    hp = HEADS // seq_size
    hidden = w_in.shape[1]
    scale_factor = KD ** (-0.5)

    vectors = (
        ln1_scale,
        ln1_offset,
        content_bias,
        position_bias,
        b_out,
        ln2_scale,
        ln2_offset,
        b_in,
        b_mlp_out,
    )
    packed = jnp.concatenate(vectors + (w_rel.T.reshape(-1),))
    packed_size = packed.shape[0]
    small_cols = -(-packed_size // 4096) * 256
    small_size = 16 * small_cols
    packed = jnp.pad(packed, (0, small_size - packed_size)).reshape(16, small_cols)
    packed, whole_qk, whole_v = gather_all(
        (packed, jnp.concatenate([w_query, w_key], axis=1), w_value),
        (256, 512, 512),
        lambda number: number % 4 != 3,
        2,
        0,
    )
    packed = packed.reshape(devices, small_size)
    whole_qk = whole_qk.reshape(width, 2 * hk)
    whole_v = whole_v.reshape(width, width)
    whole_out, whole_in, whole_mlp = gather_all(
        (w_out, w_in, w_mlp_out), (512, 512, 256), lambda number: number % 4 != 3, 2, 1
    )
    whole_out = whole_out.reshape(width, width)
    whole_in = whole_in.reshape(width, hidden)
    whole_mlp = whole_mlp.reshape(hidden, width)
    whole_vectors = []
    at = 0
    for vector in vectors:
        length = vector.shape[0]
        whole_vectors.append(packed[:, at : at + length].reshape(devices * length).astype(single))
        at += length
    whole_rel = packed[:, at:packed_size].reshape(hk, F)
    (
        ln1_gain,
        ln1_shift,
        bias_content,
        bias_position,
        bias_out,
        ln2_gain,
        ln2_shift,
        bias_in,
        bias_mlp,
    ) = whole_vectors

    features = jnp.pad(rel_features(WLEN, F).astype(bfloat), ((0, 1), (0, 0)))
    own_rel = lax.dynamic_slice_in_dim(whole_rel, seq * hp * KD, hp * KD, 0)
    table = jnp.einsum("cf,tf->ct", own_rel, features, preferred_element_type=single).astype(bfloat)

    source = inputs.reshape(tokens, width).astype(single)
    normed_one_f, norm_one_back = jax.vjp(layer_norm, source, ln1_gain, ln1_shift)
    normed_one = normed_one_f.astype(bfloat)
    proj_qk = jnp.dot(normed_one, whole_qk, preferred_element_type=single)
    query = proj_qk[:, :hk] * scale_factor
    proj_v = jnp.dot(normed_one, whole_v, preferred_element_type=single)
    parts = (
        (query + bias_content).astype(bfloat),
        (query + bias_position).astype(bfloat),
        proj_qk[:, hk:].astype(bfloat),
        proj_v.astype(bfloat),
    )
    outgoing = jnp.concatenate([part.reshape(tokens, seq_size, -1) for part in parts], axis=2)
    heads_in = exchange(jnp.transpose(outgoing, (1, 0, 2))).reshape(seq_size * tokens, -1)
    attention, mixed = attention_forward(heads_in, table, hp, vd, BLOCK_Q)
    attended = exchange(mixed.reshape(seq_size, tokens, hp * vd))
    attended = jnp.transpose(attended, (1, 0, 2)).reshape(tokens, width)

    hidden_in = source + jnp.dot(attended, whole_out, preferred_element_type=single) + bias_out
    normed_two_f, norm_two_back = jax.vjp(layer_norm, hidden_in, ln2_gain, ln2_shift)
    normed_two = normed_two_f.astype(bfloat)
    pre_act = jnp.dot(normed_two, whole_in, preferred_element_type=single) + bias_in
    gelu_out, gelu_back = jax.vjp(jax.nn.gelu, pre_act)
    activation = gelu_out.astype(bfloat)
    result = hidden_in + jnp.dot(activation, whole_mlp, preferred_element_type=single) + bias_mlp
    layer_out = result.astype(bfloat).reshape(inputs.shape)

    grid = (win_size // CORES, CORES) + (2,) * (seq_size.bit_length() - 1)

    def weight_grad(left, right):
        grad = jnp.einsum("td,te->de", left, right, preferred_element_type=single).astype(bfloat)
        rows, cols = grad.shape
        return grad.reshape(grid + (rows // devices, cols))

    cot_rows = cotangent.reshape(tokens, width)
    grad_mlp = weight_grad(activation, cot_rows)
    grad_bias_mlp = jnp.sum(cot_rows.astype(single), axis=0)
    grad_act = jnp.einsum("td,fd->tf", cot_rows, whole_mlp, preferred_element_type=single)
    grad_pre = gelu_back(grad_act)[0].astype(bfloat)
    grad_in = weight_grad(normed_two, grad_pre)
    grad_mlp, grad_in = scatter_all(
        (grad_mlp, grad_in), (256, 512), lambda number: number % 4 != 0, 2, 2
    )
    grad_bias_in = jnp.sum(grad_pre.astype(single), axis=0)
    grad_normed_two = jnp.einsum("tf,df->td", grad_pre, whole_in, preferred_element_type=single)
    hidden_term, grad_ln2_gain, grad_ln2_shift = norm_two_back(grad_normed_two)
    grad_hidden = cot_rows.astype(single) + hidden_term
    grad_branch = grad_hidden.astype(bfloat)
    grad_out = weight_grad(attended, grad_branch)
    grad_bias_out = jnp.sum(grad_branch.astype(single), axis=0)
    grad_mixed = jnp.einsum(
        "te,de->td", grad_branch, whole_out, preferred_element_type=single
    ).astype(bfloat)
    grad_mixed = jnp.transpose(grad_mixed.reshape(tokens, seq_size, hp * vd), (1, 0, 2))
    grad_heads = exchange(grad_mixed).reshape(seq_size * tokens, hp * vd)
    grad_q, grad_kv, grad_table, grad_bias = attention_backward(
        heads_in, table, attention, grad_heads, hp, vd, BLOCK_Q
    )
    own = hp * KD
    returned = exchange(
        jnp.concatenate([grad_q, grad_kv], axis=1).reshape(seq_size, tokens, 2 * own + hp * vd)
    )
    returned = jnp.transpose(returned, (1, 0, 2))
    grad_qk_rows = jnp.concatenate(
        [
            returned[:, :, :own].reshape(tokens, hk),
            returned[:, :, own : 2 * own].reshape(tokens, hk),
        ],
        axis=1,
    )
    grad_v_rows = returned[:, :, 2 * own :].reshape(tokens, width)
    grad_qk = weight_grad(normed_one, grad_qk_rows)
    grad_v = weight_grad(normed_one, grad_v_rows)
    grad_normed_one = jnp.einsum(
        "tk,dk->td", grad_qk_rows, whole_qk, preferred_element_type=single
    ) + jnp.einsum("tk,dk->td", grad_v_rows, whole_v, preferred_element_type=single)
    source_term, grad_ln1_gain, grad_ln1_shift = norm_one_back(grad_normed_one)
    grad_inputs = (grad_hidden + source_term).reshape(inputs.shape)

    grad_rel = jnp.dot(grad_table, features.astype(single), precision=lax.Precision.HIGHEST)
    whole_grad_rel = lax.dynamic_update_slice_in_dim(
        jnp.zeros((hk, F), single), grad_rel, seq * own, 0
    )

    def spread(own_heads):
        return lax.dynamic_update_slice_in_dim(jnp.zeros((hk,), single), own_heads, seq * own, 0)

    vector_grads = (
        grad_ln1_gain,
        grad_ln1_shift,
        spread(grad_bias[0]),
        spread(grad_bias[1]),
        grad_bias_out,
        grad_ln2_gain,
        grad_ln2_shift,
        grad_bias_in,
        grad_bias_mlp,
    )
    small = jnp.concatenate(
        [v.reshape(devices, -1) for v in vector_grads + (whole_grad_rel,)], axis=1
    )
    small = jnp.pad(small, ((0, 0), (0, small_size - packed_size))).astype(bfloat)
    grad_out, grad_qk, grad_v, small = scatter_all(
        (grad_out, grad_qk, grad_v, small.reshape(grid + (16, small_cols))),
        (512, 512, 512, 256),
        lambda number: number % 4 != 0,
        2,
        3,
    )
    small = small.reshape(-1)[:packed_size]
    small_grads = []
    at = 0
    for vector in vectors:
        length = vector.shape[0]
        small_grads.append(small[at : at + length])
        at += length
    g = small_grads
    own_grad_rel = small[at:].reshape(-1, F).T
    return (
        layer_out,
        grad_inputs,
        g[0],
        g[1],
        grad_qk[:, :hk],
        grad_qk[:, hk:],
        grad_v,
        own_grad_rel,
        g[2],
        g[3],
        grad_out,
        g[4],
        g[5],
        g[6],
        grad_in,
        g[7],
        grad_mlp,
        g[8],
    )


def solution(mesh):
    in_specs = (
        P("win", "seq", None),
        P("win", "seq", None),
        P(("win", "seq")),
        P(("win", "seq")),
        P(("win", "seq"), None),
        P(("win", "seq"), None),
        P(("win", "seq"), None),
        P(None, ("win", "seq")),
        P(("win", "seq")),
        P(("win", "seq")),
        P(("win", "seq"), None),
        P(("win", "seq")),
        P(("win", "seq")),
        P(("win", "seq")),
        P(("win", "seq"), None),
        P(("win", "seq")),
        P(("win", "seq"), None),
        P(("win", "seq")),
    )
    out_specs = (
        P("win", "seq", None),
        P("win", "seq", None),
        P(("win", "seq")),
        P(("win", "seq")),
        P(("win", "seq"), None),
        P(("win", "seq"), None),
        P(("win", "seq"), None),
        P(None, ("win", "seq")),
        P(("win", "seq")),
        P(("win", "seq")),
        P(("win", "seq"), None),
        P(("win", "seq")),
        P(("win", "seq")),
        P(("win", "seq")),
        P(("win", "seq"), None),
        P(("win", "seq")),
        P(("win", "seq"), None),
        P(("win", "seq")),
    )
    return jax.shard_map(shards, mesh=mesh, in_specs=in_specs, out_specs=out_specs, check_vma=False)
```

```python
import functools
import math

import jax
import jax.numpy as jnp
from jax import lax
from jax.experimental import pallas as pl
from jax.experimental.pallas import tpu as pltpu
from jax.sharding import PartitionSpec as P

HEADS = 8
KD = 64
F = 192
WLEN = 1536
CORES = 2
BLOCK_Q = 256
FIRST_BLOCK_TURN = 8
bfloat = jnp.bfloat16
single = jnp.float32


def rel_features(length, feature_count):
    per_basis = feature_count // 6
    offsets = jnp.arange(-length + 1, length).astype(jnp.float32)
    magnitude = jnp.abs(offsets)[:, None]
    half_life = 2.0 ** jnp.linspace(3.0, math.log2(length), per_basis)
    decaying = jnp.exp(-math.log(2.0) / half_life * magnitude)
    widths = 2.0 ** jnp.arange(1, per_basis + 1).astype(jnp.float32) - 1.0
    central = (widths > magnitude).astype(jnp.float32)
    stddev = length / (2.0 * per_basis)
    centers = jnp.linspace(length / per_basis, float(length), per_basis)
    shape_param = (centers / stddev) ** 2
    inverse_scale = centers / stddev**2
    peak_at = (shape_param - 1.0) / inverse_scale
    log_prob = (shape_param - 1.0) * (
        jnp.log(jnp.maximum(magnitude, 0.5)) - jnp.log(peak_at)
    ) - inverse_scale * (magnitude - peak_at)
    density = jnp.exp(log_prob) + 1e-08
    gamma_pdf = density / jnp.max(density, axis=0, keepdims=True)
    basis_set = jnp.concatenate([decaying, central, gamma_pdf], axis=1)
    return jnp.concatenate([basis_set, jnp.sign(offsets)[:, None] * basis_set], axis=1)


def layer_norm(values, norm_gain, norm_shift):
    centered = values - jnp.mean(values, axis=-1, keepdims=True)
    variance = jnp.mean(centered * centered, axis=-1, keepdims=True)
    return centered * lax.rsqrt(variance + 1e-05) * norm_gain + norm_shift


def attend_block(length, bq, hp, vd, block, x_ref, tab_ref, att_ref, mixed_ref):
    hk = hp * KD
    first = block * bq
    rows = pl.ds(first, bq)
    span = length + bq
    outs = []
    for h in range(hp):
        qc = x_ref[rows, pl.ds(h * KD, KD)]
        qp = x_ref[rows, pl.ds(hk + h * KD, KD)]
        k = x_ref[:, pl.ds(2 * hk + h * KD, KD)]
        v = x_ref[:, pl.ds(3 * hk + h * vd, vd)]
        table = tab_ref[pl.ds(h * KD, KD), pl.ds(length - bq - first, span)]
        raw = jnp.dot(qp, table, preferred_element_type=single)
        rel = pltpu.roll(raw, span - bq + 1, 1, stride=1, stride_axis=0)[:, :length]
        s = rel + lax.dot_general(qc, k, (((1,), (1,)), ((), ())), preferred_element_type=single)
        e = jnp.exp(s - jnp.max(s, axis=-1, keepdims=True))
        inverse = 1.0 / jnp.sum(e, axis=-1, keepdims=True)
        att = (e * inverse).astype(bfloat)
        att_ref[h] = att
        outs.append(jnp.dot(att, v, preferred_element_type=single).astype(bfloat))
    mixed_ref[rows, :] = jnp.concatenate(outs, axis=1) if hp > 1 else outs[0]


def bwd_kernel(L, bq, hp, vd, x_ref, tab_ref, att_ref, gm_ref, dq_ref, dkv_ref, dtab_ref, bias_ref, dkT, dvT):
    qi = pl.program_id(0)
    hk = hp * KD
    i0 = pl.multiple_of(qi * bq, bq)
    a = pl.multiple_of(L - bq - i0, bq)
    W = L + bq

    @pl.when(qi == 0)
    def _():
        dkT[...] = jnp.zeros_like(dkT)
        dvT[...] = jnp.zeros_like(dvT)
        dtab_ref[...] = jnp.zeros_like(dtab_ref)
        bias_ref[...] = jnp.zeros_like(bias_ref)

    row = lax.broadcasted_iota(jnp.int32, (bq, bq), 0)
    col = lax.broadcasted_iota(jnp.int32, (bq, bq), 1)
    flip = jnp.where(row + col == bq - 1, 1.0, 0.0).astype(jnp.bfloat16)

    def flipped(v):
        return jnp.dot(flip, v, preferred_element_type=jnp.float32)

    dqs, bc, bp = [], [], []
    for h in range(hp):
        qc = flipped(x_ref[pl.ds(i0, bq), pl.ds(h * KD, KD)]).astype(jnp.bfloat16)
        qp = flipped(x_ref[pl.ds(i0, bq), pl.ds(hk + h * KD, KD)]).astype(jnp.bfloat16)
        k = x_ref[:, pl.ds(2 * hk + h * KD, KD)]
        v = x_ref[:, pl.ds(3 * hk + h * vd, vd)]
        gm = gm_ref[:, pl.ds(h * vd, vd)]
        att = att_ref[h]
        dvT[pl.ds(h * vd, vd), :] += lax.dot_general(gm, att, (((0,), (0,)), ((), ())), preferred_element_type=jnp.float32)
        gmr = flipped(gm).astype(jnp.bfloat16)
        dp = lax.dot_general(gmr, v, (((1,), (1,)), ((), ())), preferred_element_type=jnp.float32)
        af = flipped(att)
        t = af * dp
        delta = jnp.sum(t, axis=-1, keepdims=True)
        ds = (t - af * delta).astype(jnp.bfloat16)
        dkT[pl.ds(h * KD, KD), :] += lax.dot_general(qc, ds, (((0,), (0,)), ((), ())), preferred_element_type=jnp.float32)
        gc = jnp.dot(ds, k, preferred_element_type=jnp.float32)
        wide = jnp.concatenate([ds.astype(jnp.float32), jnp.zeros((bq, bq), jnp.float32)], axis=1)
        rel = pltpu.roll(wide, 0, 1, stride=1, stride_axis=0).astype(jnp.bfloat16)
        tab = tab_ref[pl.ds(h * KD, KD), pl.ds(a, W)]
        gp = lax.dot_general(rel, tab, (((1,), (1,)), ((), ())), preferred_element_type=jnp.float32)
        dtab_ref[pl.ds(h * KD, KD), pl.ds(a, W)] += lax.dot_general(qp, rel, (((0,), (0,)), ((), ())), preferred_element_type=jnp.float32)
        dqs.append(flipped(((gc + gp) * KD ** -0.5).astype(jnp.bfloat16)).astype(jnp.bfloat16))
        bc.append(jnp.sum(gc, axis=0, keepdims=True))
        bp.append(jnp.sum(gp, axis=0, keepdims=True))
    dq_ref[...] = jnp.concatenate(dqs, axis=1) if hp > 1 else dqs[0]
    bias_ref[0:1, :] += jnp.concatenate(bc, axis=1) if hp > 1 else bc[0]
    bias_ref[1:2, :] += jnp.concatenate(bp, axis=1) if hp > 1 else bp[0]

    @pl.when(qi == pl.num_programs(0) - 1)
    def _():
        dkv_ref[:, :hk] = dkT[...].T.astype(jnp.bfloat16)
        dkv_ref[:, hk:] = dvT[...].T.astype(jnp.bfloat16)

def attention_backward(x, tab, att, gm, hp, vd, bq):
    L = x.shape[0]
    hk = hp * KD
    return pl.pallas_call(
        functools.partial(bwd_kernel, L, bq, hp, vd),
        grid=(L // bq,),
        in_specs=[pl.BlockSpec(x.shape, lambda i: (0, 0)), pl.BlockSpec(tab.shape, lambda i: (0, 0)),
                  pl.BlockSpec((hp, bq, L), lambda i: (0, i, 0)), pl.BlockSpec((bq, hp * vd), lambda i: (i, 0))],
        out_specs=[pl.BlockSpec((bq, hk), lambda i: (i, 0)), pl.BlockSpec((L, hk + hp * vd), lambda i: (0, 0)),
                   pl.BlockSpec(tab.shape, lambda i: (0, 0)), pl.BlockSpec((8, hk), lambda i: (0, 0))],
        out_shape=[jax.ShapeDtypeStruct((L, hk), jnp.bfloat16), jax.ShapeDtypeStruct((L, hk + hp * vd), jnp.bfloat16),
                   jax.ShapeDtypeStruct(tab.shape, jnp.float32), jax.ShapeDtypeStruct((8, hk), jnp.float32)],
        scratch_shapes=[pltpu.VMEM((hk, L), jnp.float32), pltpu.VMEM((hp * vd, L), jnp.float32)],
        compiler_params=pltpu.CompilerParams(vmem_limit_bytes=56 * 2**20),
    )(x, tab, att, gm)


def pick(stacked, index, axis):
    return lax.dynamic_index_in_dim(stacked, index, axis, keepdims=False)


def place(stacked, piece, index, axis):
    return lax.dynamic_update_slice_in_dim(stacked, jnp.expand_dims(piece, axis), index, axis)


def swap_seq(value, distance):
    size = lax.axis_size("seq")
    return lax.ppermute(value, "seq", [(i, i ^ distance) for i in range(size)])


def partners():
    win, seq = lax.axis_index("win"), lax.axis_index("seq")
    chips = lax.axis_size("win") // CORES
    bits = lax.axis_size("seq").bit_length() - 1
    return win, seq, win // CORES, win % CORES, chips, bits


def start_together(whole_seq=False):
    win, seq, here, core, chips, bits = partners()
    barrier = pltpu.get_barrier_semaphore()

    def greet(to_win, to_seq):
        pl.semaphore_signal(
            barrier, inc=1, device_id=(to_win, to_seq), device_id_type=pl.DeviceIdType.MESH
        )

    greet(win ^ 1, seq)
    across = range(1, 1 << bits) if whole_seq else [1 << bit for bit in range(bits)]
    for distance in across:
        greet(win, seq ^ distance)

    @pl.when(here > 0)
    def _():
        greet(win - CORES, seq)

    @pl.when(here < chips - 1)
    def _():
        greet(win + CORES, seq)

    ends = jnp.where(here > 0, 1, 0) + jnp.where(here < chips - 1, 1, 0)
    pl.semaphore_wait(barrier, 1 + len(across) + ends)


def gather_work(plan, shards, outs, send_sem, recv_sem, local_sem):
    win, seq, here, core, chips, bits = partners()
    own_bits = tuple((seq >> bit) & 1 for bit in reversed(range(bits)))
    own_seq = {bit: (seq >> bit) & 1 for bit in range(bits)}

    def region(chunk, chip, done, lead=0, span=None):
        which, col, cols, _ = chunk
        start, size = (col + lead, cols) if span is None else (col + lead, span)
        index = tuple(slice(None) if bit in done else own_seq[bit] for bit in reversed(range(bits)))
        return outs[which].at[(chip, core) + index + (slice(None), pl.ds(start, size))]

    def copy(ref, number, kind, to_win, to_seq):
        return pltpu.make_async_remote_copy(
            src_ref=ref,
            dst_ref=ref,
            send_sem=send_sem.at[number, kind],
            recv_sem=recv_sem.at[number, kind],
            device_id=(to_win, to_seq),
            device_id_type=pl.DeviceIdType.MESH,
        )

    chip_steps = chips - 1
    every_bit = frozenset(range(bits))

    def guarded(condition, action):
        pl.when(condition)(action)

    def chip_stage(chunk, number, step, done):
        up_shard, down_shard = here - step, here + step
        up = copy(region(chunk, jnp.maximum(up_shard, 0), done), number, step, win + CORES, seq)
        down = copy(
            region(chunk, jnp.minimum(down_shard, chips - 1), done),
            number,
            chip_steps + step,
            win - CORES,
            seq,
        )
        sends_up = (up_shard >= 0) & (here < chips - 1)
        sends_down = (down_shard < chips) & (here > 0)
        gets_up = here >= step + 1
        gets_down = here + step + 1 < chips

        def start():
            guarded(sends_up, up.start)
            guarded(sends_down, down.start)

        def arrive():
            guarded(gets_up, up.wait_recv)
            guarded(gets_down, down.wait_recv)

        def finish():
            guarded(sends_up, up.wait_send)
            guarded(sends_down, down.wait_send)

        return start, arrive, finish

    def bit_stage(chunk, number, step, chip):
        half = chunk[2] // 2
        copies = []
        for part in range(2):
            order = list(range(bits)) if part == 0 else list(reversed(range(bits)))
            ref = region(chunk, chip, frozenset(order[:step]), part * half, half)
            kind = 2 * chip_steps + part * bits + step
            copies.append(copy(ref, number, kind, win, seq ^ (1 << order[step])))

        def start():
            for item in copies:
                item.start()

        def arrive():
            for item in copies:
                item.wait_recv()

        def finish():
            for item in copies:
                item.wait_send()

        return start, arrive, finish

    def core_stage(chunk, number):
        kind = 2 * chip_steps + 2 * bits
        item = copy(region(chunk, slice(None), every_bit), number, kind, win ^ 1, seq)
        return item.start, item.wait_recv, item.wait_send

    def stages(chunk, number):
        if chunk[3]:
            line = [chip_stage(chunk, number, step, frozenset()) for step in range(chip_steps)]
            cube = [bit_stage(chunk, number, step, slice(None)) for step in range(bits)]
            return line + cube + [core_stage(chunk, number)]
        cube = [bit_stage(chunk, number, step, here) for step in range(bits)]
        line = [chip_stage(chunk, number, step, every_bit) for step in range(chip_steps)]
        return cube + line + [core_stage(chunk, number)]

    own = [
        pltpu.make_async_copy(shard, out.at[(here, core) + own_bits], local_sem.at[which])
        for which, (shard, out) in enumerate(zip(shards, outs))
    ]
    return own, [stages(chunk, number) for number, chunk in enumerate(plan)]


def run_turn(work, spacing, turn, last=None):
    for number, stages in enumerate(work):
        at, off = divmod(turn - number, spacing)
        if off == 0 and 0 < at <= len(stages):
            stages[at - 1][1]()
            if at == len(stages) and last is not None:
                last(number)
        if off == 0 and 0 <= at < len(stages):
            stages[at][0]()


def turns_of(work, spacing):
    return len(work) + spacing * len(work[0])


def finish_sends(work):
    for stages in work:
        for stage in stages:
            stage[2]()


def gather_kernel(plan, count, spacing, *refs):
    shards, outs, sems = refs[:count], refs[count : 2 * count], refs[2 * count :]
    own, work = gather_work(plan, shards, outs, *sems)
    for item in own:
        item.start()
    start_together()
    for item in own:
        item.wait()
    for turn in range(turns_of(work, spacing)):
        run_turn(work, spacing, turn)
    finish_sends(work)


def gather_plan(shards, widths, lines_first):
    plan = []
    for which, (shard, width) in enumerate(zip(shards, widths)):
        for col in range(0, shard.shape[1], width):
            plan.append((which, col, width, lines_first(len(plan))))
    return tuple(plan)


def gather_sems(plan, count):
    chips = lax.axis_size("win") // CORES
    bits = lax.axis_size("seq").bit_length() - 1
    kinds = 2 * (chips - 1) + 2 * bits + 1
    return [
        pltpu.SemaphoreType.DMA((len(plan), kinds)),
        pltpu.SemaphoreType.DMA((len(plan), kinds)),
        pltpu.SemaphoreType.DMA((count,)),
    ]


def gathered_shapes(shards):
    chips = lax.axis_size("win") // CORES
    bits = lax.axis_size("seq").bit_length() - 1
    return [jax.ShapeDtypeStruct((chips, CORES) + (2,) * bits + s.shape, s.dtype) for s in shards]


def gather_all(shards, widths, lines_first, spacing, collective_id):
    plan = gather_plan(shards, widths, lines_first)
    return pl.pallas_call(
        functools.partial(gather_kernel, plan, len(shards), spacing),
        in_specs=[pl.BlockSpec(memory_space=pltpu.VMEM)] * len(shards),
        out_specs=[pl.BlockSpec(memory_space=pl.ANY)] * len(shards),
        out_shape=gathered_shapes(shards),
        scratch_shapes=gather_sems(plan, len(shards)),
        compiler_params=pltpu.CompilerParams(collective_id=collective_id, has_side_effects=True),
    )(*shards)


def exchange_work(parts, target, send_sem, recv_sem, local_sem):
    win, seq = lax.axis_index("win"), lax.axis_index("seq")
    items = []
    for peer, part in enumerate(parts):
        sent = pltpu.make_async_remote_copy(
            src_ref=part,
            dst_ref=target(seq),
            send_sem=send_sem.at[peer],
            recv_sem=recv_sem.at[seq],
            device_id=(win, peer),
            device_id_type=pl.DeviceIdType.MESH,
        )
        got = pltpu.make_async_remote_copy(
            src_ref=part,
            dst_ref=target(peer),
            send_sem=send_sem.at[peer],
            recv_sem=recv_sem.at[peer],
            device_id=(win, peer),
            device_id_type=pl.DeviceIdType.MESH,
        )
        own = pltpu.make_async_copy(part, target(peer), local_sem.at[peer])

        def start(peer=peer, sent=sent, own=own):
            pl.when(peer != seq)(sent.start)
            pl.when(peer == seq)(own.start)

        def arrive(peer=peer, got=got, own=own):
            pl.when(peer != seq)(got.wait_recv)
            pl.when(peer == seq)(own.wait)

        def finish(peer=peer, sent=sent):
            pl.when(peer != seq)(sent.wait_send)

        items.append((start, arrive, finish))
    return items


def attend_kernel(plan, count, spacing, first_turn, dims, *refs):
    hp, vd, bq = dims
    shards, (outgoing, tab_ref), refs = refs[:count], refs[count : count + 2], refs[count + 2 :]
    outs, (x_ref, att_out, attended), refs = refs[:count], refs[count : count + 3], refs[count + 3 :]
    att_ref, mixed_ref, *gather_refs = refs[:-7]
    in_send, in_recv, in_local, out_send, out_recv, out_local, att_sem = refs[-7:]
    length = x_ref.shape[0]
    peers, rows = outgoing.shape[0], outgoing.shape[1]
    own, work = gather_work(plan, shards, outs, *gather_refs)
    incoming = exchange_work(
        [outgoing.at[peer] for peer in range(peers)],
        lambda peer: x_ref.at[pl.ds(peer * rows, rows)],
        in_send,
        in_recv,
        in_local,
    )
    leaving = exchange_work(
        [mixed_ref.at[pl.ds(peer * rows, rows)] for peer in range(peers)],
        lambda peer: attended.at[peer],
        out_send,
        out_recv,
        out_local,
    )
    for item in own:
        item.start()
    start_together(True)
    for item in own:
        item.wait()
    for start, _, _ in incoming:
        start()
    blocks = length // bq
    kept = [
        pltpu.make_async_copy(
            att_ref.at[block % 2], att_out.at[:, pl.ds(block * bq, bq)], att_sem.at[block]
        )
        for block in range(blocks)
    ]
    sent = 0
    for turn in range(turns_of(work, spacing)):
        run_turn(work, spacing, turn)
        block = turn - first_turn
        if block == 0:
            for _, arrive, _ in incoming:
                arrive()
        if 0 <= block < blocks:
            if block >= 2:
                kept[block - 2].wait()
            attend_block(length, bq, hp, vd, block, x_ref, tab_ref, att_ref.at[block % 2], mixed_ref)
            kept[block].start()
            while sent < peers and (sent + 1) * rows <= (block + 1) * bq:
                leaving[sent][0]()
                sent += 1
    for _, arrive, _ in leaving:
        arrive()
    for _, _, finish in incoming + leaving:
        finish()
    for item in kept[-2:]:
        item.wait()
    finish_sends(work)


def gather_and_attend(shards, widths, lines_first, spacing, first_turn, outgoing, tab, dims):
    hp, vd, bq = dims
    peers, rows, cols = outgoing.shape
    length = peers * rows
    plan = gather_plan(shards, widths, lines_first)
    count = len(shards)
    anywhere = pl.BlockSpec(memory_space=pl.ANY)
    vmem = pl.BlockSpec(memory_space=pltpu.VMEM)
    dma = pltpu.SemaphoreType.DMA
    return pl.pallas_call(
        functools.partial(attend_kernel, plan, count, spacing, first_turn, dims),
        in_specs=[vmem] * count + [anywhere, vmem],
        out_specs=[anywhere] * count + [vmem, anywhere, vmem],
        out_shape=gathered_shapes(shards)
        + [
            jax.ShapeDtypeStruct((length, cols), bfloat),
            jax.ShapeDtypeStruct((hp, length, length), bfloat),
            jax.ShapeDtypeStruct((peers, rows, hp * vd), bfloat),
        ],
        scratch_shapes=[
            pltpu.VMEM((2, hp, bq, length), bfloat),
            pltpu.VMEM((length, hp * vd), bfloat),
        ]
        + gather_sems(plan, count)
        + [dma((peers,))] * 6
        + [dma((length // bq,))],
        compiler_params=pltpu.CompilerParams(
            collective_id=1, has_side_effects=True, vmem_limit_bytes=56 * 2**20
        ),
    )(*shards, outgoing, tab)


def scatter_kernel(plan, arrays, spacing, *refs):
    count = len(arrays)
    grads, outs, rest = refs[:count], refs[count : 2 * count], refs[2 * count :]
    win, seq, here, core, chips, bits = partners()
    chip_steps = chips - 1
    kept, from_core, rest = rest[:count], rest[count : 2 * count], rest[2 * count :]
    from_bits, rest = rest[: count * bits], rest[count * bits :]
    from_chips, rest = rest[:count], rest[count:]
    send_sem, recv_sem, local_sem = rest
    own_seq = {bit: (seq >> bit) & 1 for bit in range(bits)}

    def add(target, source):
        target[...] = (target[...].astype(single) + source[...].astype(single)).astype(bfloat)

    def slabs(chunk, chip, bit_index, lead=0, span=None):
        which, slot, _ = chunk
        index = tuple(bit_index.get(bit, slice(None)) for bit in reversed(range(bits)))
        width = arrays[which][1]
        columns = pl.ds(lead, width if span is None else span)
        return kept[which].at[(slot, chip) + index + (slice(None), columns)]

    def copy(src, dst, number, kind, to_win, to_seq):
        return pltpu.make_async_remote_copy(
            src_ref=src,
            dst_ref=dst,
            send_sem=send_sem.at[number, kind],
            recv_sem=recv_sem.at[number, kind],
            device_id=(to_win, to_seq),
            device_id_type=pl.DeviceIdType.MESH,
        )

    def core_stage(chunk, number):
        which, slot, _ = chunk
        width = arrays[which][1]
        columns = (slice(None),) * bits + (slice(None), pl.ds(slot * width, width))
        kind = 2 * chip_steps + 2 * bits
        item = copy(
            grads[which].at[(slice(None), 1 - core) + columns],
            from_core[which].at[slot],
            number,
            kind,
            win ^ 1,
            seq,
        )
        own = pltpu.make_async_copy(
            grads[which].at[(slice(None), core) + columns],
            kept[which].at[slot],
            local_sem.at[number],
        )

        def start():
            item.start()
            own.start()

        def arrive():
            own.wait()
            item.wait_recv()
            add(kept[which].at[slot], from_core[which].at[slot])

        return start, arrive, item.wait_send

    def bit_stage(chunk, number, step, chip):
        which, slot, _ = chunk
        half = arrays[which][1] // 2
        items = []
        for part in range(2):
            order = list(range(bits)) if part else list(reversed(range(bits)))
            bit = order[step]
            done = {b: own_seq[b] for b in order[:step]}
            kind = 2 * chip_steps + part * bits + step
            buffer = from_bits[which * bits + step]
            target = buffer.at[(slot, part) if isinstance(chip, slice) else (slot, part, 0)]
            leaving = slabs(chunk, chip, done | {bit: 1 - own_seq[bit]}, part * half, half)
            staying = slabs(chunk, chip, done | {bit: own_seq[bit]}, part * half, half)
            sent = copy(leaving, target, number, kind, win, seq ^ (1 << bit))
            items.append((sent, staying, target))

        def start():
            for sent, _, _ in items:
                sent.start()

        def arrive():
            for sent, staying, target in items:
                sent.wait_recv()
                add(staying, target)

        def finish():
            for sent, _, _ in items:
                sent.wait_send()

        return start, arrive, finish

    def chip_stage(chunk, number, step, bit_index):
        which, slot, lines_last = chunk
        part = (0,) * bits if lines_last else ()
        up_to, down_to = here + step, here - step
        up_slot = from_chips[which].at[(slot, step - 1) + part]
        down_slot = from_chips[which].at[(slot, chip_steps + step - 1) + part]
        up = copy(
            slabs(chunk, jnp.minimum(up_to, chips - 1), bit_index),
            up_slot,
            number,
            step - 1,
            win + CORES,
            seq,
        )
        down = copy(
            slabs(chunk, jnp.maximum(down_to, 0), bit_index),
            down_slot,
            number,
            chip_steps + step - 1,
            win - CORES,
            seq,
        )
        sends_up, sends_down = up_to < chips, down_to >= 0
        gets_up = (here >= 1) & (here - 1 + step < chips)
        gets_down = (here + 1 < chips) & (here + 1 - step >= 0)

        def start():
            pl.when(sends_up)(up.start)
            pl.when(sends_down)(down.start)

        def arrive():
            @pl.when(gets_up)
            def _():
                up.wait_recv()
                add(slabs(chunk, jnp.minimum(here + step - 1, chips - 1), bit_index), up_slot)

            @pl.when(gets_down)
            def _():
                down.wait_recv()
                add(slabs(chunk, jnp.maximum(here - step + 1, 0), bit_index), down_slot)

        def finish():
            pl.when(sends_up)(up.wait_send)
            pl.when(sends_down)(down.wait_send)

        return start, arrive, finish

    def stages(chunk, number):
        steps = range(chip_steps, 0, -1)
        if chunk[2]:
            cube = [bit_stage(chunk, number, step, slice(None)) for step in range(bits)]
            line = [chip_stage(chunk, number, step, own_seq) for step in steps]
            return [core_stage(chunk, number)] + cube + line
        line = [chip_stage(chunk, number, step, {}) for step in steps]
        cube = [bit_stage(chunk, number, step, here) for step in range(bits)]
        return [core_stage(chunk, number)] + line + cube

    def last(number):
        chunk = plan[number]
        which, slot, _ = chunk
        width = arrays[which][1]
        total = slabs(chunk, here, own_seq)[...].astype(single)
        outs[which][:, pl.ds(slot * width, width)] = total

    start_together()
    work = [stages(chunk, number) for number, chunk in enumerate(plan)]
    for turn in range(turns_of(work, spacing)):
        run_turn(work, spacing, turn, last)
    finish_sends(work)


def scatter_all(grads, widths, lines_last, spacing, collective_id):
    chips = lax.axis_size("win") // CORES
    bits = lax.axis_size("seq").bit_length() - 1
    plan, arrays = [], []
    kept, from_core, from_bits, from_chips = [], [], [], []
    for which, (grad, width) in enumerate(zip(grads, widths)):
        rows, cols = grad.shape[-2:]
        slots = cols // width
        lasts = [lines_last(len(plan) + slot) for slot in range(slots)]
        plan += [(which, slot, last) for slot, last in enumerate(lasts)]
        arrays.append((rows, width))
        cube = (2,) * bits
        kept.append(pltpu.VMEM((slots, chips) + cube + (rows, width), bfloat))
        from_core.append(pltpu.VMEM((slots, chips) + cube + (rows, width), bfloat))
        for step in range(bits):
            left = (2,) * (bits - 1 - step)
            from_bits.append(
                pltpu.VMEM((slots, 2, chips) + left + (rows, width // 2), bfloat)
            )
        lone = (1,) * bits if all(lasts) else cube
        from_chips.append(pltpu.VMEM((slots, 2 * (chips - 1)) + lone + (rows, width), bfloat))
    kinds = 2 * (chips - 1) + 2 * bits + 1
    return pl.pallas_call(
        functools.partial(scatter_kernel, tuple(plan), tuple(arrays), spacing),
        in_specs=[pl.BlockSpec(memory_space=pl.ANY)] * len(grads),
        out_specs=[pl.BlockSpec(memory_space=pltpu.VMEM)] * len(grads),
        out_shape=[jax.ShapeDtypeStruct(g.shape[-2:], single) for g in grads],
        scratch_shapes=kept
        + from_core
        + from_bits
        + from_chips
        + [
            pltpu.SemaphoreType.DMA((len(plan), kinds)),
            pltpu.SemaphoreType.DMA((len(plan), kinds)),
            pltpu.SemaphoreType.DMA((len(plan),)),
        ],
        compiler_params=pltpu.CompilerParams(
            collective_id=collective_id, has_side_effects=True, vmem_limit_bytes=60 * 2**20
        ),
    )(*grads)


def exchange(blocks):
    size = lax.axis_size("seq")
    here = lax.axis_index("seq")
    out = place(jnp.zeros(blocks.shape, blocks.dtype), pick(blocks, here, 0), here, 0)
    for distance in range(1, size):
        peer = here ^ distance
        out = place(out, swap_seq(pick(blocks, peer, 0), distance), peer, 0)
    return out


def shards(
    inputs,
    cotangent,
    ln1_scale,
    ln1_offset,
    w_query,
    w_key,
    w_value,
    w_rel,
    content_bias,
    position_bias,
    w_out,
    b_out,
    ln2_scale,
    ln2_offset,
    w_in,
    b_in,
    w_mlp_out,
    b_mlp_out,
):
    win_size, seq_size = lax.axis_size("win"), lax.axis_size("seq")
    devices = win_size * seq_size
    seq = lax.axis_index("seq")
    window_count, row_count, width = inputs.shape
    tokens = window_count * row_count
    hk = HEADS * KD
    vd = width // HEADS
    hp = HEADS // seq_size
    hidden = w_in.shape[1]
    scale_factor = KD ** (-0.5)

    vectors = (
        ln1_scale,
        ln1_offset,
        content_bias,
        position_bias,
        b_out,
        ln2_scale,
        ln2_offset,
        b_in,
        b_mlp_out,
    )
    packed = jnp.concatenate(vectors + (w_rel.T.reshape(-1),))
    packed_size = packed.shape[0]
    small_cols = -(-packed_size // 4096) * 256
    small_size = 16 * small_cols
    packed = jnp.pad(packed, (0, small_size - packed_size)).reshape(16, small_cols)
    packed, whole_qk, whole_v = gather_all(
        (packed, jnp.concatenate([w_query, w_key], axis=1), w_value),
        (256, 512, 512),
        lambda number: number % 4 != 3,
        2,
        0,
    )
    packed = packed.reshape(devices, small_size)
    whole_qk = whole_qk.reshape(width, 2 * hk)
    whole_v = whole_v.reshape(width, width)
    whole_vectors = []
    at = 0
    for vector in vectors:
        length = vector.shape[0]
        whole_vectors.append(packed[:, at : at + length].reshape(devices * length).astype(single))
        at += length
    whole_rel = packed[:, at:packed_size].reshape(hk, F)
    (
        ln1_gain,
        ln1_shift,
        bias_content,
        bias_position,
        bias_out,
        ln2_gain,
        ln2_shift,
        bias_in,
        bias_mlp,
    ) = whole_vectors

    features = jnp.pad(rel_features(WLEN, F).astype(bfloat), ((0, 1), (0, 0)))
    own_rel = lax.dynamic_slice_in_dim(whole_rel, seq * hp * KD, hp * KD, 0)
    table = jnp.einsum("cf,tf->ct", own_rel, features, preferred_element_type=single).astype(bfloat)

    source = inputs.reshape(tokens, width).astype(single)
    normed_one_f, norm_one_back = jax.vjp(layer_norm, source, ln1_gain, ln1_shift)
    normed_one = normed_one_f.astype(bfloat)
    proj_qk = jnp.dot(normed_one, whole_qk, preferred_element_type=single)
    query = proj_qk[:, :hk] * scale_factor
    proj_v = jnp.dot(normed_one, whole_v, preferred_element_type=single)
    parts = (
        (query + bias_content).astype(bfloat),
        (query + bias_position).astype(bfloat),
        proj_qk[:, hk:].astype(bfloat),
        proj_v.astype(bfloat),
    )
    outgoing = jnp.concatenate([part.reshape(tokens, seq_size, -1) for part in parts], axis=2)
    outgoing = jnp.transpose(outgoing, (1, 0, 2))
    whole_out, whole_in, whole_mlp, heads_in, attention, attended = gather_and_attend(
        (w_out, w_in, w_mlp_out),
        (512, 512, 256),
        lambda number: number % 4 != 3,
        3,
        FIRST_BLOCK_TURN,
        outgoing,
        table,
        (hp, vd, BLOCK_Q),
    )
    whole_out = whole_out.reshape(width, width)
    whole_in = whole_in.reshape(width, hidden)
    whole_mlp = whole_mlp.reshape(hidden, width)
    attended = jnp.transpose(attended, (1, 0, 2)).reshape(tokens, width)

    hidden_in = source + jnp.dot(attended, whole_out, preferred_element_type=single) + bias_out
    normed_two_f, norm_two_back = jax.vjp(layer_norm, hidden_in, ln2_gain, ln2_shift)
    normed_two = normed_two_f.astype(bfloat)
    pre_act = jnp.dot(normed_two, whole_in, preferred_element_type=single) + bias_in
    gelu_out, gelu_back = jax.vjp(jax.nn.gelu, pre_act)
    activation = gelu_out.astype(bfloat)
    result = hidden_in + jnp.dot(activation, whole_mlp, preferred_element_type=single) + bias_mlp
    layer_out = result.astype(bfloat).reshape(inputs.shape)

    grid = (win_size // CORES, CORES) + (2,) * (seq_size.bit_length() - 1)

    def weight_grad(left, right):
        grad = jnp.einsum("td,te->de", left, right, preferred_element_type=single).astype(bfloat)
        rows, cols = grad.shape
        return grad.reshape(grid + (rows // devices, cols))

    cot_rows = cotangent.reshape(tokens, width)
    grad_mlp = weight_grad(activation, cot_rows)
    grad_bias_mlp = jnp.sum(cot_rows.astype(single), axis=0)
    grad_act = jnp.einsum("td,fd->tf", cot_rows, whole_mlp, preferred_element_type=single)
    grad_pre = gelu_back(grad_act)[0].astype(bfloat)
    grad_in = weight_grad(normed_two, grad_pre)
    grad_mlp, grad_in = scatter_all(
        (grad_mlp, grad_in), (256, 512), lambda number: number % 4 != 0, 2, 2
    )
    grad_bias_in = jnp.sum(grad_pre.astype(single), axis=0)
    grad_normed_two = jnp.einsum("tf,df->td", grad_pre, whole_in, preferred_element_type=single)
    hidden_term, grad_ln2_gain, grad_ln2_shift = norm_two_back(grad_normed_two)
    grad_hidden = cot_rows.astype(single) + hidden_term
    grad_branch = grad_hidden.astype(bfloat)
    grad_out = weight_grad(attended, grad_branch)
    grad_bias_out = jnp.sum(grad_branch.astype(single), axis=0)
    grad_mixed = jnp.einsum(
        "te,de->td", grad_branch, whole_out, preferred_element_type=single
    ).astype(bfloat)
    grad_mixed = jnp.transpose(grad_mixed.reshape(tokens, seq_size, hp * vd), (1, 0, 2))
    grad_heads = exchange(grad_mixed).reshape(seq_size * tokens, hp * vd)
    grad_q, grad_kv, grad_table, grad_bias = attention_backward(
        heads_in, table, attention, grad_heads, hp, vd, BLOCK_Q
    )
    own = hp * KD
    returned = exchange(
        jnp.concatenate([grad_q, grad_kv], axis=1).reshape(seq_size, tokens, 2 * own + hp * vd)
    )
    returned = jnp.transpose(returned, (1, 0, 2))
    grad_qk_rows = jnp.concatenate(
        [
            returned[:, :, :own].reshape(tokens, hk),
            returned[:, :, own : 2 * own].reshape(tokens, hk),
        ],
        axis=1,
    )
    grad_v_rows = returned[:, :, 2 * own :].reshape(tokens, width)
    grad_qk = weight_grad(normed_one, grad_qk_rows)
    grad_v = weight_grad(normed_one, grad_v_rows)
    grad_normed_one = jnp.einsum(
        "tk,dk->td", grad_qk_rows, whole_qk, preferred_element_type=single
    ) + jnp.einsum("tk,dk->td", grad_v_rows, whole_v, preferred_element_type=single)
    source_term, grad_ln1_gain, grad_ln1_shift = norm_one_back(grad_normed_one)
    grad_inputs = (grad_hidden + source_term).reshape(inputs.shape)

    grad_rel = jnp.dot(grad_table, features.astype(single), precision=lax.Precision.HIGHEST)
    whole_grad_rel = lax.dynamic_update_slice_in_dim(
        jnp.zeros((hk, F), single), grad_rel, seq * own, 0
    )

    def spread(own_heads):
        return lax.dynamic_update_slice_in_dim(jnp.zeros((hk,), single), own_heads, seq * own, 0)

    vector_grads = (
        grad_ln1_gain,
        grad_ln1_shift,
        spread(grad_bias[0]),
        spread(grad_bias[1]),
        grad_bias_out,
        grad_ln2_gain,
        grad_ln2_shift,
        grad_bias_in,
        grad_bias_mlp,
    )
    small = jnp.concatenate(
        [v.reshape(devices, -1) for v in vector_grads + (whole_grad_rel,)], axis=1
    )
    small = jnp.pad(small, ((0, 0), (0, small_size - packed_size))).astype(bfloat)
    grad_out, grad_qk, grad_v, small = scatter_all(
        (grad_out, grad_qk, grad_v, small.reshape(grid + (16, small_cols))),
        (512, 512, 512, 256),
        lambda number: number % 4 != 0,
        2,
        3,
    )
    small = small.reshape(-1)[:packed_size]
    small_grads = []
    at = 0
    for vector in vectors:
        length = vector.shape[0]
        small_grads.append(small[at : at + length])
        at += length
    g = small_grads
    own_grad_rel = small[at:].reshape(-1, F).T
    return (
        layer_out,
        grad_inputs,
        g[0],
        g[1],
        grad_qk[:, :hk],
        grad_qk[:, hk:],
        grad_v,
        own_grad_rel,
        g[2],
        g[3],
        grad_out,
        g[4],
        g[5],
        g[6],
        grad_in,
        g[7],
        grad_mlp,
        g[8],
    )


def solution(mesh):
    in_specs = (
        P("win", "seq", None),
        P("win", "seq", None),
        P(("win", "seq")),
        P(("win", "seq")),
        P(("win", "seq"), None),
        P(("win", "seq"), None),
        P(("win", "seq"), None),
        P(None, ("win", "seq")),
        P(("win", "seq")),
        P(("win", "seq")),
        P(("win", "seq"), None),
        P(("win", "seq")),
        P(("win", "seq")),
        P(("win", "seq")),
        P(("win", "seq"), None),
        P(("win", "seq")),
        P(("win", "seq"), None),
        P(("win", "seq")),
    )
    out_specs = (
        P("win", "seq", None),
        P("win", "seq", None),
        P(("win", "seq")),
        P(("win", "seq")),
        P(("win", "seq"), None),
        P(("win", "seq"), None),
        P(("win", "seq"), None),
        P(None, ("win", "seq")),
        P(("win", "seq")),
        P(("win", "seq")),
        P(("win", "seq"), None),
        P(("win", "seq")),
        P(("win", "seq")),
        P(("win", "seq")),
        P(("win", "seq"), None),
        P(("win", "seq")),
        P(("win", "seq"), None),
        P(("win", "seq")),
    )
    return jax.shard_map(shards, mesh=mesh, in_specs=in_specs, out_specs=out_specs, check_vma=False)
```

```python
import functools
import math

import jax
import jax.numpy as jnp
from jax import lax
from jax.experimental import pallas as pl
from jax.experimental.pallas import tpu as pltpu
from jax.sharding import PartitionSpec as P

HEADS = 8
KD = 64
F = 192
WLEN = 1536
CORES = 2
BLOCK_Q = 256
FIRST_BLOCK_TURN = 8
BLOCK_TURNS = (4, 6, 8, 10, 12, 13)
VMEM_LIMIT = 62 * 2**20
bfloat = jnp.bfloat16
single = jnp.float32


def rel_features(length, feature_count):
    per_basis = feature_count // 6
    offsets = jnp.arange(-length + 1, length).astype(jnp.float32)
    magnitude = jnp.abs(offsets)[:, None]
    half_life = 2.0 ** jnp.linspace(3.0, math.log2(length), per_basis)
    decaying = jnp.exp(-math.log(2.0) / half_life * magnitude)
    widths = 2.0 ** jnp.arange(1, per_basis + 1).astype(jnp.float32) - 1.0
    central = (widths > magnitude).astype(jnp.float32)
    stddev = length / (2.0 * per_basis)
    centers = jnp.linspace(length / per_basis, float(length), per_basis)
    shape_param = (centers / stddev) ** 2
    inverse_scale = centers / stddev**2
    peak_at = (shape_param - 1.0) / inverse_scale
    log_prob = (shape_param - 1.0) * (
        jnp.log(jnp.maximum(magnitude, 0.5)) - jnp.log(peak_at)
    ) - inverse_scale * (magnitude - peak_at)
    density = jnp.exp(log_prob) + 1e-08
    gamma_pdf = density / jnp.max(density, axis=0, keepdims=True)
    basis_set = jnp.concatenate([decaying, central, gamma_pdf], axis=1)
    return jnp.concatenate([basis_set, jnp.sign(offsets)[:, None] * basis_set], axis=1)


def layer_norm(values, norm_gain, norm_shift):
    centered = values - jnp.mean(values, axis=-1, keepdims=True)
    variance = jnp.mean(centered * centered, axis=-1, keepdims=True)
    return centered * lax.rsqrt(variance + 1e-05) * norm_gain + norm_shift


def attend_block(length, bq, hp, vd, block, x_ref, tab_ref, att_ref, mixed_ref):
    hk = hp * KD
    first = block * bq
    rows = pl.ds(first, bq)
    span = length + bq
    outs = []
    for h in range(hp):
        qc = x_ref[rows, pl.ds(h * KD, KD)]
        qp = x_ref[rows, pl.ds(hk + h * KD, KD)]
        k = x_ref[:, pl.ds(2 * hk + h * KD, KD)]
        v = x_ref[:, pl.ds(3 * hk + h * vd, vd)]
        table = tab_ref[pl.ds(h * KD, KD), pl.ds(length - bq - first, span)]
        raw = jnp.dot(qp, table, preferred_element_type=single)
        rel = pltpu.roll(raw, span - bq + 1, 1, stride=1, stride_axis=0)[:, :length]
        s = rel + lax.dot_general(qc, k, (((1,), (1,)), ((), ())), preferred_element_type=single)
        e = jnp.exp(s - jnp.max(s, axis=-1, keepdims=True))
        inverse = 1.0 / jnp.sum(e, axis=-1, keepdims=True)
        att = (e * inverse).astype(bfloat)
        att_ref[h] = att
        outs.append(jnp.dot(att, v, preferred_element_type=single).astype(bfloat))
    mixed_ref[rows, :] = jnp.concatenate(outs, axis=1) if hp > 1 else outs[0]


def attend_back(length, bq, hp, vd, block, x_ref, tab_ref, att_ref, gm_ref, ret_ref, sums):
    dk_ref, dv_ref, dtab_ref, bias_ref = sums
    hk = hp * KD
    first = block * bq
    rows = pl.ds(first, bq)
    span = length + bq
    row = lax.broadcasted_iota(jnp.int32, (bq, bq), 0)
    col = lax.broadcasted_iota(jnp.int32, (bq, bq), 1)
    flip = jnp.where(row + col == bq - 1, 1.0, 0.0).astype(bfloat)

    def flipped(v):
        return jnp.dot(flip, v, preferred_element_type=single)

    def dot(left, right, left_dim, right_dim):
        return lax.dot_general(
            left, right, (((left_dim,), (right_dim,)), ((), ())), preferred_element_type=single
        )

    dqs, bc, bp = [], [], []
    for h in range(hp):
        own = pl.ds(h * KD, KD)
        table_cols = pl.ds(length - bq - first, span)
        qc = flipped(x_ref[rows, own]).astype(bfloat)
        qp = flipped(x_ref[rows, pl.ds(hk + h * KD, KD)]).astype(bfloat)
        k = x_ref[:, pl.ds(2 * hk + h * KD, KD)]
        v = x_ref[:, pl.ds(3 * hk + h * vd, vd)]
        gm = gm_ref[rows, pl.ds(h * vd, vd)]
        att = att_ref[h]
        dv_ref[pl.ds(h * vd, vd), :] += dot(gm, att, 0, 0)
        dp = dot(flipped(gm).astype(bfloat), v, 1, 1)
        af = flipped(att)
        t = af * dp
        delta = jnp.sum(t, axis=-1, keepdims=True)
        ds = (t - af * delta).astype(bfloat)
        dk_ref[own, :] += dot(qc, ds, 0, 0)
        gc = jnp.dot(ds, k, preferred_element_type=single)
        wide = jnp.concatenate([ds.astype(single), jnp.zeros((bq, bq), single)], axis=1)
        rel = pltpu.roll(wide, 0, 1, stride=1, stride_axis=0).astype(bfloat)
        gp = dot(rel, tab_ref[own, table_cols], 1, 1)
        dtab_ref[own, table_cols] += dot(qp, rel, 0, 0)
        dqs.append(flipped(((gc + gp) * KD**-0.5).astype(bfloat)).astype(bfloat))
        bc.append(jnp.sum(gc, axis=0, keepdims=True))
        bp.append(jnp.sum(gp, axis=0, keepdims=True))
    ret_ref[rows, :hk] = jnp.concatenate(dqs, axis=1) if hp > 1 else dqs[0]
    bias_ref[0:1, :] += jnp.concatenate(bc, axis=1) if hp > 1 else bc[0]
    bias_ref[1:2, :] += jnp.concatenate(bp, axis=1) if hp > 1 else bp[0]


def partners():
    win, seq = lax.axis_index("win"), lax.axis_index("seq")
    chips = lax.axis_size("win") // CORES
    bits = lax.axis_size("seq").bit_length() - 1
    return win, seq, win // CORES, win % CORES, chips, bits


def start_together(whole_seq=False):
    win, seq, here, core, chips, bits = partners()
    barrier = pltpu.get_barrier_semaphore()

    def greet(to_win, to_seq):
        pl.semaphore_signal(
            barrier, inc=1, device_id=(to_win, to_seq), device_id_type=pl.DeviceIdType.MESH
        )

    greet(win ^ 1, seq)
    across = range(1, 1 << bits) if whole_seq else [1 << bit for bit in range(bits)]
    for distance in across:
        greet(win, seq ^ distance)

    @pl.when(here > 0)
    def _():
        greet(win - CORES, seq)

    @pl.when(here < chips - 1)
    def _():
        greet(win + CORES, seq)

    ends = jnp.where(here > 0, 1, 0) + jnp.where(here < chips - 1, 1, 0)
    pl.semaphore_wait(barrier, 1 + len(across) + ends)


def gather_work(plan, shards, outs, send_sem, recv_sem, local_sem):
    win, seq, here, core, chips, bits = partners()
    own_bits = tuple((seq >> bit) & 1 for bit in reversed(range(bits)))
    own_seq = {bit: (seq >> bit) & 1 for bit in range(bits)}

    def region(chunk, chip, done, lead=0, span=None):
        which, col, cols, _ = chunk
        start, size = (col + lead, cols) if span is None else (col + lead, span)
        index = tuple(slice(None) if bit in done else own_seq[bit] for bit in reversed(range(bits)))
        return outs[which].at[(chip, core) + index + (slice(None), pl.ds(start, size))]

    def copy(ref, number, kind, to_win, to_seq):
        return pltpu.make_async_remote_copy(
            src_ref=ref,
            dst_ref=ref,
            send_sem=send_sem.at[number, kind],
            recv_sem=recv_sem.at[number, kind],
            device_id=(to_win, to_seq),
            device_id_type=pl.DeviceIdType.MESH,
        )

    chip_steps = chips - 1
    every_bit = frozenset(range(bits))

    def guarded(condition, action):
        pl.when(condition)(action)

    def chip_stage(chunk, number, step, done):
        up_shard, down_shard = here - step, here + step
        up = copy(region(chunk, jnp.maximum(up_shard, 0), done), number, step, win + CORES, seq)
        down = copy(
            region(chunk, jnp.minimum(down_shard, chips - 1), done),
            number,
            chip_steps + step,
            win - CORES,
            seq,
        )
        sends_up = (up_shard >= 0) & (here < chips - 1)
        sends_down = (down_shard < chips) & (here > 0)
        gets_up = here >= step + 1
        gets_down = here + step + 1 < chips

        def start():
            guarded(sends_up, up.start)
            guarded(sends_down, down.start)

        def arrive():
            guarded(gets_up, up.wait_recv)
            guarded(gets_down, down.wait_recv)

        def finish():
            guarded(sends_up, up.wait_send)
            guarded(sends_down, down.wait_send)

        return start, arrive, finish

    def bit_stage(chunk, number, step, chip):
        half = chunk[2] // 2
        copies = []
        for part in range(2):
            order = list(range(bits)) if part == 0 else list(reversed(range(bits)))
            ref = region(chunk, chip, frozenset(order[:step]), part * half, half)
            kind = 2 * chip_steps + part * bits + step
            copies.append(copy(ref, number, kind, win, seq ^ (1 << order[step])))

        def start():
            for item in copies:
                item.start()

        def arrive():
            for item in copies:
                item.wait_recv()

        def finish():
            for item in copies:
                item.wait_send()

        return start, arrive, finish

    def core_stage(chunk, number):
        kind = 2 * chip_steps + 2 * bits
        item = copy(region(chunk, slice(None), every_bit), number, kind, win ^ 1, seq)
        return item.start, item.wait_recv, item.wait_send

    def stages(chunk, number):
        if chunk[3]:
            line = [chip_stage(chunk, number, step, frozenset()) for step in range(chip_steps)]
            cube = [bit_stage(chunk, number, step, slice(None)) for step in range(bits)]
            return line + cube + [core_stage(chunk, number)]
        cube = [bit_stage(chunk, number, step, here) for step in range(bits)]
        line = [chip_stage(chunk, number, step, every_bit) for step in range(chip_steps)]
        return cube + line + [core_stage(chunk, number)]

    own = [
        pltpu.make_async_copy(shard, out.at[(here, core) + own_bits], local_sem.at[which])
        for which, (shard, out) in enumerate(zip(shards, outs))
    ]
    return own, [stages(chunk, number) for number, chunk in enumerate(plan)]


def run_turn(work, spacing, turn, last=None):
    for number, stages in enumerate(work):
        at, off = divmod(turn - number, spacing)
        if off == 0 and 0 < at <= len(stages):
            stages[at - 1][1]()
            if at == len(stages) and last is not None:
                last(number)
        if off == 0 and 0 <= at < len(stages):
            stages[at][0]()


def turns_of(work, spacing):
    return len(work) + spacing * len(work[0])


def finish_sends(work):
    for stages in work:
        for stage in stages:
            stage[2]()


def gather_kernel(plan, count, spacing, *refs):
    shards, outs, sems = refs[:count], refs[count : 2 * count], refs[2 * count :]
    own, work = gather_work(plan, shards, outs, *sems)
    for item in own:
        item.start()
    start_together()
    for item in own:
        item.wait()
    for turn in range(turns_of(work, spacing)):
        run_turn(work, spacing, turn)
    finish_sends(work)


def gather_plan(shards, widths, lines_first):
    plan = []
    for which, (shard, width) in enumerate(zip(shards, widths)):
        for col in range(0, shard.shape[1], width):
            plan.append((which, col, width, lines_first(len(plan))))
    return tuple(plan)


def gather_sems(plan, count):
    chips = lax.axis_size("win") // CORES
    bits = lax.axis_size("seq").bit_length() - 1
    kinds = 2 * (chips - 1) + 2 * bits + 1
    return [
        pltpu.SemaphoreType.DMA((len(plan), kinds)),
        pltpu.SemaphoreType.DMA((len(plan), kinds)),
        pltpu.SemaphoreType.DMA((count,)),
    ]


def gathered_shapes(shards):
    chips = lax.axis_size("win") // CORES
    bits = lax.axis_size("seq").bit_length() - 1
    return [jax.ShapeDtypeStruct((chips, CORES) + (2,) * bits + s.shape, s.dtype) for s in shards]


def gather_all(shards, widths, lines_first, spacing, collective_id):
    plan = gather_plan(shards, widths, lines_first)
    return pl.pallas_call(
        functools.partial(gather_kernel, plan, len(shards), spacing),
        in_specs=[pl.BlockSpec(memory_space=pltpu.VMEM)] * len(shards),
        out_specs=[pl.BlockSpec(memory_space=pl.ANY)] * len(shards),
        out_shape=gathered_shapes(shards),
        scratch_shapes=gather_sems(plan, len(shards)),
        compiler_params=pltpu.CompilerParams(collective_id=collective_id, has_side_effects=True),
    )(*shards)


def exchange_work(parts, target, send_sem, recv_sem, local_sem):
    win, seq = lax.axis_index("win"), lax.axis_index("seq")
    items = []
    for peer, part in enumerate(parts):
        sent = pltpu.make_async_remote_copy(
            src_ref=part,
            dst_ref=target(seq),
            send_sem=send_sem.at[peer],
            recv_sem=recv_sem.at[seq],
            device_id=(win, peer),
            device_id_type=pl.DeviceIdType.MESH,
        )
        got = pltpu.make_async_remote_copy(
            src_ref=part,
            dst_ref=target(peer),
            send_sem=send_sem.at[peer],
            recv_sem=recv_sem.at[peer],
            device_id=(win, peer),
            device_id_type=pl.DeviceIdType.MESH,
        )
        own = pltpu.make_async_copy(part, target(peer), local_sem.at[peer])

        def start(peer=peer, sent=sent, own=own):
            pl.when(peer != seq)(sent.start)
            pl.when(peer == seq)(own.start)

        def arrive(peer=peer, got=got, own=own):
            pl.when(peer != seq)(got.wait_recv)
            pl.when(peer == seq)(own.wait)

        def finish(peer=peer, sent=sent):
            pl.when(peer != seq)(sent.wait_send)

        items.append((start, arrive, finish))
    return items


def attend_kernel(plan, count, spacing, first_turn, dims, *refs):
    hp, vd, bq = dims
    shards, (outgoing, tab_ref), refs = refs[:count], refs[count : count + 2], refs[count + 2 :]
    outs, (x_ref, att_out, attended), refs = refs[:count], refs[count : count + 3], refs[count + 3 :]
    att_ref, mixed_ref, *gather_refs = refs[:-7]
    in_send, in_recv, in_local, out_send, out_recv, out_local, att_sem = refs[-7:]
    length = x_ref.shape[0]
    peers, rows = outgoing.shape[0], outgoing.shape[1]
    own, work = gather_work(plan, shards, outs, *gather_refs)
    incoming = exchange_work(
        [outgoing.at[peer] for peer in range(peers)],
        lambda peer: x_ref.at[pl.ds(peer * rows, rows)],
        in_send,
        in_recv,
        in_local,
    )
    leaving = exchange_work(
        [mixed_ref.at[pl.ds(peer * rows, rows)] for peer in range(peers)],
        lambda peer: attended.at[peer],
        out_send,
        out_recv,
        out_local,
    )
    for item in own:
        item.start()
    start_together(True)
    for item in own:
        item.wait()
    for start, _, _ in incoming:
        start()
    blocks = length // bq
    kept = [
        pltpu.make_async_copy(
            att_ref.at[block % 2], att_out.at[:, pl.ds(block * bq, bq)], att_sem.at[block]
        )
        for block in range(blocks)
    ]
    sent = 0
    for turn in range(turns_of(work, spacing)):
        run_turn(work, spacing, turn)
        block = turn - first_turn
        if block == 0:
            for _, arrive, _ in incoming:
                arrive()
        if 0 <= block < blocks:
            if block >= 2:
                kept[block - 2].wait()
            attend_block(length, bq, hp, vd, block, x_ref, tab_ref, att_ref.at[block % 2], mixed_ref)
            kept[block].start()
            while sent < peers and (sent + 1) * rows <= (block + 1) * bq:
                leaving[sent][0]()
                sent += 1
    for _, arrive, _ in leaving:
        arrive()
    for _, _, finish in incoming + leaving:
        finish()
    for item in kept[-2:]:
        item.wait()
    finish_sends(work)


def gather_and_attend(shards, widths, lines_first, spacing, first_turn, outgoing, tab, dims):
    hp, vd, bq = dims
    peers, rows, cols = outgoing.shape
    length = peers * rows
    plan = gather_plan(shards, widths, lines_first)
    count = len(shards)
    anywhere = pl.BlockSpec(memory_space=pl.ANY)
    vmem = pl.BlockSpec(memory_space=pltpu.VMEM)
    dma = pltpu.SemaphoreType.DMA
    return pl.pallas_call(
        functools.partial(attend_kernel, plan, count, spacing, first_turn, dims),
        in_specs=[vmem] * count + [anywhere, vmem],
        out_specs=[anywhere] * count + [vmem, anywhere, anywhere],
        out_shape=gathered_shapes(shards)
        + [
            jax.ShapeDtypeStruct((length, cols), bfloat),
            jax.ShapeDtypeStruct((hp, length, length), bfloat),
            jax.ShapeDtypeStruct((peers, rows, hp * vd), bfloat),
        ],
        scratch_shapes=[
            pltpu.VMEM((2, hp, bq, length), bfloat),
            pltpu.VMEM((length, hp * vd), bfloat),
        ]
        + gather_sems(plan, count)
        + [dma((peers,))] * 6
        + [dma((length // bq,))],
        compiler_params=pltpu.CompilerParams(
            collective_id=1, has_side_effects=True, vmem_limit_bytes=VMEM_LIMIT
        ),
    )(*shards, outgoing, tab)


def scatter_work(plan, arrays, spacing, refs):
    count = len(arrays)
    sources, outs, rest = refs
    win, seq, here, core, chips, bits = partners()
    chip_steps = chips - 1
    ring, kept, rest = rest[:count], rest[count : 2 * count], rest[2 * count :]
    from_bits, rest = rest[: count * bits], rest[count * bits :]
    from_chips, rest = rest[:count], rest[count:]
    send_sem, recv_sem, local_sem = rest
    own_seq = {bit: (seq >> bit) & 1 for bit in range(bits)}

    def add(target, source):
        target[...] = (target[...].astype(single) + source[...].astype(single)).astype(bfloat)

    def slabs(chunk, chip, bit_index, lead=0, span=None):
        which, slot, _ = chunk
        index = tuple(bit_index.get(bit, slice(None)) for bit in reversed(range(bits)))
        width = arrays[which][1]
        columns = pl.ds(lead, width if span is None else span)
        return kept[which].at[(slot, chip) + index + (slice(None), columns)]

    def copy(src, dst, number, kind, to_win, to_seq):
        return pltpu.make_async_remote_copy(
            src_ref=src,
            dst_ref=dst,
            send_sem=send_sem.at[number, kind],
            recv_sem=recv_sem.at[number, kind],
            device_id=(to_win, to_seq),
            device_id_type=pl.DeviceIdType.MESH,
        )

    def core_stage(chunk, number):
        which, slot, _ = chunk
        width = arrays[which][1]
        product = isinstance(sources[which], tuple)
        held = ring[which].at[slot % spacing]
        columns = (slice(None),) * bits + (slice(None), pl.ds(slot * width, width))
        if product:
            leaving, own = held.at[:, 1 - core], held.at[:, core]
        else:
            leaving, own = sources[which].at[(slice(None), 1 - core) + columns], held
        kind = 2 * chip_steps + 2 * bits
        item = copy(leaving, kept[which].at[slot], number, kind, win ^ 1, seq)
        if not product:
            placed = pltpu.make_async_copy(
                sources[which].at[(slice(None), core) + columns], held, local_sem.at[number]
            )

        def start():
            if product:
                left, right = sources[which]
                grad = lax.dot_general(
                    left[...],
                    right[:, pl.ds(slot * width, width)],
                    (((0,), (0,)), ((), ())),
                    preferred_element_type=single,
                )
                held[...] = grad.astype(bfloat).reshape(held.shape)
            else:
                placed.start()
            item.start()

        def arrive():
            if not product:
                placed.wait()
            item.wait_recv()
            add(kept[which].at[slot], own)
            item.wait_send()

        return start, arrive, lambda: None

    def bit_stage(chunk, number, step, chip):
        which, slot, _ = chunk
        half = arrays[which][1] // 2
        items = []
        for part in range(2):
            order = list(range(bits)) if part else list(reversed(range(bits)))
            bit = order[step]
            done = {b: own_seq[b] for b in order[:step]}
            kind = 2 * chip_steps + part * bits + step
            buffer = from_bits[which * bits + step]
            target = buffer.at[(slot, part) if isinstance(chip, slice) else (slot, part, 0)]
            leaving = slabs(chunk, chip, done | {bit: 1 - own_seq[bit]}, part * half, half)
            staying = slabs(chunk, chip, done | {bit: own_seq[bit]}, part * half, half)
            sent = copy(leaving, target, number, kind, win, seq ^ (1 << bit))
            items.append((sent, staying, target))

        def start():
            for sent, _, _ in items:
                sent.start()

        def arrive():
            for sent, staying, target in items:
                sent.wait_recv()
                add(staying, target)

        def finish():
            for sent, _, _ in items:
                sent.wait_send()

        return start, arrive, finish

    def chip_stage(chunk, number, step, bit_index):
        which, slot, lines_last = chunk
        part = (0,) * bits if lines_last else ()
        up_to, down_to = here + step, here - step
        up_slot = from_chips[which].at[(slot, step - 1) + part]
        down_slot = from_chips[which].at[(slot, chip_steps + step - 1) + part]
        up = copy(
            slabs(chunk, jnp.minimum(up_to, chips - 1), bit_index),
            up_slot,
            number,
            step - 1,
            win + CORES,
            seq,
        )
        down = copy(
            slabs(chunk, jnp.maximum(down_to, 0), bit_index),
            down_slot,
            number,
            chip_steps + step - 1,
            win - CORES,
            seq,
        )
        sends_up, sends_down = up_to < chips, down_to >= 0
        gets_up = (here >= 1) & (here - 1 + step < chips)
        gets_down = (here + 1 < chips) & (here + 1 - step >= 0)

        def start():
            pl.when(sends_up)(up.start)
            pl.when(sends_down)(down.start)

        def arrive():
            @pl.when(gets_up)
            def _():
                up.wait_recv()
                add(slabs(chunk, jnp.minimum(here + step - 1, chips - 1), bit_index), up_slot)

            @pl.when(gets_down)
            def _():
                down.wait_recv()
                add(slabs(chunk, jnp.maximum(here - step + 1, 0), bit_index), down_slot)

        def finish():
            pl.when(sends_up)(up.wait_send)
            pl.when(sends_down)(down.wait_send)

        return start, arrive, finish

    def stages(chunk, number):
        steps = range(chip_steps, 0, -1)
        if chunk[2]:
            cube = [bit_stage(chunk, number, step, slice(None)) for step in range(bits)]
            line = [chip_stage(chunk, number, step, own_seq) for step in steps]
            return [core_stage(chunk, number)] + cube + line
        line = [chip_stage(chunk, number, step, {}) for step in steps]
        cube = [bit_stage(chunk, number, step, here) for step in range(bits)]
        return [core_stage(chunk, number)] + line + cube

    def last(number):
        chunk = plan[number]
        which, slot, _ = chunk
        width = arrays[which][1]
        total = slabs(chunk, here, own_seq)[...].astype(single)
        outs[which][:, pl.ds(slot * width, width)] = total

    return [stages(chunk, number) for number, chunk in enumerate(plan)], last


def scatter_plan(grads, widths, lines_last):
    devices = lax.axis_size("win") * lax.axis_size("seq")
    plan, arrays = [], []
    for which, (grad, width) in enumerate(zip(grads, widths)):
        if isinstance(grad, tuple):
            rows, cols = grad[0].shape[1] // devices, grad[1].shape[1]
        else:
            rows, cols = grad.shape[-2:]
        slots = cols // width
        lasts = [lines_last(len(plan) + slot) for slot in range(slots)]
        plan += [(which, slot, last) for slot, last in enumerate(lasts)]
        arrays.append((rows, width, slots, isinstance(grad, tuple)))
    return tuple(plan), tuple(arrays)


def scatter_scratch(plan, arrays, spacing):
    chips = lax.axis_size("win") // CORES
    bits = lax.axis_size("seq").bit_length() - 1
    cube = (2,) * bits
    ring, kept, from_bits, from_chips = [], [], [], []
    for which, (rows, width, slots, product) in enumerate(arrays):
        halves = (CORES,) if product else ()
        ring.append(pltpu.VMEM((spacing, chips) + halves + cube + (rows, width), bfloat))
        kept.append(pltpu.VMEM((slots, chips) + cube + (rows, width), bfloat))
        for step in range(bits):
            left = (2,) * (bits - 1 - step)
            from_bits.append(pltpu.VMEM((slots, 2, chips) + left + (rows, width // 2), bfloat))
        lone = (1,) * bits if all(c[2] for c in plan if c[0] == which) else cube
        from_chips.append(pltpu.VMEM((slots, 2 * (chips - 1)) + lone + (rows, width), bfloat))
    kinds = 2 * (chips - 1) + 2 * bits + 1
    dma = pltpu.SemaphoreType.DMA
    sems = [dma((len(plan), kinds)), dma((len(plan), kinds)), dma((len(plan),))]
    return ring + kept + from_bits + from_chips + sems


def flat_sources(grads):
    flat, specs = [], []
    for grad in grads:
        whole = isinstance(grad, tuple)
        flat += grad if whole else (grad,)
        specs += [pl.BlockSpec(memory_space=pltpu.VMEM if whole else pl.ANY)] * (2 if whole else 1)
    return flat, specs


def group_sources(arrays, refs):
    sources = []
    for _, _, _, product in arrays:
        sources.append((refs[0], refs[1]) if product else refs[0])
        refs = refs[2 if product else 1 :]
    return sources, refs


def scatter_kernel(plan, arrays, spacing, *refs):
    count = len(arrays)
    sources, refs = group_sources(arrays, refs)
    start_together()
    work, last = scatter_work(plan, arrays, spacing, (sources, refs[:count], refs[count:]))
    for turn in range(turns_of(work, spacing)):
        run_turn(work, spacing, turn, last)
    finish_sends(work)


def scatter_all(grads, widths, lines_last, spacing, collective_id):
    plan, arrays = scatter_plan(grads, widths, lines_last)
    flat, specs = flat_sources(grads)
    return pl.pallas_call(
        functools.partial(scatter_kernel, plan, arrays, spacing),
        in_specs=specs,
        out_specs=[pl.BlockSpec(memory_space=pltpu.VMEM)] * len(grads),
        out_shape=[jax.ShapeDtypeStruct((a[0], a[1] * a[2]), single) for a in arrays],
        scratch_shapes=scatter_scratch(plan, arrays, spacing),
        compiler_params=pltpu.CompilerParams(
            collective_id=collective_id, has_side_effects=True, vmem_limit_bytes=VMEM_LIMIT
        ),
    )(*flat)


def attend_back_kernel(plan, arrays, spacing, block_turns, dims, *refs):
    hp, vd, bq = dims
    count = len(arrays)
    sources, refs = group_sources(arrays, refs)
    (leaving_ref, x_ref, tab_ref, att_in), refs = refs[:4], refs[4:]
    outs, (returned, dtab_ref, bias_ref), refs = refs[:count], refs[count : count + 3], refs[count + 3 :]
    gm_ref, ret_ref, att_ref, dk_ref, dv_ref, *scatter_refs = refs[:-7]
    in_send, in_recv, in_local, out_send, out_recv, out_local, att_sem = refs[-7:]
    length = x_ref.shape[0]
    hk = hp * KD
    peers, rows = leaving_ref.shape[:2]
    blocks = length // bq
    incoming = exchange_work(
        [leaving_ref.at[peer] for peer in range(peers)],
        lambda peer: gm_ref.at[pl.ds(peer * rows, rows)],
        in_send,
        in_recv,
        in_local,
    )
    leaving = exchange_work(
        [ret_ref.at[pl.ds(peer * rows, rows)] for peer in range(peers)],
        lambda peer: returned.at[peer],
        out_send,
        out_recv,
        out_local,
    )
    loads = [
        pltpu.make_async_copy(
            att_in.at[:, pl.ds(block * bq, bq)], att_ref.at[block % 2], att_sem.at[block]
        )
        for block in range(blocks)
    ]
    for load in loads[:2]:
        load.start()
    start_together(True)
    for start, _, _ in incoming:
        start()
    work, last = scatter_work(plan, arrays, spacing, (sources, outs, scatter_refs))
    dk_ref[...] = jnp.zeros_like(dk_ref)
    dv_ref[...] = jnp.zeros_like(dv_ref)
    dtab_ref[...] = jnp.zeros_like(dtab_ref)
    bias_ref[...] = jnp.zeros_like(bias_ref)
    for turn in range(turns_of(work, spacing)):
        run_turn(work, spacing, turn, last)
        for block in range(blocks):
            if block_turns[block] != turn:
                continue
            if block == 0:
                for _, arrive, _ in incoming:
                    arrive()
            loads[block].wait()
            attend_back(
                length,
                bq,
                hp,
                vd,
                block,
                x_ref,
                tab_ref,
                att_ref.at[block % 2],
                gm_ref,
                ret_ref,
                (dk_ref, dv_ref, dtab_ref, bias_ref),
            )
            if block + 2 < blocks:
                loads[block + 2].start()
            if block == blocks - 1:
                ret_ref[:, hk : 2 * hk] = dk_ref[...].T.astype(bfloat)
                ret_ref[:, 2 * hk :] = dv_ref[...].T.astype(bfloat)
                for start, _, _ in leaving:
                    start()
    for _, arrive, _ in leaving:
        arrive()
    for _, _, finish in incoming + leaving:
        finish()
    finish_sends(work)


def scatter_and_attend_back(
    grads, widths, lines_last, spacing, block_turns, leaving, x, tab, attention, dims
):
    hp, vd, bq = dims
    peers, rows, _ = leaving.shape
    length = peers * rows
    hk = hp * KD
    back = 2 * hk + hp * vd
    plan, arrays = scatter_plan(grads, widths, lines_last)
    flat, specs = flat_sources(grads)
    anywhere = pl.BlockSpec(memory_space=pl.ANY)
    vmem = pl.BlockSpec(memory_space=pltpu.VMEM)
    dma = pltpu.SemaphoreType.DMA
    return pl.pallas_call(
        functools.partial(attend_back_kernel, plan, arrays, spacing, block_turns, dims),
        in_specs=specs + [anywhere, vmem, vmem, anywhere],
        out_specs=[vmem] * len(grads) + [anywhere, vmem, vmem],
        out_shape=[jax.ShapeDtypeStruct((a[0], a[1] * a[2]), single) for a in arrays]
        + [
            jax.ShapeDtypeStruct((peers, rows, back), bfloat),
            jax.ShapeDtypeStruct(tab.shape, single),
            jax.ShapeDtypeStruct((8, hk), single),
        ],
        scratch_shapes=[
            pltpu.VMEM((length, hp * vd), bfloat),
            pltpu.VMEM((length, back), bfloat),
            pltpu.VMEM((2, hp, bq, length), bfloat),
            pltpu.VMEM((hk, length), single),
            pltpu.VMEM((hp * vd, length), single),
        ]
        + scatter_scratch(plan, arrays, spacing)
        + [dma((peers,))] * 6
        + [dma((length // bq,))],
        compiler_params=pltpu.CompilerParams(
            collective_id=2, has_side_effects=True, vmem_limit_bytes=VMEM_LIMIT
        ),
    )(*flat, leaving, x, tab, attention)


def shards(
    inputs,
    cotangent,
    ln1_scale,
    ln1_offset,
    w_query,
    w_key,
    w_value,
    w_rel,
    content_bias,
    position_bias,
    w_out,
    b_out,
    ln2_scale,
    ln2_offset,
    w_in,
    b_in,
    w_mlp_out,
    b_mlp_out,
):
    win_size, seq_size = lax.axis_size("win"), lax.axis_size("seq")
    devices = win_size * seq_size
    seq = lax.axis_index("seq")
    window_count, row_count, width = inputs.shape
    tokens = window_count * row_count
    hk = HEADS * KD
    vd = width // HEADS
    hp = HEADS // seq_size
    hidden = w_in.shape[1]
    scale_factor = KD ** (-0.5)

    vectors = (
        ln1_scale,
        ln1_offset,
        content_bias,
        position_bias,
        b_out,
        ln2_scale,
        ln2_offset,
        b_in,
        b_mlp_out,
    )
    packed = jnp.concatenate(vectors + (w_rel.T.reshape(-1),))
    packed_size = packed.shape[0]
    small_cols = -(-packed_size // 4096) * 256
    small_size = 16 * small_cols
    packed = jnp.pad(packed, (0, small_size - packed_size)).reshape(16, small_cols)
    packed, whole_qk, whole_v = gather_all(
        (packed, jnp.concatenate([w_query, w_key], axis=1), w_value),
        (256, 512, 512),
        lambda number: number % 4 != 3,
        2,
        0,
    )
    packed = packed.reshape(devices, small_size)
    whole_qk = whole_qk.reshape(width, 2 * hk)
    whole_v = whole_v.reshape(width, width)
    whole_vectors = []
    at = 0
    for vector in vectors:
        length = vector.shape[0]
        whole_vectors.append(packed[:, at : at + length].reshape(devices * length).astype(single))
        at += length
    whole_rel = packed[:, at:packed_size].reshape(hk, F)
    (
        ln1_gain,
        ln1_shift,
        bias_content,
        bias_position,
        bias_out,
        ln2_gain,
        ln2_shift,
        bias_in,
        bias_mlp,
    ) = whole_vectors

    features = jnp.pad(rel_features(WLEN, F).astype(bfloat), ((0, 1), (0, 0)))
    own_rel = lax.dynamic_slice_in_dim(whole_rel, seq * hp * KD, hp * KD, 0)
    table = jnp.einsum("cf,tf->ct", own_rel, features, preferred_element_type=single).astype(bfloat)

    source = inputs.reshape(tokens, width).astype(single)
    normed_one_f, norm_one_back = jax.vjp(layer_norm, source, ln1_gain, ln1_shift)
    normed_one = normed_one_f.astype(bfloat)
    proj_qk = jnp.dot(normed_one, whole_qk, preferred_element_type=single)
    query = proj_qk[:, :hk] * scale_factor
    proj_v = jnp.dot(normed_one, whole_v, preferred_element_type=single)
    parts = (
        (query + bias_content).astype(bfloat),
        (query + bias_position).astype(bfloat),
        proj_qk[:, hk:].astype(bfloat),
        proj_v.astype(bfloat),
    )
    outgoing = jnp.concatenate([part.reshape(tokens, seq_size, -1) for part in parts], axis=2)
    outgoing = jnp.transpose(outgoing, (1, 0, 2))
    whole_out, whole_in, whole_mlp, heads_in, attention, attended = gather_and_attend(
        (w_out, w_in, w_mlp_out),
        (512, 512, 256),
        lambda number: number % 4 != 3,
        3,
        FIRST_BLOCK_TURN,
        outgoing,
        table,
        (hp, vd, BLOCK_Q),
    )
    whole_out = whole_out.reshape(width, width)
    whole_in = whole_in.reshape(width, hidden)
    whole_mlp = whole_mlp.reshape(hidden, width)
    attended = jnp.transpose(attended, (1, 0, 2)).reshape(tokens, width)

    hidden_in = source + jnp.dot(attended, whole_out, preferred_element_type=single) + bias_out
    normed_two_f, norm_two_back = jax.vjp(layer_norm, hidden_in, ln2_gain, ln2_shift)
    normed_two = normed_two_f.astype(bfloat)
    pre_act = jnp.dot(normed_two, whole_in, preferred_element_type=single) + bias_in
    gelu_out, gelu_back = jax.vjp(jax.nn.gelu, pre_act)
    activation = gelu_out.astype(bfloat)
    result = hidden_in + jnp.dot(activation, whole_mlp, preferred_element_type=single) + bias_mlp
    layer_out = result.astype(bfloat).reshape(inputs.shape)

    grid = (win_size // CORES, CORES) + (2,) * (seq_size.bit_length() - 1)

    def weight_grad(left, right):
        if left.shape[1] // devices % 16 == 0:
            return left, right
        grad = jnp.einsum("td,te->de", left, right, preferred_element_type=single).astype(bfloat)
        rows, cols = grad.shape
        return grad.reshape(grid + (rows // devices, cols))

    cot_rows = cotangent.reshape(tokens, width)
    grad_mlp = weight_grad(activation, cot_rows)
    grad_bias_mlp = jnp.sum(cot_rows.astype(single), axis=0)
    grad_act = jnp.einsum("td,fd->tf", cot_rows, whole_mlp, preferred_element_type=single)
    grad_pre = gelu_back(grad_act)[0].astype(bfloat)
    grad_in = weight_grad(normed_two, grad_pre)
    grad_bias_in = jnp.sum(grad_pre.astype(single), axis=0)
    grad_normed_two = jnp.einsum("tf,df->td", grad_pre, whole_in, preferred_element_type=single)
    hidden_term, grad_ln2_gain, grad_ln2_shift = norm_two_back(grad_normed_two)
    grad_hidden = cot_rows.astype(single) + hidden_term
    grad_branch = grad_hidden.astype(bfloat)
    grad_out = weight_grad(attended, grad_branch)
    grad_bias_out = jnp.sum(grad_branch.astype(single), axis=0)
    grad_mixed = jnp.einsum(
        "te,de->td", grad_branch, whole_out, preferred_element_type=single
    ).astype(bfloat)
    grad_mixed = jnp.transpose(grad_mixed.reshape(tokens, seq_size, hp * vd), (1, 0, 2))
    grad_mlp, grad_in, returned, grad_table, grad_bias = scatter_and_attend_back(
        (grad_mlp, grad_in),
        (256, 512),
        lambda number: number % 4 != 0,
        2,
        BLOCK_TURNS,
        grad_mixed,
        heads_in,
        table,
        attention,
        (hp, vd, BLOCK_Q),
    )
    own = hp * KD
    returned = jnp.transpose(returned, (1, 0, 2))
    grad_qk_rows = jnp.concatenate(
        [
            returned[:, :, :own].reshape(tokens, hk),
            returned[:, :, own : 2 * own].reshape(tokens, hk),
        ],
        axis=1,
    )
    grad_v_rows = returned[:, :, 2 * own :].reshape(tokens, width)
    grad_qk = weight_grad(normed_one, grad_qk_rows)
    grad_v = weight_grad(normed_one, grad_v_rows)
    grad_normed_one = jnp.einsum(
        "tk,dk->td", grad_qk_rows, whole_qk, preferred_element_type=single
    ) + jnp.einsum("tk,dk->td", grad_v_rows, whole_v, preferred_element_type=single)
    source_term, grad_ln1_gain, grad_ln1_shift = norm_one_back(grad_normed_one)
    grad_inputs = (grad_hidden + source_term).reshape(inputs.shape)

    grad_rel = jnp.dot(grad_table, features.astype(single), precision=lax.Precision.HIGHEST)
    whole_grad_rel = lax.dynamic_update_slice_in_dim(
        jnp.zeros((hk, F), single), grad_rel, seq * own, 0
    )

    def spread(own_heads):
        return lax.dynamic_update_slice_in_dim(jnp.zeros((hk,), single), own_heads, seq * own, 0)

    vector_grads = (
        grad_ln1_gain,
        grad_ln1_shift,
        spread(grad_bias[0]),
        spread(grad_bias[1]),
        grad_bias_out,
        grad_ln2_gain,
        grad_ln2_shift,
        grad_bias_in,
        grad_bias_mlp,
    )
    small = jnp.concatenate(
        [v.reshape(devices, -1) for v in vector_grads + (whole_grad_rel,)], axis=1
    )
    small = jnp.pad(small, ((0, 0), (0, small_size - packed_size))).astype(bfloat)
    grad_out, grad_qk, grad_v, small = scatter_all(
        (grad_out, grad_qk, grad_v, small.reshape(grid + (16, small_cols))),
        (512, 512, 512, 256),
        lambda number: number % 4 != 0,
        2,
        3,
    )
    small = small.reshape(-1)[:packed_size]
    small_grads = []
    at = 0
    for vector in vectors:
        length = vector.shape[0]
        small_grads.append(small[at : at + length])
        at += length
    g = small_grads
    own_grad_rel = small[at:].reshape(-1, F).T
    return (
        layer_out,
        grad_inputs,
        g[0],
        g[1],
        grad_qk[:, :hk],
        grad_qk[:, hk:],
        grad_v,
        own_grad_rel,
        g[2],
        g[3],
        grad_out,
        g[4],
        g[5],
        g[6],
        grad_in,
        g[7],
        grad_mlp,
        g[8],
    )


def solution(mesh):
    in_specs = (
        P("win", "seq", None),
        P("win", "seq", None),
        P(("win", "seq")),
        P(("win", "seq")),
        P(("win", "seq"), None),
        P(("win", "seq"), None),
        P(("win", "seq"), None),
        P(None, ("win", "seq")),
        P(("win", "seq")),
        P(("win", "seq")),
        P(("win", "seq"), None),
        P(("win", "seq")),
        P(("win", "seq")),
        P(("win", "seq")),
        P(("win", "seq"), None),
        P(("win", "seq")),
        P(("win", "seq"), None),
        P(("win", "seq")),
    )
    out_specs = (
        P("win", "seq", None),
        P("win", "seq", None),
        P(("win", "seq")),
        P(("win", "seq")),
        P(("win", "seq"), None),
        P(("win", "seq"), None),
        P(("win", "seq"), None),
        P(None, ("win", "seq")),
        P(("win", "seq")),
        P(("win", "seq")),
        P(("win", "seq"), None),
        P(("win", "seq")),
        P(("win", "seq")),
        P(("win", "seq")),
        P(("win", "seq"), None),
        P(("win", "seq")),
        P(("win", "seq"), None),
        P(("win", "seq")),
    )
    return jax.shard_map(shards, mesh=mesh, in_specs=in_specs, out_specs=out_specs, check_vma=False)
```

```python
import functools
import math

import jax
import jax.numpy as jnp
from jax import lax
from jax.experimental import pallas as pl
from jax.experimental.pallas import tpu as pltpu
from jax.sharding import PartitionSpec as P

HEADS = 8
KD = 64
F = 192
WLEN = 1536
CORES = 2
BLOCK_Q = 256
FIRST_BLOCK_TURN = 8
BLOCK_TURNS = (6, 8, 10, 12, 14, 16)
VMEM_LIMIT = 62 * 2**20
bfloat = jnp.bfloat16
single = jnp.float32


def rel_features(length, feature_count):
    per_basis = feature_count // 6
    offsets = jnp.arange(-length + 1, length).astype(jnp.float32)
    magnitude = jnp.abs(offsets)[:, None]
    half_life = 2.0 ** jnp.linspace(3.0, math.log2(length), per_basis)
    decaying = jnp.exp(-math.log(2.0) / half_life * magnitude)
    widths = 2.0 ** jnp.arange(1, per_basis + 1).astype(jnp.float32) - 1.0
    central = (widths > magnitude).astype(jnp.float32)
    stddev = length / (2.0 * per_basis)
    centers = jnp.linspace(length / per_basis, float(length), per_basis)
    shape_param = (centers / stddev) ** 2
    inverse_scale = centers / stddev**2
    peak_at = (shape_param - 1.0) / inverse_scale
    log_prob = (shape_param - 1.0) * (
        jnp.log(jnp.maximum(magnitude, 0.5)) - jnp.log(peak_at)
    ) - inverse_scale * (magnitude - peak_at)
    density = jnp.exp(log_prob) + 1e-08
    gamma_pdf = density / jnp.max(density, axis=0, keepdims=True)
    basis_set = jnp.concatenate([decaying, central, gamma_pdf], axis=1)
    return jnp.concatenate([basis_set, jnp.sign(offsets)[:, None] * basis_set], axis=1)


def layer_norm(values, norm_gain, norm_shift):
    centered = values - jnp.mean(values, axis=-1, keepdims=True)
    variance = jnp.mean(centered * centered, axis=-1, keepdims=True)
    return centered * lax.rsqrt(variance + 1e-05) * norm_gain + norm_shift


def attend_block(length, bq, hp, vd, block, x_ref, tab_ref, att_ref, mixed_ref):
    hk = hp * KD
    first = block * bq
    rows = pl.ds(first, bq)
    span = length + bq
    outs = []
    for h in range(hp):
        qc = x_ref[rows, pl.ds(h * KD, KD)]
        qp = x_ref[rows, pl.ds(hk + h * KD, KD)]
        k = x_ref[:, pl.ds(2 * hk + h * KD, KD)]
        v = x_ref[:, pl.ds(3 * hk + h * vd, vd)]
        table = tab_ref[pl.ds(h * KD, KD), pl.ds(length - bq - first, span)]
        raw = jnp.dot(qp, table, preferred_element_type=single)
        rel = pltpu.roll(raw, span - bq + 1, 1, stride=1, stride_axis=0)[:, :length]
        s = rel + lax.dot_general(qc, k, (((1,), (1,)), ((), ())), preferred_element_type=single)
        e = jnp.exp(s - jnp.max(s, axis=-1, keepdims=True))
        inverse = 1.0 / jnp.sum(e, axis=-1, keepdims=True)
        att = (e * inverse).astype(bfloat)
        att_ref[h] = att
        outs.append(jnp.dot(att, v, preferred_element_type=single).astype(bfloat))
    mixed_ref[rows, :] = jnp.concatenate(outs, axis=1) if hp > 1 else outs[0]


def attend_back(length, bq, hp, vd, block, x_ref, tab_ref, att_ref, gm_ref, ret_ref, sums):
    dk_ref, dv_ref, dtab_ref, bias_ref = sums
    hk = hp * KD
    first = block * bq
    rows = pl.ds(first, bq)
    span = length + bq
    row = lax.broadcasted_iota(jnp.int32, (bq, bq), 0)
    col = lax.broadcasted_iota(jnp.int32, (bq, bq), 1)
    flip = jnp.where(row + col == bq - 1, 1.0, 0.0).astype(bfloat)

    def flipped(v):
        return jnp.dot(flip, v, preferred_element_type=single)

    def dot(left, right, left_dim, right_dim):
        return lax.dot_general(
            left, right, (((left_dim,), (right_dim,)), ((), ())), preferred_element_type=single
        )

    dqs, bc, bp = [], [], []
    for h in range(hp):
        own = pl.ds(h * KD, KD)
        table_cols = pl.ds(length - bq - first, span)
        qc = flipped(x_ref[rows, own]).astype(bfloat)
        qp = flipped(x_ref[rows, pl.ds(hk + h * KD, KD)]).astype(bfloat)
        k = x_ref[:, pl.ds(2 * hk + h * KD, KD)]
        v = x_ref[:, pl.ds(3 * hk + h * vd, vd)]
        gm = gm_ref[rows, pl.ds(h * vd, vd)]
        att = att_ref[h]
        dv_ref[pl.ds(h * vd, vd), :] += dot(gm, att, 0, 0)
        dp = dot(flipped(gm).astype(bfloat), v, 1, 1)
        af = flipped(att)
        t = af * dp
        delta = jnp.sum(t, axis=-1, keepdims=True)
        ds = (t - af * delta).astype(bfloat)
        dk_ref[own, :] += dot(qc, ds, 0, 0)
        gc = jnp.dot(ds, k, preferred_element_type=single)
        wide = jnp.concatenate([ds.astype(single), jnp.zeros((bq, bq), single)], axis=1)
        rel = pltpu.roll(wide, 0, 1, stride=1, stride_axis=0).astype(bfloat)
        gp = dot(rel, tab_ref[own, table_cols], 1, 1)
        dtab_ref[own, table_cols] += dot(qp, rel, 0, 0)
        dqs.append(flipped(((gc + gp) * KD**-0.5).astype(bfloat)).astype(bfloat))
        bc.append(jnp.sum(gc, axis=0, keepdims=True))
        bp.append(jnp.sum(gp, axis=0, keepdims=True))
    ret_ref[rows, :hk] = jnp.concatenate(dqs, axis=1) if hp > 1 else dqs[0]
    bias_ref[0:1, :] += jnp.concatenate(bc, axis=1) if hp > 1 else bc[0]
    bias_ref[1:2, :] += jnp.concatenate(bp, axis=1) if hp > 1 else bp[0]


def partners():
    win, seq = lax.axis_index("win"), lax.axis_index("seq")
    chips = lax.axis_size("win") // CORES
    bits = lax.axis_size("seq").bit_length() - 1
    return win, seq, win // CORES, win % CORES, chips, bits


def start_together(whole_seq=False):
    win, seq, here, core, chips, bits = partners()
    barrier = pltpu.get_barrier_semaphore()

    def greet(to_win, to_seq):
        pl.semaphore_signal(
            barrier, inc=1, device_id=(to_win, to_seq), device_id_type=pl.DeviceIdType.MESH
        )

    greet(win ^ 1, seq)
    across = range(1, 1 << bits) if whole_seq else [1 << bit for bit in range(bits)]
    for distance in across:
        greet(win, seq ^ distance)

    @pl.when(here > 0)
    def _():
        greet(win - CORES, seq)

    @pl.when(here < chips - 1)
    def _():
        greet(win + CORES, seq)

    ends = jnp.where(here > 0, 1, 0) + jnp.where(here < chips - 1, 1, 0)
    pl.semaphore_wait(barrier, 1 + len(across) + ends)


def gather_work(plan, shards, outs, send_sem, recv_sem, local_sem):
    win, seq, here, core, chips, bits = partners()
    own_bits = tuple((seq >> bit) & 1 for bit in reversed(range(bits)))
    own_seq = {bit: (seq >> bit) & 1 for bit in range(bits)}

    def region(chunk, chip, done, lead=0, span=None):
        which, col, cols, _ = chunk
        start, size = (col + lead, cols) if span is None else (col + lead, span)
        index = tuple(slice(None) if bit in done else own_seq[bit] for bit in reversed(range(bits)))
        return outs[which].at[(chip, core) + index + (slice(None), pl.ds(start, size))]

    def copy(ref, number, kind, to_win, to_seq):
        return pltpu.make_async_remote_copy(
            src_ref=ref,
            dst_ref=ref,
            send_sem=send_sem.at[number, kind],
            recv_sem=recv_sem.at[number, kind],
            device_id=(to_win, to_seq),
            device_id_type=pl.DeviceIdType.MESH,
        )

    chip_steps = chips - 1
    every_bit = frozenset(range(bits))

    def guarded(condition, action):
        pl.when(condition)(action)

    def chip_stage(chunk, number, step, done):
        up_shard, down_shard = here - step, here + step
        up = copy(region(chunk, jnp.maximum(up_shard, 0), done), number, step, win + CORES, seq)
        down = copy(
            region(chunk, jnp.minimum(down_shard, chips - 1), done),
            number,
            chip_steps + step,
            win - CORES,
            seq,
        )
        sends_up = (up_shard >= 0) & (here < chips - 1)
        sends_down = (down_shard < chips) & (here > 0)
        gets_up = here >= step + 1
        gets_down = here + step + 1 < chips

        def start():
            guarded(sends_up, up.start)
            guarded(sends_down, down.start)

        def arrive():
            guarded(gets_up, up.wait_recv)
            guarded(gets_down, down.wait_recv)

        def finish():
            guarded(sends_up, up.wait_send)
            guarded(sends_down, down.wait_send)

        return start, arrive, finish

    def bit_stage(chunk, number, step, chip):
        half = chunk[2] // 2
        copies = []
        for part in range(2):
            order = list(range(bits)) if part == 0 else list(reversed(range(bits)))
            ref = region(chunk, chip, frozenset(order[:step]), part * half, half)
            kind = 2 * chip_steps + part * bits + step
            copies.append(copy(ref, number, kind, win, seq ^ (1 << order[step])))

        def start():
            for item in copies:
                item.start()

        def arrive():
            for item in copies:
                item.wait_recv()

        def finish():
            for item in copies:
                item.wait_send()

        return start, arrive, finish

    def core_stage(chunk, number):
        kind = 2 * chip_steps + 2 * bits
        item = copy(region(chunk, slice(None), every_bit), number, kind, win ^ 1, seq)
        return item.start, item.wait_recv, item.wait_send

    def stages(chunk, number):
        if chunk[3]:
            line = [chip_stage(chunk, number, step, frozenset()) for step in range(chip_steps)]
            cube = [bit_stage(chunk, number, step, slice(None)) for step in range(bits)]
            return line + cube + [core_stage(chunk, number)]
        cube = [bit_stage(chunk, number, step, here) for step in range(bits)]
        line = [chip_stage(chunk, number, step, every_bit) for step in range(chip_steps)]
        return cube + line + [core_stage(chunk, number)]

    own = [
        pltpu.make_async_copy(shard, out.at[(here, core) + own_bits], local_sem.at[which])
        for which, (shard, out) in enumerate(zip(shards, outs))
    ]
    return own, [stages(chunk, number) for number, chunk in enumerate(plan)]


def run_turn(work, spacing, turn, last=None):
    for number, stages in enumerate(work):
        at, off = divmod(turn - number, spacing)
        if off == 0 and 0 < at <= len(stages):
            stages[at - 1][1]()
            if at == len(stages) and last is not None:
                last(number)
        if off == 0 and 0 <= at < len(stages):
            stages[at][0]()


def turns_of(work, spacing):
    return len(work) + spacing * len(work[0])


def finish_sends(work):
    for stages in work:
        for stage in stages:
            stage[2]()


def gather_kernel(plan, count, spacing, *refs):
    shards, outs, sems = refs[:count], refs[count : 2 * count], refs[2 * count :]
    own, work = gather_work(plan, shards, outs, *sems)
    for item in own:
        item.start()
    start_together()
    for item in own:
        item.wait()
    for turn in range(turns_of(work, spacing)):
        run_turn(work, spacing, turn)
    finish_sends(work)


def gather_plan(shards, widths, lines_first):
    plan = []
    for which, (shard, width) in enumerate(zip(shards, widths)):
        for col in range(0, shard.shape[1], width):
            plan.append((which, col, width, lines_first(len(plan))))
    return tuple(plan)


def gather_sems(plan, count):
    chips = lax.axis_size("win") // CORES
    bits = lax.axis_size("seq").bit_length() - 1
    kinds = 2 * (chips - 1) + 2 * bits + 1
    return [
        pltpu.SemaphoreType.DMA((len(plan), kinds)),
        pltpu.SemaphoreType.DMA((len(plan), kinds)),
        pltpu.SemaphoreType.DMA((count,)),
    ]


def gathered_shapes(shards):
    chips = lax.axis_size("win") // CORES
    bits = lax.axis_size("seq").bit_length() - 1
    return [jax.ShapeDtypeStruct((chips, CORES) + (2,) * bits + s.shape, s.dtype) for s in shards]


def gather_all(shards, widths, lines_first, spacing, collective_id):
    plan = gather_plan(shards, widths, lines_first)
    return pl.pallas_call(
        functools.partial(gather_kernel, plan, len(shards), spacing),
        in_specs=[pl.BlockSpec(memory_space=pltpu.VMEM)] * len(shards),
        out_specs=[pl.BlockSpec(memory_space=pl.ANY)] * len(shards),
        out_shape=gathered_shapes(shards),
        scratch_shapes=gather_sems(plan, len(shards)),
        compiler_params=pltpu.CompilerParams(collective_id=collective_id, has_side_effects=True),
    )(*shards)


def exchange_work(parts, target, send_sem, recv_sem, local_sem):
    win, seq = lax.axis_index("win"), lax.axis_index("seq")
    items = []
    for peer, part in enumerate(parts):
        sent = pltpu.make_async_remote_copy(
            src_ref=part,
            dst_ref=target(seq),
            send_sem=send_sem.at[peer],
            recv_sem=recv_sem.at[seq],
            device_id=(win, peer),
            device_id_type=pl.DeviceIdType.MESH,
        )
        got = pltpu.make_async_remote_copy(
            src_ref=part,
            dst_ref=target(peer),
            send_sem=send_sem.at[peer],
            recv_sem=recv_sem.at[peer],
            device_id=(win, peer),
            device_id_type=pl.DeviceIdType.MESH,
        )
        own = pltpu.make_async_copy(part, target(peer), local_sem.at[peer])

        def start(peer=peer, sent=sent, own=own):
            pl.when(peer != seq)(sent.start)
            pl.when(peer == seq)(own.start)

        def arrive(peer=peer, got=got, own=own):
            pl.when(peer != seq)(got.wait_recv)
            pl.when(peer == seq)(own.wait)

        def finish(peer=peer, sent=sent):
            pl.when(peer != seq)(sent.wait_send)

        items.append((start, arrive, finish))
    return items


def gelu_parts(v):
    root = math.sqrt(2.0 / math.pi)
    t = jnp.tanh(root * (v + 0.044715 * (v * v * v)))
    cdf = 0.5 * (1.0 + t)
    slope = cdf + 0.5 * v * (1.0 - t * t) * (root * (1.0 + 3 * 0.044715 * (v * v)))
    return v * cdf, slope


def ffn_tasks(plan, gathered, received, ins, outs, scratch):
    source, cot, vectors, bias_in = ins
    attended, hidden_in, normed_two, activation, grad_pre, layer_out = outs
    slope, grad_act, rings, load_sem = scratch
    peers = received.shape[0]
    tokens, width = source.shape
    last = {chunk[0]: number for number, chunk in enumerate(plan)}
    first = {}
    for number, chunk in enumerate(plan):
        first.setdefault(chunk[0], number)

    def task(number, chunk):
        which, col, cols, _ = chunk
        ring = rings[which]
        held = ring.at[number % 2]
        columns = pl.ds(col, cols)
        lead = (slice(None),) * (len(ring.shape) - 2)
        load = pltpu.make_async_copy(
            gathered[which].at[lead + (columns,)], held, load_sem.at[number]
        )

        def weight():
            return held[...].reshape(math.prod(ring.shape[1:-1]), cols)

        def project():
            if number == first[which]:
                attended[...] = jnp.concatenate([received[peer] for peer in range(peers)], axis=1)
            branch = jnp.dot(attended[...], weight(), preferred_element_type=single)
            hidden_in[:, columns] = (
                source[:, columns].astype(single) + branch + vectors[0:1, columns]
            )
            if number == last[which]:
                normed = layer_norm(hidden_in[...], vectors[1:2, :], vectors[2:3, :])
                normed_two[...] = normed.astype(bfloat)

        def widen():
            pre = jnp.dot(normed_two[...], weight(), preferred_element_type=single)
            value, derivative = gelu_parts(pre + bias_in[0:1, columns])
            activation[:, columns] = value.astype(bfloat)
            slope[:, columns] = derivative

        def narrow():
            w = weight()
            out = jnp.dot(activation[...], w, preferred_element_type=single)
            out = hidden_in[:, columns] + out + vectors[3:4, columns]
            layer_out[:, columns] = out.astype(bfloat)
            back = lax.dot_general(
                cot[:, columns], w, (((1,), (1,)), ((), ())), preferred_element_type=single
            )
            if number != first[which]:
                back = grad_act[...] + back
            if number == last[which]:
                grad_pre[...] = (back * slope[...]).astype(bfloat)
            else:
                grad_act[...] = back

        return load, (project, widen, narrow)[which]

    return [task(number, chunk) for number, chunk in enumerate(plan)]


def attend_kernel(plan, count, spacing, first_turn, dims, *refs):
    hp, vd, bq, ffn = dims
    shards, (outgoing, tab_ref), refs = refs[:count], refs[count : count + 2], refs[count + 2 :]
    if ffn:
        ffn_ins, refs = refs[:4], refs[4:]
    outs, (x_ref, att_out), refs = refs[:count], refs[count : count + 2], refs[count + 2 :]
    if not ffn:
        received, refs = refs[0], refs[1:]
    else:
        ffn_outs, refs = refs[:6], refs[6:]
        (slope, grad_act, *rings, load_sem), refs = refs[: 3 + count], refs[3 + count :]
        received, refs = refs[0], refs[1:]
    att_ref, mixed_ref, *gather_refs = refs[:-7]
    in_send, in_recv, in_local, out_send, out_recv, out_local, att_sem = refs[-7:]
    length = x_ref.shape[0]
    peers, rows = outgoing.shape[0], outgoing.shape[1]
    own, work = gather_work(plan, shards, outs, *gather_refs)
    tasks = []
    if ffn:
        tasks = ffn_tasks(
            plan, outs, received, ffn_ins, ffn_outs, (slope, grad_act, rings, load_sem)
        )
    incoming = exchange_work(
        [outgoing.at[peer] for peer in range(peers)],
        lambda peer: x_ref.at[pl.ds(peer * rows, rows)],
        in_send,
        in_recv,
        in_local,
    )
    leaving = exchange_work(
        [mixed_ref.at[pl.ds(peer * rows, rows)] for peer in range(peers)],
        lambda peer: received.at[peer],
        out_send,
        out_recv,
        out_local,
    )
    for item in own:
        item.start()
    start_together(True)
    for item in own:
        item.wait()
    for start, _, _ in incoming:
        start()
    blocks = length // bq
    kept = [
        pltpu.make_async_copy(
            att_ref.at[block % 2], att_out.at[:, pl.ds(block * bq, bq)], att_sem.at[block]
        )
        for block in range(blocks)
    ]
    sent = loaded = done = 0
    arrived = set()
    for turn in range(turns_of(work, spacing)):
        run_turn(work, spacing, turn, arrived.add)
        block = turn - first_turn
        if block == 0:
            for _, arrive, _ in incoming:
                arrive()
        if 0 <= block < blocks:
            if block >= 2:
                kept[block - 2].wait()
            attend_block(length, bq, hp, vd, block, x_ref, tab_ref, att_ref.at[block % 2], mixed_ref)
            kept[block].start()
            while sent < peers and (sent + 1) * rows <= (block + 1) * bq:
                leaving[sent][0]()
                sent += 1
        if block >= blocks and done < loaded:
            if done == 0:
                for _, arrive, _ in leaving:
                    arrive()
            tasks[done][0].wait()
            tasks[done][1]()
            done += 1
        while loaded < len(tasks) and loaded in arrived and loaded < done + 2:
            tasks[loaded][0].start()
            loaded += 1
    if done == 0:
        for _, arrive, _ in leaving:
            arrive()
    while done < len(tasks):
        while loaded < len(tasks) and loaded < done + 2:
            tasks[loaded][0].start()
            loaded += 1
        tasks[done][0].wait()
        tasks[done][1]()
        done += 1
    for _, _, finish in incoming + leaving:
        finish()
    for item in kept[-2:]:
        item.wait()
    finish_sends(work)


def gather_and_attend(shards, widths, lines_first, spacing, first_turn, outgoing, tab, ffn_ins, dims):
    hp, vd, bq, ffn = dims
    peers, rows, cols = outgoing.shape
    length = peers * rows
    plan = gather_plan(shards, widths, lines_first)
    count = len(shards)
    anywhere = pl.BlockSpec(memory_space=pl.ANY)
    vmem = pl.BlockSpec(memory_space=pltpu.VMEM)
    dma = pltpu.SemaphoreType.DMA
    gathered = gathered_shapes(shards)
    extra_out, extra_scratch = [], []
    if ffn:
        width, hidden = ffn_ins[0].shape[1], ffn_ins[3].shape[1]
        extra_out = [
            jax.ShapeDtypeStruct((rows, width), bfloat),
            jax.ShapeDtypeStruct((rows, width), single),
            jax.ShapeDtypeStruct((rows, width), bfloat),
            jax.ShapeDtypeStruct((rows, hidden), bfloat),
            jax.ShapeDtypeStruct((rows, hidden), bfloat),
            jax.ShapeDtypeStruct((rows, width), bfloat),
        ]
        extra_scratch = [pltpu.VMEM((rows, hidden), single)] * 2
        for shape, cut in zip(gathered, widths):
            extra_scratch.append(pltpu.VMEM((2,) + shape.shape[:-1] + (cut,), bfloat))
        extra_scratch += [dma((len(plan),)), pltpu.VMEM((peers, rows, hp * vd), bfloat)]
    else:
        ffn_ins = ()
        extra_out = [jax.ShapeDtypeStruct((peers, rows, hp * vd), bfloat)]
    result = pl.pallas_call(
        functools.partial(attend_kernel, plan, count, spacing, first_turn, dims),
        in_specs=[vmem] * count + [anywhere, vmem] + [vmem] * len(ffn_ins),
        out_specs=[anywhere] * count + [vmem, anywhere] + [vmem if ffn else anywhere] * len(extra_out),
        out_shape=gathered
        + [
            jax.ShapeDtypeStruct((length, cols), bfloat),
            jax.ShapeDtypeStruct((hp, length, length), bfloat),
        ]
        + extra_out,
        scratch_shapes=extra_scratch
        + [
            pltpu.VMEM((2, hp, bq, length), bfloat),
            pltpu.VMEM((length, hp * vd), bfloat),
        ]
        + gather_sems(plan, count)
        + [dma((peers,))] * 6
        + [dma((length // bq,))],
        compiler_params=pltpu.CompilerParams(
            collective_id=1, has_side_effects=True, vmem_limit_bytes=VMEM_LIMIT
        ),
    )(*shards, outgoing, tab, *ffn_ins)
    return result[: count + 2], result[count + 2 :]


def scatter_work(plan, arrays, spacing, refs):
    count = len(arrays)
    sources, outs, rest = refs
    win, seq, here, core, chips, bits = partners()
    chip_steps = chips - 1
    ring, kept, rest = rest[:count], rest[count : 2 * count], rest[2 * count :]
    from_bits, rest = rest[: count * bits], rest[count * bits :]
    from_chips, rest = rest[:count], rest[count:]
    send_sem, recv_sem, local_sem = rest
    own_seq = {bit: (seq >> bit) & 1 for bit in range(bits)}

    def add(target, source):
        target[...] = (target[...].astype(single) + source[...].astype(single)).astype(bfloat)

    def slabs(chunk, chip, bit_index, lead=0, span=None):
        which, slot, _ = chunk
        index = tuple(bit_index.get(bit, slice(None)) for bit in reversed(range(bits)))
        width = arrays[which][1]
        columns = pl.ds(lead, width if span is None else span)
        return kept[which].at[(slot, chip) + index + (slice(None), columns)]

    def copy(src, dst, number, kind, to_win, to_seq):
        return pltpu.make_async_remote_copy(
            src_ref=src,
            dst_ref=dst,
            send_sem=send_sem.at[number, kind],
            recv_sem=recv_sem.at[number, kind],
            device_id=(to_win, to_seq),
            device_id_type=pl.DeviceIdType.MESH,
        )

    def core_stage(chunk, number):
        which, slot, _ = chunk
        width = arrays[which][1]
        product = isinstance(sources[which], tuple)
        held = ring[which].at[slot % spacing]
        columns = (slice(None),) * bits + (slice(None), pl.ds(slot * width, width))
        if product:
            leaving, own = held.at[:, 1 - core], held.at[:, core]
        else:
            leaving, own = sources[which].at[(slice(None), 1 - core) + columns], held
        kind = 2 * chip_steps + 2 * bits
        item = copy(leaving, kept[which].at[slot], number, kind, win ^ 1, seq)
        if not product:
            placed = pltpu.make_async_copy(
                sources[which].at[(slice(None), core) + columns], held, local_sem.at[number]
            )

        def start():
            if product:
                left, right = sources[which]
                grad = lax.dot_general(
                    left[...],
                    right[:, pl.ds(slot * width, width)],
                    (((0,), (0,)), ((), ())),
                    preferred_element_type=single,
                )
                held[...] = grad.astype(bfloat).reshape(held.shape)
            else:
                placed.start()
            item.start()

        def arrive():
            if not product:
                placed.wait()
            item.wait_recv()
            add(kept[which].at[slot], own)
            item.wait_send()

        return start, arrive, lambda: None

    def bit_stage(chunk, number, step, chip):
        which, slot, _ = chunk
        half = arrays[which][1] // 2
        items = []
        for part in range(2):
            order = list(range(bits)) if part else list(reversed(range(bits)))
            bit = order[step]
            done = {b: own_seq[b] for b in order[:step]}
            kind = 2 * chip_steps + part * bits + step
            buffer = from_bits[which * bits + step]
            target = buffer.at[(slot, part) if isinstance(chip, slice) else (slot, part, 0)]
            leaving = slabs(chunk, chip, done | {bit: 1 - own_seq[bit]}, part * half, half)
            staying = slabs(chunk, chip, done | {bit: own_seq[bit]}, part * half, half)
            sent = copy(leaving, target, number, kind, win, seq ^ (1 << bit))
            items.append((sent, staying, target))

        def start():
            for sent, _, _ in items:
                sent.start()

        def arrive():
            for sent, staying, target in items:
                sent.wait_recv()
                add(staying, target)

        def finish():
            for sent, _, _ in items:
                sent.wait_send()

        return start, arrive, finish

    def chip_stage(chunk, number, step, bit_index):
        which, slot, lines_last = chunk
        part = (0,) * bits if lines_last else ()
        up_to, down_to = here + step, here - step
        up_slot = from_chips[which].at[(slot, step - 1) + part]
        down_slot = from_chips[which].at[(slot, chip_steps + step - 1) + part]
        up = copy(
            slabs(chunk, jnp.minimum(up_to, chips - 1), bit_index),
            up_slot,
            number,
            step - 1,
            win + CORES,
            seq,
        )
        down = copy(
            slabs(chunk, jnp.maximum(down_to, 0), bit_index),
            down_slot,
            number,
            chip_steps + step - 1,
            win - CORES,
            seq,
        )
        sends_up, sends_down = up_to < chips, down_to >= 0
        gets_up = (here >= 1) & (here - 1 + step < chips)
        gets_down = (here + 1 < chips) & (here + 1 - step >= 0)

        def start():
            pl.when(sends_up)(up.start)
            pl.when(sends_down)(down.start)

        def arrive():
            @pl.when(gets_up)
            def _():
                up.wait_recv()
                add(slabs(chunk, jnp.minimum(here + step - 1, chips - 1), bit_index), up_slot)

            @pl.when(gets_down)
            def _():
                down.wait_recv()
                add(slabs(chunk, jnp.maximum(here - step + 1, 0), bit_index), down_slot)

        def finish():
            pl.when(sends_up)(up.wait_send)
            pl.when(sends_down)(down.wait_send)

        return start, arrive, finish

    def stages(chunk, number):
        steps = range(chip_steps, 0, -1)
        if chunk[2]:
            cube = [bit_stage(chunk, number, step, slice(None)) for step in range(bits)]
            line = [chip_stage(chunk, number, step, own_seq) for step in steps]
            return [core_stage(chunk, number)] + cube + line
        line = [chip_stage(chunk, number, step, {}) for step in steps]
        cube = [bit_stage(chunk, number, step, here) for step in range(bits)]
        return [core_stage(chunk, number)] + line + cube

    def last(number):
        chunk = plan[number]
        which, slot, _ = chunk
        width = arrays[which][1]
        total = slabs(chunk, here, own_seq)[...].astype(single)
        outs[which][:, pl.ds(slot * width, width)] = total

    return [stages(chunk, number) for number, chunk in enumerate(plan)], last


def scatter_plan(grads, widths, lines_last):
    devices = lax.axis_size("win") * lax.axis_size("seq")
    plan, arrays = [], []
    for which, (grad, width) in enumerate(zip(grads, widths)):
        if isinstance(grad, tuple):
            rows, cols = grad[0].shape[1] // devices, grad[1].shape[1]
        else:
            rows, cols = grad.shape[-2:]
        slots = cols // width
        lasts = [lines_last(len(plan) + slot) for slot in range(slots)]
        plan += [(which, slot, last) for slot, last in enumerate(lasts)]
        arrays.append((rows, width, slots, isinstance(grad, tuple)))
    return tuple(plan), tuple(arrays)


def scatter_scratch(plan, arrays, spacing):
    chips = lax.axis_size("win") // CORES
    bits = lax.axis_size("seq").bit_length() - 1
    cube = (2,) * bits
    ring, kept, from_bits, from_chips = [], [], [], []
    for which, (rows, width, slots, product) in enumerate(arrays):
        halves = (CORES,) if product else ()
        ring.append(pltpu.VMEM((spacing, chips) + halves + cube + (rows, width), bfloat))
        kept.append(pltpu.VMEM((slots, chips) + cube + (rows, width), bfloat))
        for step in range(bits):
            left = (2,) * (bits - 1 - step)
            from_bits.append(pltpu.VMEM((slots, 2, chips) + left + (rows, width // 2), bfloat))
        lone = (1,) * bits if all(c[2] for c in plan if c[0] == which) else cube
        from_chips.append(pltpu.VMEM((slots, 2 * (chips - 1)) + lone + (rows, width), bfloat))
    kinds = 2 * (chips - 1) + 2 * bits + 1
    dma = pltpu.SemaphoreType.DMA
    sems = [dma((len(plan), kinds)), dma((len(plan), kinds)), dma((len(plan),))]
    return ring + kept + from_bits + from_chips + sems


def flat_sources(grads):
    flat, specs = [], []
    for grad in grads:
        whole = isinstance(grad, tuple)
        flat += grad if whole else (grad,)
        specs += [pl.BlockSpec(memory_space=pltpu.VMEM if whole else pl.ANY)] * (2 if whole else 1)
    return flat, specs


def group_sources(arrays, refs):
    sources = []
    for _, _, _, product in arrays:
        sources.append((refs[0], refs[1]) if product else refs[0])
        refs = refs[2 if product else 1 :]
    return sources, refs


def scatter_kernel(plan, arrays, spacing, *refs):
    count = len(arrays)
    sources, refs = group_sources(arrays, refs)
    start_together()
    work, last = scatter_work(plan, arrays, spacing, (sources, refs[:count], refs[count:]))
    for turn in range(turns_of(work, spacing)):
        run_turn(work, spacing, turn, last)
    finish_sends(work)


def scatter_all(grads, widths, lines_last, spacing, collective_id):
    plan, arrays = scatter_plan(grads, widths, lines_last)
    flat, specs = flat_sources(grads)
    return pl.pallas_call(
        functools.partial(scatter_kernel, plan, arrays, spacing),
        in_specs=specs,
        out_specs=[pl.BlockSpec(memory_space=pltpu.VMEM)] * len(grads),
        out_shape=[jax.ShapeDtypeStruct((a[0], a[1] * a[2]), single) for a in arrays],
        scratch_shapes=scatter_scratch(plan, arrays, spacing),
        compiler_params=pltpu.CompilerParams(
            collective_id=collective_id, has_side_effects=True, vmem_limit_bytes=VMEM_LIMIT
        ),
    )(*flat)


def attend_back_kernel(plan, arrays, spacing, block_turns, dims, *refs):
    hp, vd, bq = dims
    count = len(arrays)
    sources, refs = group_sources(arrays, refs)
    (leaving_ref, x_ref, tab_ref, att_in), refs = refs[:4], refs[4:]
    outs, (returned, dtab_ref, bias_ref), refs = refs[:count], refs[count : count + 3], refs[count + 3 :]
    gm_ref, ret_ref, att_ref, dk_ref, dv_ref, *scatter_refs = refs[:-7]
    in_send, in_recv, in_local, out_send, out_recv, out_local, att_sem = refs[-7:]
    length = x_ref.shape[0]
    hk = hp * KD
    peers, rows = leaving_ref.shape[:2]
    blocks = length // bq
    incoming = exchange_work(
        [leaving_ref.at[peer] for peer in range(peers)],
        lambda peer: gm_ref.at[pl.ds(peer * rows, rows)],
        in_send,
        in_recv,
        in_local,
    )
    leaving = exchange_work(
        [ret_ref.at[pl.ds(peer * rows, rows)] for peer in range(peers)],
        lambda peer: returned.at[peer],
        out_send,
        out_recv,
        out_local,
    )
    loads = [
        pltpu.make_async_copy(
            att_in.at[:, pl.ds(block * bq, bq)], att_ref.at[block % 2], att_sem.at[block]
        )
        for block in range(blocks)
    ]
    for load in loads[:2]:
        load.start()
    start_together(True)
    for start, _, _ in incoming:
        start()
    work, last = scatter_work(plan, arrays, spacing, (sources, outs, scatter_refs))
    dk_ref[...] = jnp.zeros_like(dk_ref)
    dv_ref[...] = jnp.zeros_like(dv_ref)
    dtab_ref[...] = jnp.zeros_like(dtab_ref)
    bias_ref[...] = jnp.zeros_like(bias_ref)
    for turn in range(turns_of(work, spacing)):
        run_turn(work, spacing, turn, last)
        for block in range(blocks):
            if block_turns[block] != turn:
                continue
            if block == 0:
                for _, arrive, _ in incoming:
                    arrive()
            loads[block].wait()
            attend_back(
                length,
                bq,
                hp,
                vd,
                block,
                x_ref,
                tab_ref,
                att_ref.at[block % 2],
                gm_ref,
                ret_ref,
                (dk_ref, dv_ref, dtab_ref, bias_ref),
            )
            if block + 2 < blocks:
                loads[block + 2].start()
            if block == blocks - 1:
                ret_ref[:, hk : 2 * hk] = dk_ref[...].T.astype(bfloat)
                ret_ref[:, 2 * hk :] = dv_ref[...].T.astype(bfloat)
                for start, _, _ in leaving:
                    start()
    for _, arrive, _ in leaving:
        arrive()
    for _, _, finish in incoming + leaving:
        finish()
    finish_sends(work)


def scatter_and_attend_back(
    grads, widths, lines_last, spacing, block_turns, leaving, x, tab, attention, dims
):
    hp, vd, bq = dims
    peers, rows, _ = leaving.shape
    length = peers * rows
    hk = hp * KD
    back = 2 * hk + hp * vd
    plan, arrays = scatter_plan(grads, widths, lines_last)
    flat, specs = flat_sources(grads)
    anywhere = pl.BlockSpec(memory_space=pl.ANY)
    vmem = pl.BlockSpec(memory_space=pltpu.VMEM)
    dma = pltpu.SemaphoreType.DMA
    return pl.pallas_call(
        functools.partial(attend_back_kernel, plan, arrays, spacing, block_turns, dims),
        in_specs=specs + [anywhere, vmem, vmem, anywhere],
        out_specs=[vmem] * len(grads) + [anywhere, vmem, vmem],
        out_shape=[jax.ShapeDtypeStruct((a[0], a[1] * a[2]), single) for a in arrays]
        + [
            jax.ShapeDtypeStruct((peers, rows, back), bfloat),
            jax.ShapeDtypeStruct(tab.shape, single),
            jax.ShapeDtypeStruct((8, hk), single),
        ],
        scratch_shapes=[
            pltpu.VMEM((length, hp * vd), bfloat),
            pltpu.VMEM((length, back), bfloat),
            pltpu.VMEM((2, hp, bq, length), bfloat),
            pltpu.VMEM((hk, length), single),
            pltpu.VMEM((hp * vd, length), single),
        ]
        + scatter_scratch(plan, arrays, spacing)
        + [dma((peers,))] * 6
        + [dma((length // bq,))],
        compiler_params=pltpu.CompilerParams(
            collective_id=2, has_side_effects=True, vmem_limit_bytes=VMEM_LIMIT
        ),
    )(*flat, leaving, x, tab, attention)


def shards(
    inputs,
    cotangent,
    ln1_scale,
    ln1_offset,
    w_query,
    w_key,
    w_value,
    w_rel,
    content_bias,
    position_bias,
    w_out,
    b_out,
    ln2_scale,
    ln2_offset,
    w_in,
    b_in,
    w_mlp_out,
    b_mlp_out,
):
    win_size, seq_size = lax.axis_size("win"), lax.axis_size("seq")
    devices = win_size * seq_size
    seq = lax.axis_index("seq")
    window_count, row_count, width = inputs.shape
    tokens = window_count * row_count
    hk = HEADS * KD
    vd = width // HEADS
    hp = HEADS // seq_size
    hidden = w_in.shape[1]
    scale_factor = KD ** (-0.5)

    wide = (ln1_scale, ln1_offset, b_out, ln2_scale, ln2_offset, b_mlp_out)
    narrow = (content_bias, position_bias)
    packed = jnp.concatenate(wide + (b_in,) + narrow + (w_rel.T.reshape(-1),))
    cuts = [len(wide) * ln1_scale.shape[0]]
    cuts.append(cuts[0] + b_in.shape[0])
    cuts.append(cuts[1] + len(narrow) * content_bias.shape[0])
    packed_size = packed.shape[0]
    small_cols = -(-packed_size // 4096) * 256
    small_size = 16 * small_cols
    packed = jnp.pad(packed, (0, small_size - packed_size)).reshape(16, small_cols)
    packed, whole_qk, whole_v = gather_all(
        (packed, jnp.concatenate([w_query, w_key], axis=1), w_value),
        (256, 512, 512),
        lambda number: number % 3 != 2,
        3,
        0,
    )
    packed = packed.reshape(devices, small_size)
    whole_qk = whole_qk.reshape(width, 2 * hk)
    whole_v = whole_v.reshape(width, width)

    def rows_of(columns, count):
        rows = columns.reshape(devices, count, -1).transpose(1, 0, 2)
        return rows.reshape(count, -1).astype(single)

    wide_rows = rows_of(packed[:, : cuts[0]], len(wide))
    ln1_gain, ln1_shift, bias_out, ln2_gain, ln2_shift, bias_mlp = wide_rows
    bias_in = packed[:, cuts[0] : cuts[1]].reshape(-1).astype(single)
    bias_content, bias_position = rows_of(packed[:, cuts[1] : cuts[2]], len(narrow))
    whole_rel = packed[:, cuts[2] : packed_size].reshape(hk, F)

    features = jnp.pad(rel_features(WLEN, F).astype(bfloat), ((0, 1), (0, 0)))
    own_rel = lax.dynamic_slice_in_dim(whole_rel, seq * hp * KD, hp * KD, 0)
    table = jnp.einsum("cf,tf->ct", own_rel, features, preferred_element_type=single).astype(bfloat)

    source = inputs.reshape(tokens, width).astype(single)
    normed_one_f, norm_one_back = jax.vjp(layer_norm, source, ln1_gain, ln1_shift)
    normed_one = normed_one_f.astype(bfloat)
    proj_qk = jnp.dot(normed_one, whole_qk, preferred_element_type=single)
    query = proj_qk[:, :hk] * scale_factor
    proj_v = jnp.dot(normed_one, whole_v, preferred_element_type=single)
    parts = (
        (query + bias_content).astype(bfloat),
        (query + bias_position).astype(bfloat),
        proj_qk[:, hk:].astype(bfloat),
        proj_v.astype(bfloat),
    )
    outgoing = jnp.concatenate([part.reshape(tokens, seq_size, -1) for part in parts], axis=2)
    outgoing = jnp.transpose(outgoing, (1, 0, 2))
    in_kernel = w_out.shape[0] % 16 == 0 and hp * vd % 128 == 0
    row_vectors = wide_rows[2:]
    cot_rows = cotangent.reshape(tokens, width)
    first_results, ffn_results = gather_and_attend(
        (w_out, w_in, w_mlp_out),
        (512, 512, 256),
        lambda number: number % 3 != 1,
        3,
        FIRST_BLOCK_TURN,
        outgoing,
        table,
        (inputs.reshape(tokens, width), cot_rows, row_vectors, bias_in[None, :]),
        (hp, vd, BLOCK_Q, in_kernel),
    )
    whole_out, whole_in, whole_mlp, heads_in, attention = first_results
    whole_out = whole_out.reshape(width, width)
    whole_in = whole_in.reshape(width, hidden)
    whole_mlp = whole_mlp.reshape(hidden, width)
    if in_kernel:
        attended, hidden_in, normed_two, activation, grad_pre, result = ffn_results
    else:
        attended = jnp.transpose(ffn_results[0], (1, 0, 2)).reshape(tokens, width)
        branch = jnp.dot(attended, whole_out, preferred_element_type=single)
        hidden_in = source + branch + bias_out
        normed_two = layer_norm(hidden_in, ln2_gain, ln2_shift).astype(bfloat)
        pre_act = jnp.dot(normed_two, whole_in, preferred_element_type=single) + bias_in
        gelu_out, gelu_back = jax.vjp(jax.nn.gelu, pre_act)
        activation = gelu_out.astype(bfloat)
        result = hidden_in + jnp.dot(activation, whole_mlp, preferred_element_type=single)
        result = (result + bias_mlp).astype(bfloat)
        grad_act = jnp.einsum("td,fd->tf", cot_rows, whole_mlp, preferred_element_type=single)
        grad_pre = gelu_back(grad_act)[0].astype(bfloat)
    layer_out = result.reshape(inputs.shape)

    grid = (win_size // CORES, CORES) + (2,) * (seq_size.bit_length() - 1)

    def weight_grad(left, right):
        if left.shape[1] // devices % 16 == 0:
            return left, right
        grad = jnp.einsum("td,te->de", left, right, preferred_element_type=single).astype(bfloat)
        rows, cols = grad.shape
        return grad.reshape(grid + (rows // devices, cols))

    grad_mlp = weight_grad(activation, cot_rows)
    grad_bias_mlp = jnp.sum(cot_rows.astype(single), axis=0)
    grad_in = weight_grad(normed_two, grad_pre)
    grad_bias_in = jnp.sum(grad_pre.astype(single), axis=0)
    grad_normed_two = jnp.einsum("tf,df->td", grad_pre, whole_in, preferred_element_type=single)
    _, norm_two_back = jax.vjp(layer_norm, hidden_in, ln2_gain, ln2_shift)
    hidden_term, grad_ln2_gain, grad_ln2_shift = norm_two_back(grad_normed_two)
    grad_hidden = cot_rows.astype(single) + hidden_term
    grad_branch = grad_hidden.astype(bfloat)
    grad_out = weight_grad(attended, grad_branch)
    grad_bias_out = jnp.sum(grad_branch.astype(single), axis=0)
    grad_mixed = jnp.einsum(
        "te,de->td", grad_branch, whole_out, preferred_element_type=single
    ).astype(bfloat)
    grad_mixed = jnp.transpose(grad_mixed.reshape(tokens, seq_size, hp * vd), (1, 0, 2))
    grad_mlp, grad_in, returned, grad_table, grad_bias = scatter_and_attend_back(
        (grad_mlp, grad_in),
        (256, 512),
        lambda number: number % 4 != 0,
        2,
        BLOCK_TURNS,
        grad_mixed,
        heads_in,
        table,
        attention,
        (hp, vd, BLOCK_Q),
    )
    own = hp * KD
    returned = jnp.transpose(returned, (1, 0, 2))
    grad_qk_rows = jnp.concatenate(
        [
            returned[:, :, :own].reshape(tokens, hk),
            returned[:, :, own : 2 * own].reshape(tokens, hk),
        ],
        axis=1,
    )
    grad_v_rows = returned[:, :, 2 * own :].reshape(tokens, width)
    grad_qk = weight_grad(normed_one, grad_qk_rows)
    grad_v = weight_grad(normed_one, grad_v_rows)
    grad_normed_one = jnp.einsum(
        "tk,dk->td", grad_qk_rows, whole_qk, preferred_element_type=single
    ) + jnp.einsum("tk,dk->td", grad_v_rows, whole_v, preferred_element_type=single)
    source_term, grad_ln1_gain, grad_ln1_shift = norm_one_back(grad_normed_one)
    grad_inputs = (grad_hidden + source_term).reshape(inputs.shape)

    grad_rel = jnp.dot(grad_table, features.astype(single), precision=lax.Precision.HIGHEST)
    whole_grad_rel = lax.dynamic_update_slice_in_dim(
        jnp.zeros((hk, F), single), grad_rel, seq * own, 0
    )

    wide_grads = jnp.stack(
        [
            grad_ln1_gain,
            grad_ln1_shift,
            grad_bias_out,
            grad_ln2_gain,
            grad_ln2_shift,
            grad_bias_mlp,
        ]
    )
    narrow_grads = lax.dynamic_update_slice_in_dim(
        jnp.zeros((len(narrow), hk), single), grad_bias[: len(narrow)], seq * own, 1
    )

    def by_owner(rows):
        count = rows.shape[0]
        return rows.reshape(count, devices, -1).transpose(1, 0, 2).reshape(devices, -1)

    small = jnp.concatenate(
        [
            by_owner(wide_grads),
            grad_bias_in.reshape(devices, -1),
            by_owner(narrow_grads),
            whole_grad_rel.reshape(devices, -1),
        ],
        axis=1,
    )
    small = jnp.pad(small, ((0, 0), (0, small_size - packed_size))).astype(bfloat)
    grad_out, grad_qk, grad_v, small = scatter_all(
        (grad_out, grad_qk, grad_v, small.reshape(grid + (16, small_cols))),
        (512, 512, 512, 256),
        lambda number: number % 4 != 0,
        2,
        3,
    )
    small = small.reshape(-1)[:packed_size]
    wide_own = small[: cuts[0]].reshape(len(wide), -1)
    narrow_own = small[cuts[1] : cuts[2]].reshape(len(narrow), -1)
    own_grad_rel = small[cuts[2] :].reshape(-1, F).T
    return (
        layer_out,
        grad_inputs,
        wide_own[0],
        wide_own[1],
        grad_qk[:, :hk],
        grad_qk[:, hk:],
        grad_v,
        own_grad_rel,
        narrow_own[0],
        narrow_own[1],
        grad_out,
        wide_own[2],
        wide_own[3],
        wide_own[4],
        grad_in,
        small[cuts[0] : cuts[1]],
        grad_mlp,
        wide_own[5],
    )


def solution(mesh):
    in_specs = (
        P("win", "seq", None),
        P("win", "seq", None),
        P(("win", "seq")),
        P(("win", "seq")),
        P(("win", "seq"), None),
        P(("win", "seq"), None),
        P(("win", "seq"), None),
        P(None, ("win", "seq")),
        P(("win", "seq")),
        P(("win", "seq")),
        P(("win", "seq"), None),
        P(("win", "seq")),
        P(("win", "seq")),
        P(("win", "seq")),
        P(("win", "seq"), None),
        P(("win", "seq")),
        P(("win", "seq"), None),
        P(("win", "seq")),
    )
    out_specs = (
        P("win", "seq", None),
        P("win", "seq", None),
        P(("win", "seq")),
        P(("win", "seq")),
        P(("win", "seq"), None),
        P(("win", "seq"), None),
        P(("win", "seq"), None),
        P(None, ("win", "seq")),
        P(("win", "seq")),
        P(("win", "seq")),
        P(("win", "seq"), None),
        P(("win", "seq")),
        P(("win", "seq")),
        P(("win", "seq")),
        P(("win", "seq"), None),
        P(("win", "seq")),
        P(("win", "seq"), None),
        P(("win", "seq")),
    )
    return jax.shard_map(shards, mesh=mesh, in_specs=in_specs, out_specs=out_specs, check_vma=False)
```

```python
import functools
import math

import jax
import jax.numpy as jnp
from jax import lax
from jax.experimental import pallas as pl
from jax.experimental.pallas import tpu as pltpu
from jax.sharding import PartitionSpec as P

HEADS = 8
KD = 64
F = 192
WLEN = 1536
CORES = 2
BLOCK_Q = 256
FIRST_BLOCK_TURN = 8
BLOCK_TURNS = (6, 8, 10, 12, 14, 16)
VMEM_LIMIT = 62 * 2**20
bfloat = jnp.bfloat16
single = jnp.float32


def rel_features(length, feature_count):
    per_basis = feature_count // 6
    offsets = jnp.arange(-length + 1, length).astype(jnp.float32)
    magnitude = jnp.abs(offsets)[:, None]
    half_life = 2.0 ** jnp.linspace(3.0, math.log2(length), per_basis)
    decaying = jnp.exp(-math.log(2.0) / half_life * magnitude)
    widths = 2.0 ** jnp.arange(1, per_basis + 1).astype(jnp.float32) - 1.0
    central = (widths > magnitude).astype(jnp.float32)
    stddev = length / (2.0 * per_basis)
    centers = jnp.linspace(length / per_basis, float(length), per_basis)
    shape_param = (centers / stddev) ** 2
    inverse_scale = centers / stddev**2
    peak_at = (shape_param - 1.0) / inverse_scale
    log_prob = (shape_param - 1.0) * (
        jnp.log(jnp.maximum(magnitude, 0.5)) - jnp.log(peak_at)
    ) - inverse_scale * (magnitude - peak_at)
    density = jnp.exp(log_prob) + 1e-08
    gamma_pdf = density / jnp.max(density, axis=0, keepdims=True)
    basis_set = jnp.concatenate([decaying, central, gamma_pdf], axis=1)
    return jnp.concatenate([basis_set, jnp.sign(offsets)[:, None] * basis_set], axis=1)


def layer_norm(values, norm_gain, norm_shift):
    centered = values - jnp.mean(values, axis=-1, keepdims=True)
    variance = jnp.mean(centered * centered, axis=-1, keepdims=True)
    return centered * lax.rsqrt(variance + 1e-05) * norm_gain + norm_shift


def attend_block(length, bq, hp, vd, block, x_ref, tab_ref, att_ref, mixed_ref):
    hk = hp * KD
    first = block * bq
    rows = pl.ds(first, bq)
    span = length + bq
    outs = []
    for h in range(hp):
        qc = x_ref[rows, pl.ds(h * KD, KD)]
        qp = x_ref[rows, pl.ds(hk + h * KD, KD)]
        k = x_ref[:, pl.ds(2 * hk + h * KD, KD)]
        v = x_ref[:, pl.ds(3 * hk + h * vd, vd)]
        table = tab_ref[pl.ds(h * KD, KD), pl.ds(length - bq - first, span)]
        raw = jnp.dot(qp, table, preferred_element_type=single)
        rel = pltpu.roll(raw, span - bq + 1, 1, stride=1, stride_axis=0)[:, :length]
        s = rel + lax.dot_general(qc, k, (((1,), (1,)), ((), ())), preferred_element_type=single)
        e = jnp.exp(s - jnp.max(s, axis=-1, keepdims=True))
        inverse = 1.0 / jnp.sum(e, axis=-1, keepdims=True)
        att = (e * inverse).astype(bfloat)
        att_ref[h] = att
        outs.append(jnp.dot(att, v, preferred_element_type=single).astype(bfloat))
    mixed_ref[rows, :] = jnp.concatenate(outs, axis=1) if hp > 1 else outs[0]


def attend_back(length, bq, hp, vd, block, x_ref, tab_ref, att_ref, gm_ref, ret_ref, sums):
    dk_ref, dv_ref, dtab_ref, bias_ref = sums
    hk = hp * KD
    first = block * bq
    rows = pl.ds(first, bq)
    span = length + bq
    row = lax.broadcasted_iota(jnp.int32, (bq, bq), 0)
    col = lax.broadcasted_iota(jnp.int32, (bq, bq), 1)
    flip = jnp.where(row + col == bq - 1, 1.0, 0.0).astype(bfloat)

    def flipped(v):
        return jnp.dot(flip, v, preferred_element_type=single)

    def dot(left, right, left_dim, right_dim):
        return lax.dot_general(
            left, right, (((left_dim,), (right_dim,)), ((), ())), preferred_element_type=single
        )

    dqs, bc, bp = [], [], []
    for h in range(hp):
        own = pl.ds(h * KD, KD)
        table_cols = pl.ds(length - bq - first, span)
        qc = flipped(x_ref[rows, own]).astype(bfloat)
        qp = flipped(x_ref[rows, pl.ds(hk + h * KD, KD)]).astype(bfloat)
        k = x_ref[:, pl.ds(2 * hk + h * KD, KD)]
        v = x_ref[:, pl.ds(3 * hk + h * vd, vd)]
        gm = gm_ref[rows, pl.ds(h * vd, vd)]
        att = att_ref[h]
        dv_ref[pl.ds(h * vd, vd), :] += dot(gm, att, 0, 0)
        dp = dot(flipped(gm).astype(bfloat), v, 1, 1)
        af = flipped(att)
        t = af * dp
        delta = jnp.sum(t, axis=-1, keepdims=True)
        ds = (t - af * delta).astype(bfloat)
        dk_ref[own, :] += dot(qc, ds, 0, 0)
        gc = jnp.dot(ds, k, preferred_element_type=single)
        wide = jnp.concatenate([ds.astype(single), jnp.zeros((bq, bq), single)], axis=1)
        rel = pltpu.roll(wide, 0, 1, stride=1, stride_axis=0).astype(bfloat)
        gp = dot(rel, tab_ref[own, table_cols], 1, 1)
        dtab_ref[own, table_cols] += dot(qp, rel, 0, 0)
        dqs.append(flipped(((gc + gp) * KD**-0.5).astype(bfloat)).astype(bfloat))
        bc.append(jnp.sum(gc, axis=0, keepdims=True))
        bp.append(jnp.sum(gp, axis=0, keepdims=True))
    ret_ref[rows, :hk] = jnp.concatenate(dqs, axis=1) if hp > 1 else dqs[0]
    bias_ref[0:1, :] += jnp.concatenate(bc, axis=1) if hp > 1 else bc[0]
    bias_ref[1:2, :] += jnp.concatenate(bp, axis=1) if hp > 1 else bp[0]


def partners():
    win, seq = lax.axis_index("win"), lax.axis_index("seq")
    chips = lax.axis_size("win") // CORES
    bits = lax.axis_size("seq").bit_length() - 1
    return win, seq, win // CORES, win % CORES, chips, bits


def start_together(whole_seq=False):
    win, seq, here, core, chips, bits = partners()
    barrier = pltpu.get_barrier_semaphore()

    def greet(to_win, to_seq):
        pl.semaphore_signal(
            barrier, inc=1, device_id=(to_win, to_seq), device_id_type=pl.DeviceIdType.MESH
        )

    greet(win ^ 1, seq)
    across = range(1, 1 << bits) if whole_seq else [1 << bit for bit in range(bits)]
    for distance in across:
        greet(win, seq ^ distance)

    @pl.when(here > 0)
    def _():
        greet(win - CORES, seq)

    @pl.when(here < chips - 1)
    def _():
        greet(win + CORES, seq)

    ends = jnp.where(here > 0, 1, 0) + jnp.where(here < chips - 1, 1, 0)
    pl.semaphore_wait(barrier, 1 + len(across) + ends)


def gather_work(plan, shards, outs, send_sem, recv_sem, local_sem):
    win, seq, here, core, chips, bits = partners()
    own_bits = tuple((seq >> bit) & 1 for bit in reversed(range(bits)))
    own_seq = {bit: (seq >> bit) & 1 for bit in range(bits)}

    def region(chunk, chip, done, lead=0, span=None):
        which, col, cols, _ = chunk
        start, size = (col + lead, cols) if span is None else (col + lead, span)
        index = tuple(slice(None) if bit in done else own_seq[bit] for bit in reversed(range(bits)))
        return outs[which].at[(chip, core) + index + (slice(None), pl.ds(start, size))]

    def copy(ref, number, kind, to_win, to_seq):
        return pltpu.make_async_remote_copy(
            src_ref=ref,
            dst_ref=ref,
            send_sem=send_sem.at[number, kind],
            recv_sem=recv_sem.at[number, kind],
            device_id=(to_win, to_seq),
            device_id_type=pl.DeviceIdType.MESH,
        )

    chip_steps = chips - 1
    every_bit = frozenset(range(bits))

    def guarded(condition, action):
        pl.when(condition)(action)

    def chip_stage(chunk, number, step, done):
        up_shard, down_shard = here - step, here + step
        up = copy(region(chunk, jnp.maximum(up_shard, 0), done), number, step, win + CORES, seq)
        down = copy(
            region(chunk, jnp.minimum(down_shard, chips - 1), done),
            number,
            chip_steps + step,
            win - CORES,
            seq,
        )
        sends_up = (up_shard >= 0) & (here < chips - 1)
        sends_down = (down_shard < chips) & (here > 0)
        gets_up = here >= step + 1
        gets_down = here + step + 1 < chips

        def start():
            guarded(sends_up, up.start)
            guarded(sends_down, down.start)

        def arrive():
            guarded(gets_up, up.wait_recv)
            guarded(gets_down, down.wait_recv)

        def finish():
            guarded(sends_up, up.wait_send)
            guarded(sends_down, down.wait_send)

        return start, arrive, finish

    def bit_stage(chunk, number, step, chip):
        half = chunk[2] // 2
        copies = []
        for part in range(2):
            order = list(range(bits)) if part == 0 else list(reversed(range(bits)))
            ref = region(chunk, chip, frozenset(order[:step]), part * half, half)
            kind = 2 * chip_steps + part * bits + step
            copies.append(copy(ref, number, kind, win, seq ^ (1 << order[step])))

        def start():
            for item in copies:
                item.start()

        def arrive():
            for item in copies:
                item.wait_recv()

        def finish():
            for item in copies:
                item.wait_send()

        return start, arrive, finish

    def core_stage(chunk, number):
        kind = 2 * chip_steps + 2 * bits
        item = copy(region(chunk, slice(None), every_bit), number, kind, win ^ 1, seq)
        return item.start, item.wait_recv, item.wait_send

    def stages(chunk, number):
        if chunk[3]:
            line = [chip_stage(chunk, number, step, frozenset()) for step in range(chip_steps)]
            cube = [bit_stage(chunk, number, step, slice(None)) for step in range(bits)]
            return line + cube + [core_stage(chunk, number)]
        cube = [bit_stage(chunk, number, step, here) for step in range(bits)]
        line = [chip_stage(chunk, number, step, every_bit) for step in range(chip_steps)]
        return cube + line + [core_stage(chunk, number)]

    own = [
        pltpu.make_async_copy(shard, out.at[(here, core) + own_bits], local_sem.at[which])
        for which, (shard, out) in enumerate(zip(shards, outs))
    ]
    return own, [stages(chunk, number) for number, chunk in enumerate(plan)]


def run_turn(work, spacing, turn, last=None):
    for number, stages in enumerate(work):
        at, off = divmod(turn - number, spacing)
        if off == 0 and 0 < at <= len(stages):
            stages[at - 1][1]()
            if at == len(stages) and last is not None:
                last(number)
        if off == 0 and 0 <= at < len(stages):
            stages[at][0]()


def turns_of(work, spacing):
    return len(work) + spacing * len(work[0])


def finish_sends(work):
    for stages in work:
        for stage in stages:
            stage[2]()


def gather_kernel(plan, count, spacing, *refs):
    shards, outs, sems = refs[:count], refs[count : 2 * count], refs[2 * count :]
    own, work = gather_work(plan, shards, outs, *sems)
    for item in own:
        item.start()
    start_together()
    for item in own:
        item.wait()
    for turn in range(turns_of(work, spacing)):
        run_turn(work, spacing, turn)
    finish_sends(work)


def gather_plan(shards, widths, lines_first):
    plan = []
    for which, (shard, width) in enumerate(zip(shards, widths)):
        for col in range(0, shard.shape[1], width):
            plan.append((which, col, width, lines_first(len(plan))))
    return tuple(plan)


def gather_sems(plan, count):
    chips = lax.axis_size("win") // CORES
    bits = lax.axis_size("seq").bit_length() - 1
    kinds = 2 * (chips - 1) + 2 * bits + 1
    return [
        pltpu.SemaphoreType.DMA((len(plan), kinds)),
        pltpu.SemaphoreType.DMA((len(plan), kinds)),
        pltpu.SemaphoreType.DMA((count,)),
    ]


def gathered_shapes(shards):
    chips = lax.axis_size("win") // CORES
    bits = lax.axis_size("seq").bit_length() - 1
    return [jax.ShapeDtypeStruct((chips, CORES) + (2,) * bits + s.shape, s.dtype) for s in shards]


def gather_all(shards, widths, lines_first, spacing, collective_id):
    plan = gather_plan(shards, widths, lines_first)
    return pl.pallas_call(
        functools.partial(gather_kernel, plan, len(shards), spacing),
        in_specs=[pl.BlockSpec(memory_space=pltpu.VMEM)] * len(shards),
        out_specs=[pl.BlockSpec(memory_space=pl.ANY)] * len(shards),
        out_shape=gathered_shapes(shards),
        scratch_shapes=gather_sems(plan, len(shards)),
        compiler_params=pltpu.CompilerParams(collective_id=collective_id, has_side_effects=True),
    )(*shards)


def exchange_work(parts, target, send_sem, recv_sem, local_sem):
    win, seq = lax.axis_index("win"), lax.axis_index("seq")
    items = []
    for peer, part in enumerate(parts):
        sent = pltpu.make_async_remote_copy(
            src_ref=part,
            dst_ref=target(seq),
            send_sem=send_sem.at[peer],
            recv_sem=recv_sem.at[seq],
            device_id=(win, peer),
            device_id_type=pl.DeviceIdType.MESH,
        )
        got = pltpu.make_async_remote_copy(
            src_ref=part,
            dst_ref=target(peer),
            send_sem=send_sem.at[peer],
            recv_sem=recv_sem.at[peer],
            device_id=(win, peer),
            device_id_type=pl.DeviceIdType.MESH,
        )
        own = pltpu.make_async_copy(part, target(peer), local_sem.at[peer])

        def start(peer=peer, sent=sent, own=own):
            pl.when(peer != seq)(sent.start)
            pl.when(peer == seq)(own.start)

        def arrive(peer=peer, got=got, own=own):
            pl.when(peer != seq)(got.wait_recv)
            pl.when(peer == seq)(own.wait)

        def finish(peer=peer, sent=sent):
            pl.when(peer != seq)(sent.wait_send)

        items.append((start, arrive, finish))
    return items


def gelu_parts(v):
    root = math.sqrt(2.0 / math.pi)
    t = jnp.tanh(root * (v + 0.044715 * (v * v * v)))
    cdf = 0.5 * (1.0 + t)
    slope = cdf + 0.5 * v * (1.0 - t * t) * (root * (1.0 + 3 * 0.044715 * (v * v)))
    return v * cdf, slope


def ffn_tasks(plan, gathered, received, ins, outs, scratch):
    source, cot, vectors, bias_in = ins
    attended, hidden_in, normed_two, activation, grad_pre = outs
    grad_act, rings, load_sem = scratch
    peers = received.shape[0]
    last = {chunk[0]: number for number, chunk in enumerate(plan)}
    first = {}
    for number, chunk in enumerate(plan):
        first.setdefault(chunk[0], number)

    def task(number, chunk):
        which, col, cols, _ = chunk
        ring = rings[which]
        held = ring.at[number % 2]
        columns = pl.ds(col, cols)
        lead = (slice(None),) * (len(ring.shape) - 2)
        load = pltpu.make_async_copy(
            gathered[which].at[lead + (columns,)], held, load_sem.at[number]
        )

        def weight():
            return held[...].reshape(math.prod(ring.shape[1:-1]), cols)

        def project():
            if number == first[which]:
                attended[...] = jnp.concatenate([received[peer] for peer in range(peers)], axis=1)
            branch = jnp.dot(attended[...], weight(), preferred_element_type=single)
            hidden_in[:, columns] = (
                source[:, columns].astype(single) + branch + vectors[0:1, columns]
            )
            if number == last[which]:
                normed = layer_norm(hidden_in[...], vectors[1:2, :], vectors[2:3, :])
                normed_two[...] = normed.astype(bfloat)

        def fold():
            term = lax.dot_general(
                cot[:, columns], weight(), (((1,), (1,)), ((), ())), preferred_element_type=single
            )
            grad_act[...] = term if number == first[which] else grad_act[...] + term

        def widen():
            pre = jnp.dot(normed_two[...], weight(), preferred_element_type=single)
            value, derivative = gelu_parts(pre + bias_in[0:1, columns])
            activation[:, columns] = value.astype(bfloat)
            grad_pre[:, columns] = (grad_act[:, columns] * derivative).astype(bfloat)

        return load, (project, fold, widen)[which]

    return [task(number, chunk) for number, chunk in enumerate(plan)]


def attend_kernel(plan, count, spacing, first_turn, dims, *refs):
    hp, vd, bq, ffn = dims
    shards, (outgoing, tab_ref), refs = refs[:count], refs[count : count + 2], refs[count + 2 :]
    if ffn:
        ffn_ins, refs = refs[:4], refs[4:]
    outs, (x_ref, att_out), refs = refs[:count], refs[count : count + 2], refs[count + 2 :]
    if not ffn:
        received, refs = refs[0], refs[1:]
    else:
        ffn_outs, refs = refs[:5], refs[5:]
        (grad_act, *rings, load_sem), refs = refs[: 2 + count], refs[2 + count :]
        received, refs = refs[0], refs[1:]
    att_ref, mixed_ref, *gather_refs = refs[:-7]
    in_send, in_recv, in_local, out_send, out_recv, out_local, att_sem = refs[-7:]
    length = x_ref.shape[0]
    peers, rows = outgoing.shape[0], outgoing.shape[1]
    own, work = gather_work(plan, shards, outs, *gather_refs)
    tasks = []
    if ffn:
        tasks = ffn_tasks(plan, outs, received, ffn_ins, ffn_outs, (grad_act, rings, load_sem))
    incoming = exchange_work(
        [outgoing.at[peer] for peer in range(peers)],
        lambda peer: x_ref.at[pl.ds(peer * rows, rows)],
        in_send,
        in_recv,
        in_local,
    )
    leaving = exchange_work(
        [mixed_ref.at[pl.ds(peer * rows, rows)] for peer in range(peers)],
        lambda peer: received.at[peer],
        out_send,
        out_recv,
        out_local,
    )
    for item in own:
        item.start()
    start_together(True)
    for item in own:
        item.wait()
    for start, _, _ in incoming:
        start()
    blocks = length // bq
    kept = [
        pltpu.make_async_copy(
            att_ref.at[block % 2], att_out.at[:, pl.ds(block * bq, bq)], att_sem.at[block]
        )
        for block in range(blocks)
    ]
    sent = loaded = done = 0
    arrived = set()
    for turn in range(turns_of(work, spacing)):
        run_turn(work, spacing, turn, arrived.add)
        block = turn - first_turn
        if block == 0:
            for _, arrive, _ in incoming:
                arrive()
        if 0 <= block < blocks:
            if block >= 2:
                kept[block - 2].wait()
            attend_block(length, bq, hp, vd, block, x_ref, tab_ref, att_ref.at[block % 2], mixed_ref)
            kept[block].start()
            while sent < peers and (sent + 1) * rows <= (block + 1) * bq:
                leaving[sent][0]()
                sent += 1
        if block >= blocks and done < loaded:
            if done == 0:
                for _, arrive, _ in leaving:
                    arrive()
            tasks[done][0].wait()
            tasks[done][1]()
            done += 1
        while loaded < len(tasks) and loaded in arrived and loaded < done + 2:
            tasks[loaded][0].start()
            loaded += 1
    if done == 0:
        for _, arrive, _ in leaving:
            arrive()
    while done < len(tasks):
        while loaded < len(tasks) and loaded < done + 2:
            tasks[loaded][0].start()
            loaded += 1
        tasks[done][0].wait()
        tasks[done][1]()
        done += 1
    for _, _, finish in incoming + leaving:
        finish()
    for item in kept[-2:]:
        item.wait()
    finish_sends(work)


def gather_and_attend(shards, widths, lines_first, spacing, first_turn, outgoing, tab, ffn_ins, dims):
    hp, vd, bq, ffn = dims
    peers, rows, cols = outgoing.shape
    length = peers * rows
    plan = gather_plan(shards, widths, lines_first)
    count = len(shards)
    anywhere = pl.BlockSpec(memory_space=pl.ANY)
    vmem = pl.BlockSpec(memory_space=pltpu.VMEM)
    dma = pltpu.SemaphoreType.DMA
    gathered = gathered_shapes(shards)
    extra_out, extra_scratch = [], []
    if ffn:
        width, hidden = ffn_ins[0].shape[1], ffn_ins[3].shape[1]
        extra_out = [
            jax.ShapeDtypeStruct((rows, width), bfloat),
            jax.ShapeDtypeStruct((rows, width), single),
            jax.ShapeDtypeStruct((rows, width), bfloat),
            jax.ShapeDtypeStruct((rows, hidden), bfloat),
            jax.ShapeDtypeStruct((rows, hidden), bfloat),
        ]
        extra_scratch = [pltpu.VMEM((rows, hidden), single)]
        for shape, cut in zip(gathered, widths):
            extra_scratch.append(pltpu.VMEM((2,) + shape.shape[:-1] + (cut,), bfloat))
        extra_scratch += [dma((len(plan),)), pltpu.VMEM((peers, rows, hp * vd), bfloat)]
    else:
        ffn_ins = ()
        extra_out = [jax.ShapeDtypeStruct((peers, rows, hp * vd), bfloat)]
    result = pl.pallas_call(
        functools.partial(attend_kernel, plan, count, spacing, first_turn, dims),
        in_specs=[vmem] * count + [anywhere, vmem] + [vmem] * len(ffn_ins),
        out_specs=[anywhere] * count + [vmem, anywhere] + [vmem if ffn else anywhere] * len(extra_out),
        out_shape=gathered
        + [
            jax.ShapeDtypeStruct((length, cols), bfloat),
            jax.ShapeDtypeStruct((hp, length, length), bfloat),
        ]
        + extra_out,
        scratch_shapes=extra_scratch
        + [
            pltpu.VMEM((2, hp, bq, length), bfloat),
            pltpu.VMEM((length, hp * vd), bfloat),
        ]
        + gather_sems(plan, count)
        + [dma((peers,))] * 6
        + [dma((length // bq,))],
        compiler_params=pltpu.CompilerParams(
            collective_id=1, has_side_effects=True, vmem_limit_bytes=VMEM_LIMIT
        ),
    )(*shards, outgoing, tab, *ffn_ins)
    return result[: count + 2], result[count + 2 :]


def scatter_work(plan, arrays, spacing, refs):
    count = len(arrays)
    sources, outs, rest = refs
    win, seq, here, core, chips, bits = partners()
    chip_steps = chips - 1
    ring, kept, rest = rest[:count], rest[count : 2 * count], rest[2 * count :]
    from_bits, rest = rest[: count * bits], rest[count * bits :]
    from_chips, rest = rest[:count], rest[count:]
    send_sem, recv_sem, local_sem = rest
    own_seq = {bit: (seq >> bit) & 1 for bit in range(bits)}

    def add(target, source):
        target[...] = (target[...].astype(single) + source[...].astype(single)).astype(bfloat)

    def slabs(chunk, chip, bit_index, lead=0, span=None):
        which, slot, _ = chunk
        index = tuple(bit_index.get(bit, slice(None)) for bit in reversed(range(bits)))
        width = arrays[which][1]
        columns = pl.ds(lead, width if span is None else span)
        return kept[which].at[(slot, chip) + index + (slice(None), columns)]

    def copy(src, dst, number, kind, to_win, to_seq):
        return pltpu.make_async_remote_copy(
            src_ref=src,
            dst_ref=dst,
            send_sem=send_sem.at[number, kind],
            recv_sem=recv_sem.at[number, kind],
            device_id=(to_win, to_seq),
            device_id_type=pl.DeviceIdType.MESH,
        )

    def core_stage(chunk, number):
        which, slot, _ = chunk
        width = arrays[which][1]
        product = isinstance(sources[which], tuple)
        held = ring[which].at[slot % spacing]
        columns = (slice(None),) * bits + (slice(None), pl.ds(slot * width, width))
        if product:
            leaving, own = held.at[:, 1 - core], held.at[:, core]
        else:
            leaving, own = sources[which].at[(slice(None), 1 - core) + columns], held
        kind = 2 * chip_steps + 2 * bits
        item = copy(leaving, kept[which].at[slot], number, kind, win ^ 1, seq)
        if not product:
            placed = pltpu.make_async_copy(
                sources[which].at[(slice(None), core) + columns], held, local_sem.at[number]
            )

        def start():
            if product:
                left, right = sources[which]
                grad = lax.dot_general(
                    left[...],
                    right[:, pl.ds(slot * width, width)],
                    (((0,), (0,)), ((), ())),
                    preferred_element_type=single,
                )
                held[...] = grad.astype(bfloat).reshape(held.shape)
            else:
                placed.start()
            item.start()

        def arrive():
            if not product:
                placed.wait()
            item.wait_recv()
            add(kept[which].at[slot], own)
            item.wait_send()

        return start, arrive, lambda: None

    def bit_stage(chunk, number, step, chip):
        which, slot, _ = chunk
        half = arrays[which][1] // 2
        items = []
        for part in range(2):
            order = list(range(bits)) if part else list(reversed(range(bits)))
            bit = order[step]
            done = {b: own_seq[b] for b in order[:step]}
            kind = 2 * chip_steps + part * bits + step
            buffer = from_bits[which * bits + step]
            target = buffer.at[(slot, part) if isinstance(chip, slice) else (slot, part, 0)]
            leaving = slabs(chunk, chip, done | {bit: 1 - own_seq[bit]}, part * half, half)
            staying = slabs(chunk, chip, done | {bit: own_seq[bit]}, part * half, half)
            sent = copy(leaving, target, number, kind, win, seq ^ (1 << bit))
            items.append((sent, staying, target))

        def start():
            for sent, _, _ in items:
                sent.start()

        def arrive():
            for sent, staying, target in items:
                sent.wait_recv()
                add(staying, target)

        def finish():
            for sent, _, _ in items:
                sent.wait_send()

        return start, arrive, finish

    def chip_stage(chunk, number, step, bit_index):
        which, slot, lines_last = chunk
        part = (0,) * bits if lines_last else ()
        up_to, down_to = here + step, here - step
        up_slot = from_chips[which].at[(slot, step - 1) + part]
        down_slot = from_chips[which].at[(slot, chip_steps + step - 1) + part]
        up = copy(
            slabs(chunk, jnp.minimum(up_to, chips - 1), bit_index),
            up_slot,
            number,
            step - 1,
            win + CORES,
            seq,
        )
        down = copy(
            slabs(chunk, jnp.maximum(down_to, 0), bit_index),
            down_slot,
            number,
            chip_steps + step - 1,
            win - CORES,
            seq,
        )
        sends_up, sends_down = up_to < chips, down_to >= 0
        gets_up = (here >= 1) & (here - 1 + step < chips)
        gets_down = (here + 1 < chips) & (here + 1 - step >= 0)

        def start():
            pl.when(sends_up)(up.start)
            pl.when(sends_down)(down.start)

        def arrive():
            @pl.when(gets_up)
            def _():
                up.wait_recv()
                add(slabs(chunk, jnp.minimum(here + step - 1, chips - 1), bit_index), up_slot)

            @pl.when(gets_down)
            def _():
                down.wait_recv()
                add(slabs(chunk, jnp.maximum(here - step + 1, 0), bit_index), down_slot)

        def finish():
            pl.when(sends_up)(up.wait_send)
            pl.when(sends_down)(down.wait_send)

        return start, arrive, finish

    def stages(chunk, number):
        steps = range(chip_steps, 0, -1)
        if chunk[2]:
            cube = [bit_stage(chunk, number, step, slice(None)) for step in range(bits)]
            line = [chip_stage(chunk, number, step, own_seq) for step in steps]
            return [core_stage(chunk, number)] + cube + line
        line = [chip_stage(chunk, number, step, {}) for step in steps]
        cube = [bit_stage(chunk, number, step, here) for step in range(bits)]
        return [core_stage(chunk, number)] + line + cube

    def last(number):
        chunk = plan[number]
        which, slot, _ = chunk
        width = arrays[which][1]
        total = slabs(chunk, here, own_seq)[...].astype(single)
        outs[which][:, pl.ds(slot * width, width)] = total

    return [stages(chunk, number) for number, chunk in enumerate(plan)], last


def scatter_plan(grads, widths, lines_last):
    devices = lax.axis_size("win") * lax.axis_size("seq")
    plan, arrays = [], []
    for which, (grad, width) in enumerate(zip(grads, widths)):
        if isinstance(grad, tuple):
            rows, cols = grad[0].shape[1] // devices, grad[1].shape[1]
        else:
            rows, cols = grad.shape[-2:]
        slots = cols // width
        lasts = [lines_last(len(plan) + slot) for slot in range(slots)]
        plan += [(which, slot, last) for slot, last in enumerate(lasts)]
        arrays.append((rows, width, slots, isinstance(grad, tuple)))
    return tuple(plan), tuple(arrays)


def scatter_scratch(plan, arrays, spacing):
    chips = lax.axis_size("win") // CORES
    bits = lax.axis_size("seq").bit_length() - 1
    cube = (2,) * bits
    ring, kept, from_bits, from_chips = [], [], [], []
    for which, (rows, width, slots, product) in enumerate(arrays):
        halves = (CORES,) if product else ()
        ring.append(pltpu.VMEM((spacing, chips) + halves + cube + (rows, width), bfloat))
        kept.append(pltpu.VMEM((slots, chips) + cube + (rows, width), bfloat))
        for step in range(bits):
            left = (2,) * (bits - 1 - step)
            from_bits.append(pltpu.VMEM((slots, 2, chips) + left + (rows, width // 2), bfloat))
        lone = (1,) * bits if all(c[2] for c in plan if c[0] == which) else cube
        from_chips.append(pltpu.VMEM((slots, 2 * (chips - 1)) + lone + (rows, width), bfloat))
    kinds = 2 * (chips - 1) + 2 * bits + 1
    dma = pltpu.SemaphoreType.DMA
    sems = [dma((len(plan), kinds)), dma((len(plan), kinds)), dma((len(plan),))]
    return ring + kept + from_bits + from_chips + sems


def flat_sources(grads):
    flat, specs = [], []
    for grad in grads:
        whole = isinstance(grad, tuple)
        flat += grad if whole else (grad,)
        specs += [pl.BlockSpec(memory_space=pltpu.VMEM if whole else pl.ANY)] * (2 if whole else 1)
    return flat, specs


def group_sources(arrays, refs):
    sources = []
    for _, _, _, product in arrays:
        sources.append((refs[0], refs[1]) if product else refs[0])
        refs = refs[2 if product else 1 :]
    return sources, refs


def scatter_kernel(plan, arrays, spacing, *refs):
    count = len(arrays)
    sources, refs = group_sources(arrays, refs)
    start_together()
    work, last = scatter_work(plan, arrays, spacing, (sources, refs[:count], refs[count:]))
    for turn in range(turns_of(work, spacing)):
        run_turn(work, spacing, turn, last)
    finish_sends(work)


def scatter_all(grads, widths, lines_last, spacing, collective_id):
    plan, arrays = scatter_plan(grads, widths, lines_last)
    flat, specs = flat_sources(grads)
    return pl.pallas_call(
        functools.partial(scatter_kernel, plan, arrays, spacing),
        in_specs=specs,
        out_specs=[pl.BlockSpec(memory_space=pltpu.VMEM)] * len(grads),
        out_shape=[jax.ShapeDtypeStruct((a[0], a[1] * a[2]), single) for a in arrays],
        scratch_shapes=scatter_scratch(plan, arrays, spacing),
        compiler_params=pltpu.CompilerParams(
            collective_id=collective_id, has_side_effects=True, vmem_limit_bytes=VMEM_LIMIT
        ),
    )(*flat)


def scatter_and_widen_kernel(plan, arrays, spacing, first_turn, cols, *refs):
    count = len(arrays)
    sources, refs = group_sources(arrays, refs)
    (weights, activation, hidden_in, bias), refs = refs[:4], refs[4:]
    outs, layer_out, ring, load_sem, *refs = refs[:count], *refs[count:]
    pieces = layer_out.shape[1] // cols
    lead = (slice(None),) * (len(ring.shape) - 2)
    loads = [
        pltpu.make_async_copy(
            weights.at[lead + (pl.ds(piece * cols, cols),)], ring.at[piece % 2], load_sem.at[piece]
        )
        for piece in range(pieces)
    ]
    for load in loads[:2]:
        load.start()
    start_together()
    work, last = scatter_work(plan, arrays, spacing, (sources, outs, refs))
    for turn in range(turns_of(work, spacing)):
        run_turn(work, spacing, turn, last)
        piece = turn - first_turn
        if 0 <= piece < pieces:
            loads[piece].wait()
            columns = pl.ds(piece * cols, cols)
            w = ring[piece % 2].reshape(activation.shape[1], cols)
            out = jnp.dot(activation[...], w, preferred_element_type=single)
            out = hidden_in[:, columns] + out + bias[:, columns]
            layer_out[:, columns] = out.astype(bfloat)
            if piece + 2 < pieces:
                loads[piece + 2].start()
    finish_sends(work)


def scatter_and_widen(grads, widths, lines_last, spacing, first_turn, layer_ins, collective_id):
    weights, activation, hidden_in, _ = layer_ins
    cols = 256
    plan, arrays = scatter_plan(grads, widths, lines_last)
    flat, specs = flat_sources(grads)
    vmem = pl.BlockSpec(memory_space=pltpu.VMEM)
    return pl.pallas_call(
        functools.partial(scatter_and_widen_kernel, plan, arrays, spacing, first_turn, cols),
        in_specs=specs + [pl.BlockSpec(memory_space=pl.ANY), vmem, vmem, vmem],
        out_specs=[vmem] * (len(arrays) + 1),
        out_shape=[jax.ShapeDtypeStruct((a[0], a[1] * a[2]), single) for a in arrays]
        + [jax.ShapeDtypeStruct(hidden_in.shape, bfloat)],
        scratch_shapes=[
            pltpu.VMEM((2,) + weights.shape[:-1] + (cols,), bfloat),
            pltpu.SemaphoreType.DMA((hidden_in.shape[1] // cols,)),
        ]
        + scatter_scratch(plan, arrays, spacing),
        compiler_params=pltpu.CompilerParams(
            collective_id=collective_id, has_side_effects=True, vmem_limit_bytes=VMEM_LIMIT
        ),
    )(*flat, *layer_ins)


def attend_back_kernel(plan, arrays, spacing, block_turns, dims, *refs):
    hp, vd, bq = dims
    count = len(arrays)
    sources, refs = group_sources(arrays, refs)
    (leaving_ref, x_ref, tab_ref, att_in), refs = refs[:4], refs[4:]
    outs, (returned, dtab_ref, bias_ref), refs = refs[:count], refs[count : count + 3], refs[count + 3 :]
    gm_ref, ret_ref, att_ref, dk_ref, dv_ref, *scatter_refs = refs[:-7]
    in_send, in_recv, in_local, out_send, out_recv, out_local, att_sem = refs[-7:]
    length = x_ref.shape[0]
    hk = hp * KD
    peers, rows = leaving_ref.shape[:2]
    blocks = length // bq
    incoming = exchange_work(
        [leaving_ref.at[peer] for peer in range(peers)],
        lambda peer: gm_ref.at[pl.ds(peer * rows, rows)],
        in_send,
        in_recv,
        in_local,
    )
    leaving = exchange_work(
        [ret_ref.at[pl.ds(peer * rows, rows)] for peer in range(peers)],
        lambda peer: returned.at[peer],
        out_send,
        out_recv,
        out_local,
    )
    loads = [
        pltpu.make_async_copy(
            att_in.at[:, pl.ds(block * bq, bq)], att_ref.at[block % 2], att_sem.at[block]
        )
        for block in range(blocks)
    ]
    for load in loads[:2]:
        load.start()
    start_together(True)
    for start, _, _ in incoming:
        start()
    work, last = scatter_work(plan, arrays, spacing, (sources, outs, scatter_refs))
    dk_ref[...] = jnp.zeros_like(dk_ref)
    dv_ref[...] = jnp.zeros_like(dv_ref)
    dtab_ref[...] = jnp.zeros_like(dtab_ref)
    bias_ref[...] = jnp.zeros_like(bias_ref)
    for turn in range(turns_of(work, spacing)):
        run_turn(work, spacing, turn, last)
        for block in range(blocks):
            if block_turns[block] != turn:
                continue
            if block == 0:
                for _, arrive, _ in incoming:
                    arrive()
            loads[block].wait()
            attend_back(
                length,
                bq,
                hp,
                vd,
                block,
                x_ref,
                tab_ref,
                att_ref.at[block % 2],
                gm_ref,
                ret_ref,
                (dk_ref, dv_ref, dtab_ref, bias_ref),
            )
            if block + 2 < blocks:
                loads[block + 2].start()
            if block == blocks - 1:
                ret_ref[:, hk : 2 * hk] = dk_ref[...].T.astype(bfloat)
                ret_ref[:, 2 * hk :] = dv_ref[...].T.astype(bfloat)
                for start, _, _ in leaving:
                    start()
    for _, arrive, _ in leaving:
        arrive()
    for _, _, finish in incoming + leaving:
        finish()
    finish_sends(work)


def scatter_and_attend_back(
    grads, widths, lines_last, spacing, block_turns, leaving, x, tab, attention, dims
):
    hp, vd, bq = dims
    peers, rows, _ = leaving.shape
    length = peers * rows
    hk = hp * KD
    back = 2 * hk + hp * vd
    plan, arrays = scatter_plan(grads, widths, lines_last)
    flat, specs = flat_sources(grads)
    anywhere = pl.BlockSpec(memory_space=pl.ANY)
    vmem = pl.BlockSpec(memory_space=pltpu.VMEM)
    dma = pltpu.SemaphoreType.DMA
    return pl.pallas_call(
        functools.partial(attend_back_kernel, plan, arrays, spacing, block_turns, dims),
        in_specs=specs + [anywhere, vmem, vmem, anywhere],
        out_specs=[vmem] * len(grads) + [anywhere, vmem, vmem],
        out_shape=[jax.ShapeDtypeStruct((a[0], a[1] * a[2]), single) for a in arrays]
        + [
            jax.ShapeDtypeStruct((peers, rows, back), bfloat),
            jax.ShapeDtypeStruct(tab.shape, single),
            jax.ShapeDtypeStruct((8, hk), single),
        ],
        scratch_shapes=[
            pltpu.VMEM((length, hp * vd), bfloat),
            pltpu.VMEM((length, back), bfloat),
            pltpu.VMEM((2, hp, bq, length), bfloat),
            pltpu.VMEM((hk, length), single),
            pltpu.VMEM((hp * vd, length), single),
        ]
        + scatter_scratch(plan, arrays, spacing)
        + [dma((peers,))] * 6
        + [dma((length // bq,))],
        compiler_params=pltpu.CompilerParams(
            collective_id=2, has_side_effects=True, vmem_limit_bytes=VMEM_LIMIT
        ),
    )(*flat, leaving, x, tab, attention)


def shards(
    inputs,
    cotangent,
    ln1_scale,
    ln1_offset,
    w_query,
    w_key,
    w_value,
    w_rel,
    content_bias,
    position_bias,
    w_out,
    b_out,
    ln2_scale,
    ln2_offset,
    w_in,
    b_in,
    w_mlp_out,
    b_mlp_out,
):
    win_size, seq_size = lax.axis_size("win"), lax.axis_size("seq")
    devices = win_size * seq_size
    seq = lax.axis_index("seq")
    window_count, row_count, width = inputs.shape
    tokens = window_count * row_count
    hk = HEADS * KD
    vd = width // HEADS
    hp = HEADS // seq_size
    hidden = w_in.shape[1]
    scale_factor = KD ** (-0.5)

    wide = (ln1_scale, ln1_offset, b_out, ln2_scale, ln2_offset, b_mlp_out)
    narrow = (content_bias, position_bias)
    packed = jnp.concatenate(wide + (b_in,) + narrow + (w_rel.T.reshape(-1),))
    cuts = [len(wide) * ln1_scale.shape[0]]
    cuts.append(cuts[0] + b_in.shape[0])
    cuts.append(cuts[1] + len(narrow) * content_bias.shape[0])
    packed_size = packed.shape[0]
    small_cols = -(-packed_size // 4096) * 256
    small_size = 16 * small_cols
    packed = jnp.pad(packed, (0, small_size - packed_size)).reshape(16, small_cols)
    packed, whole_qk, whole_v = gather_all(
        (packed, jnp.concatenate([w_query, w_key], axis=1), w_value),
        (256, 512, 512),
        lambda number: number % 3 != 2,
        3,
        0,
    )
    packed = packed.reshape(devices, small_size)
    whole_qk = whole_qk.reshape(width, 2 * hk)
    whole_v = whole_v.reshape(width, width)

    def rows_of(columns, count):
        rows = columns.reshape(devices, count, -1).transpose(1, 0, 2)
        return rows.reshape(count, -1).astype(single)

    wide_rows = rows_of(packed[:, : cuts[0]], len(wide))
    ln1_gain, ln1_shift, bias_out, ln2_gain, ln2_shift, bias_mlp = wide_rows
    bias_in = packed[:, cuts[0] : cuts[1]].reshape(-1).astype(single)
    bias_content, bias_position = rows_of(packed[:, cuts[1] : cuts[2]], len(narrow))
    whole_rel = packed[:, cuts[2] : packed_size].reshape(hk, F)

    features = jnp.pad(rel_features(WLEN, F).astype(bfloat), ((0, 1), (0, 0)))
    own_rel = lax.dynamic_slice_in_dim(whole_rel, seq * hp * KD, hp * KD, 0)
    table = jnp.einsum("cf,tf->ct", own_rel, features, preferred_element_type=single).astype(bfloat)

    source = inputs.reshape(tokens, width).astype(single)
    normed_one_f, norm_one_back = jax.vjp(layer_norm, source, ln1_gain, ln1_shift)
    normed_one = normed_one_f.astype(bfloat)
    proj_qk = jnp.dot(normed_one, whole_qk, preferred_element_type=single)
    query = proj_qk[:, :hk] * scale_factor
    proj_v = jnp.dot(normed_one, whole_v, preferred_element_type=single)
    parts = (
        (query + bias_content).astype(bfloat),
        (query + bias_position).astype(bfloat),
        proj_qk[:, hk:].astype(bfloat),
        proj_v.astype(bfloat),
    )
    outgoing = jnp.concatenate([part.reshape(tokens, seq_size, -1) for part in parts], axis=2)
    outgoing = jnp.transpose(outgoing, (1, 0, 2))
    in_kernel = w_out.shape[0] % 16 == 0 and hp * vd % 128 == 0
    row_vectors = wide_rows[2:]
    cot_rows = cotangent.reshape(tokens, width)
    first_results, ffn_results = gather_and_attend(
        (w_out, w_mlp_out, w_in),
        (512, 256, 512),
        lambda number: number % 3 != 1,
        3,
        FIRST_BLOCK_TURN,
        outgoing,
        table,
        (inputs.reshape(tokens, width), cot_rows, row_vectors, bias_in[None, :]),
        (hp, vd, BLOCK_Q, in_kernel),
    )
    whole_out, gathered_mlp, whole_in, heads_in, attention = first_results
    whole_out = whole_out.reshape(width, width)
    whole_in = whole_in.reshape(width, hidden)
    whole_mlp = gathered_mlp.reshape(hidden, width)
    if in_kernel:
        attended, hidden_in, normed_two, activation, grad_pre = ffn_results
    else:
        attended = jnp.transpose(ffn_results[0], (1, 0, 2)).reshape(tokens, width)
        branch = jnp.dot(attended, whole_out, preferred_element_type=single)
        hidden_in = source + branch + bias_out
        normed_two = layer_norm(hidden_in, ln2_gain, ln2_shift).astype(bfloat)
        pre_act = jnp.dot(normed_two, whole_in, preferred_element_type=single) + bias_in
        gelu_out, gelu_back = jax.vjp(jax.nn.gelu, pre_act)
        activation = gelu_out.astype(bfloat)
        result = hidden_in + jnp.dot(activation, whole_mlp, preferred_element_type=single)
        result = (result + bias_mlp).astype(bfloat)
        grad_act = jnp.einsum("td,fd->tf", cot_rows, whole_mlp, preferred_element_type=single)
        grad_pre = gelu_back(grad_act)[0].astype(bfloat)

    grid = (win_size // CORES, CORES) + (2,) * (seq_size.bit_length() - 1)

    def weight_grad(left, right):
        if left.shape[1] // devices % 16 == 0:
            return left, right
        grad = jnp.einsum("td,te->de", left, right, preferred_element_type=single).astype(bfloat)
        rows, cols = grad.shape
        return grad.reshape(grid + (rows // devices, cols))

    grad_mlp = weight_grad(activation, cot_rows)
    grad_bias_mlp = jnp.sum(cot_rows.astype(single), axis=0)
    grad_in = weight_grad(normed_two, grad_pre)
    grad_bias_in = jnp.sum(grad_pre.astype(single), axis=0)
    grad_normed_two = jnp.einsum("tf,df->td", grad_pre, whole_in, preferred_element_type=single)
    _, norm_two_back = jax.vjp(layer_norm, hidden_in, ln2_gain, ln2_shift)
    hidden_term, grad_ln2_gain, grad_ln2_shift = norm_two_back(grad_normed_two)
    grad_hidden = cot_rows.astype(single) + hidden_term
    grad_branch = grad_hidden.astype(bfloat)
    grad_out = weight_grad(attended, grad_branch)
    grad_bias_out = jnp.sum(grad_branch.astype(single), axis=0)
    grad_mixed = jnp.einsum(
        "te,de->td", grad_branch, whole_out, preferred_element_type=single
    ).astype(bfloat)
    grad_mixed = jnp.transpose(grad_mixed.reshape(tokens, seq_size, hp * vd), (1, 0, 2))
    grad_mlp, grad_in, returned, grad_table, grad_bias = scatter_and_attend_back(
        (grad_mlp, grad_in),
        (256, 512),
        lambda number: number % 4 != 0,
        2,
        BLOCK_TURNS,
        grad_mixed,
        heads_in,
        table,
        attention,
        (hp, vd, BLOCK_Q),
    )
    own = hp * KD
    returned = jnp.transpose(returned, (1, 0, 2))
    grad_qk_rows = jnp.concatenate(
        [
            returned[:, :, :own].reshape(tokens, hk),
            returned[:, :, own : 2 * own].reshape(tokens, hk),
        ],
        axis=1,
    )
    grad_v_rows = returned[:, :, 2 * own :].reshape(tokens, width)
    grad_qk = weight_grad(normed_one, grad_qk_rows)
    grad_v = weight_grad(normed_one, grad_v_rows)
    grad_normed_one = jnp.einsum(
        "tk,dk->td", grad_qk_rows, whole_qk, preferred_element_type=single
    ) + jnp.einsum("tk,dk->td", grad_v_rows, whole_v, preferred_element_type=single)
    source_term, grad_ln1_gain, grad_ln1_shift = norm_one_back(grad_normed_one)
    grad_inputs = (grad_hidden + source_term).reshape(inputs.shape)

    grad_rel = jnp.dot(grad_table, features.astype(single), precision=lax.Precision.HIGHEST)
    whole_grad_rel = lax.dynamic_update_slice_in_dim(
        jnp.zeros((hk, F), single), grad_rel, seq * own, 0
    )

    wide_grads = jnp.stack(
        [
            grad_ln1_gain,
            grad_ln1_shift,
            grad_bias_out,
            grad_ln2_gain,
            grad_ln2_shift,
            grad_bias_mlp,
        ]
    )
    narrow_grads = lax.dynamic_update_slice_in_dim(
        jnp.zeros((len(narrow), hk), single), grad_bias[: len(narrow)], seq * own, 1
    )

    def by_owner(rows):
        count = rows.shape[0]
        return rows.reshape(count, devices, -1).transpose(1, 0, 2).reshape(devices, -1)

    small = jnp.concatenate(
        [
            by_owner(wide_grads),
            grad_bias_in.reshape(devices, -1),
            by_owner(narrow_grads),
            whole_grad_rel.reshape(devices, -1),
        ],
        axis=1,
    )
    small = jnp.pad(small, ((0, 0), (0, small_size - packed_size))).astype(bfloat)
    final = (grad_out, grad_qk, grad_v, small.reshape(grid + (16, small_cols)))
    cuts_of = (512, 512, 512, 256)
    if in_kernel:
        layer_ins = (gathered_mlp, activation, hidden_in, row_vectors[3:4])
        grad_out, grad_qk, grad_v, small, result = scatter_and_widen(
            final, cuts_of, lambda number: number % 4 != 0, 2, 3, layer_ins, 3
        )
    else:
        grad_out, grad_qk, grad_v, small = scatter_all(
            final, cuts_of, lambda number: number % 4 != 0, 2, 3
        )
    layer_out = result.reshape(inputs.shape)
    small = small.reshape(-1)[:packed_size]
    wide_own = small[: cuts[0]].reshape(len(wide), -1)
    narrow_own = small[cuts[1] : cuts[2]].reshape(len(narrow), -1)
    own_grad_rel = small[cuts[2] :].reshape(-1, F).T
    return (
        layer_out,
        grad_inputs,
        wide_own[0],
        wide_own[1],
        grad_qk[:, :hk],
        grad_qk[:, hk:],
        grad_v,
        own_grad_rel,
        narrow_own[0],
        narrow_own[1],
        grad_out,
        wide_own[2],
        wide_own[3],
        wide_own[4],
        grad_in,
        small[cuts[0] : cuts[1]],
        grad_mlp,
        wide_own[5],
    )


def solution(mesh):
    in_specs = (
        P("win", "seq", None),
        P("win", "seq", None),
        P(("win", "seq")),
        P(("win", "seq")),
        P(("win", "seq"), None),
        P(("win", "seq"), None),
        P(("win", "seq"), None),
        P(None, ("win", "seq")),
        P(("win", "seq")),
        P(("win", "seq")),
        P(("win", "seq"), None),
        P(("win", "seq")),
        P(("win", "seq")),
        P(("win", "seq")),
        P(("win", "seq"), None),
        P(("win", "seq")),
        P(("win", "seq"), None),
        P(("win", "seq")),
    )
    out_specs = (
        P("win", "seq", None),
        P("win", "seq", None),
        P(("win", "seq")),
        P(("win", "seq")),
        P(("win", "seq"), None),
        P(("win", "seq"), None),
        P(("win", "seq"), None),
        P(None, ("win", "seq")),
        P(("win", "seq")),
        P(("win", "seq")),
        P(("win", "seq"), None),
        P(("win", "seq")),
        P(("win", "seq")),
        P(("win", "seq")),
        P(("win", "seq"), None),
        P(("win", "seq")),
        P(("win", "seq"), None),
        P(("win", "seq")),
    )
    return jax.shard_map(shards, mesh=mesh, in_specs=in_specs, out_specs=out_specs, check_vma=False)
```

```python
import functools
import math

import jax
import jax.numpy as jnp
from jax import lax
from jax.experimental import pallas as pl
from jax.experimental.pallas import tpu as pltpu
from jax.sharding import PartitionSpec as P

HEADS = 8
KD = 64
F = 192
WLEN = 1536
CORES = 2
BLOCK_Q = 256
FIRST_BLOCK_TURN = 8
BLOCK_TURNS = (6, 8, 10, 12, 14, 16)
VMEM_LIMIT = 62 * 2**20
bfloat = jnp.bfloat16
single = jnp.float32


def rel_features(length, feature_count):
    per_basis = feature_count // 6
    offsets = jnp.arange(-length + 1, length).astype(jnp.float32)
    magnitude = jnp.abs(offsets)[:, None]
    half_life = 2.0 ** jnp.linspace(3.0, math.log2(length), per_basis)
    decaying = jnp.exp(-math.log(2.0) / half_life * magnitude)
    widths = 2.0 ** jnp.arange(1, per_basis + 1).astype(jnp.float32) - 1.0
    central = (widths > magnitude).astype(jnp.float32)
    stddev = length / (2.0 * per_basis)
    centers = jnp.linspace(length / per_basis, float(length), per_basis)
    shape_param = (centers / stddev) ** 2
    inverse_scale = centers / stddev**2
    peak_at = (shape_param - 1.0) / inverse_scale
    log_prob = (shape_param - 1.0) * (
        jnp.log(jnp.maximum(magnitude, 0.5)) - jnp.log(peak_at)
    ) - inverse_scale * (magnitude - peak_at)
    density = jnp.exp(log_prob) + 1e-08
    gamma_pdf = density / jnp.max(density, axis=0, keepdims=True)
    basis_set = jnp.concatenate([decaying, central, gamma_pdf], axis=1)
    return jnp.concatenate([basis_set, jnp.sign(offsets)[:, None] * basis_set], axis=1)


def layer_norm(values, norm_gain, norm_shift):
    centered = values - jnp.mean(values, axis=-1, keepdims=True)
    variance = jnp.mean(centered * centered, axis=-1, keepdims=True)
    return centered * lax.rsqrt(variance + 1e-05) * norm_gain + norm_shift


def attend_block(length, bq, hp, vd, block, x_ref, tab_ref, att_ref, mixed_ref):
    hk = hp * KD
    first = block * bq
    rows = pl.ds(first, bq)
    span = length + bq
    outs = []
    for h in range(hp):
        qc = x_ref[rows, pl.ds(h * KD, KD)]
        qp = x_ref[rows, pl.ds(hk + h * KD, KD)]
        k = x_ref[:, pl.ds(2 * hk + h * KD, KD)]
        v = x_ref[:, pl.ds(3 * hk + h * vd, vd)]
        table = tab_ref[pl.ds(h * KD, KD), pl.ds(length - bq - first, span)]
        raw = jnp.dot(qp, table, preferred_element_type=single)
        rel = pltpu.roll(raw, span - bq + 1, 1, stride=1, stride_axis=0)[:, :length]
        s = rel + lax.dot_general(qc, k, (((1,), (1,)), ((), ())), preferred_element_type=single)
        e = jnp.exp(s - jnp.max(s, axis=-1, keepdims=True))
        inverse = 1.0 / jnp.sum(e, axis=-1, keepdims=True)
        att = (e * inverse).astype(bfloat)
        att_ref[h] = att
        outs.append(jnp.dot(att, v, preferred_element_type=single).astype(bfloat))
    mixed_ref[rows, :] = jnp.concatenate(outs, axis=1) if hp > 1 else outs[0]


def attend_back(length, bq, hp, vd, block, x_ref, tab_ref, att_ref, gm_ref, ret_ref, sums):
    dk_ref, dv_ref, dtab_ref, bias_ref = sums
    hk = hp * KD
    first = block * bq
    rows = pl.ds(first, bq)
    span = length + bq
    row = lax.broadcasted_iota(jnp.int32, (bq, bq), 0)
    col = lax.broadcasted_iota(jnp.int32, (bq, bq), 1)
    flip = jnp.where(row + col == bq - 1, 1.0, 0.0).astype(bfloat)

    def flipped(v):
        return jnp.dot(flip, v, preferred_element_type=single)

    def dot(left, right, left_dim, right_dim):
        return lax.dot_general(
            left, right, (((left_dim,), (right_dim,)), ((), ())), preferred_element_type=single
        )

    dqs, bc, bp = [], [], []
    for h in range(hp):
        own = pl.ds(h * KD, KD)
        table_cols = pl.ds(length - bq - first, span)
        qc = flipped(x_ref[rows, own]).astype(bfloat)
        qp = flipped(x_ref[rows, pl.ds(hk + h * KD, KD)]).astype(bfloat)
        k = x_ref[:, pl.ds(2 * hk + h * KD, KD)]
        v = x_ref[:, pl.ds(3 * hk + h * vd, vd)]
        gm = gm_ref[rows, pl.ds(h * vd, vd)]
        att = att_ref[h]
        dv_ref[pl.ds(h * vd, vd), :] += dot(gm, att, 0, 0)
        dp = dot(flipped(gm).astype(bfloat), v, 1, 1)
        af = flipped(att)
        t = af * dp
        delta = jnp.sum(t, axis=-1, keepdims=True)
        ds = (t - af * delta).astype(bfloat)
        dk_ref[own, :] += dot(qc, ds, 0, 0)
        gc = jnp.dot(ds, k, preferred_element_type=single)
        wide = jnp.concatenate([ds.astype(single), jnp.zeros((bq, bq), single)], axis=1)
        rel = pltpu.roll(wide, 0, 1, stride=1, stride_axis=0).astype(bfloat)
        gp = dot(rel, tab_ref[own, table_cols], 1, 1)
        dtab_ref[own, table_cols] += dot(qp, rel, 0, 0)
        dqs.append(flipped(((gc + gp) * KD**-0.5).astype(bfloat)).astype(bfloat))
        bc.append(jnp.sum(gc, axis=0, keepdims=True))
        bp.append(jnp.sum(gp, axis=0, keepdims=True))
    ret_ref[rows, :hk] = jnp.concatenate(dqs, axis=1) if hp > 1 else dqs[0]
    bias_ref[0:1, :] += jnp.concatenate(bc, axis=1) if hp > 1 else bc[0]
    bias_ref[1:2, :] += jnp.concatenate(bp, axis=1) if hp > 1 else bp[0]


def partners():
    win, seq = lax.axis_index("win"), lax.axis_index("seq")
    chips = lax.axis_size("win") // CORES
    bits = lax.axis_size("seq").bit_length() - 1
    return win, seq, win // CORES, win % CORES, chips, bits


def start_together(whole_seq=False):
    win, seq, here, core, chips, bits = partners()
    barrier = pltpu.get_barrier_semaphore()

    def greet(to_win, to_seq):
        pl.semaphore_signal(
            barrier, inc=1, device_id=(to_win, to_seq), device_id_type=pl.DeviceIdType.MESH
        )

    greet(win ^ 1, seq)
    across = range(1, 1 << bits) if whole_seq else [1 << bit for bit in range(bits)]
    for distance in across:
        greet(win, seq ^ distance)

    @pl.when(here > 0)
    def _():
        greet(win - CORES, seq)

    @pl.when(here < chips - 1)
    def _():
        greet(win + CORES, seq)

    ends = jnp.where(here > 0, 1, 0) + jnp.where(here < chips - 1, 1, 0)
    pl.semaphore_wait(barrier, 1 + len(across) + ends)


def gather_work(plan, shards, outs, send_sem, recv_sem, local_sem):
    win, seq, here, core, chips, bits = partners()
    own_bits = tuple((seq >> bit) & 1 for bit in reversed(range(bits)))
    own_seq = {bit: (seq >> bit) & 1 for bit in range(bits)}

    def region(chunk, chip, done, lead=0, span=None):
        which, col, cols, _ = chunk
        start, size = (col + lead, cols) if span is None else (col + lead, span)
        index = tuple(slice(None) if bit in done else own_seq[bit] for bit in reversed(range(bits)))
        return outs[which].at[(chip, core) + index + (slice(None), pl.ds(start, size))]

    def copy(ref, number, kind, to_win, to_seq):
        return pltpu.make_async_remote_copy(
            src_ref=ref,
            dst_ref=ref,
            send_sem=send_sem.at[number, kind],
            recv_sem=recv_sem.at[number, kind],
            device_id=(to_win, to_seq),
            device_id_type=pl.DeviceIdType.MESH,
        )

    chip_steps = chips - 1
    every_bit = frozenset(range(bits))

    def guarded(condition, action):
        pl.when(condition)(action)

    def chip_stage(chunk, number, step, done):
        up_shard, down_shard = here - step, here + step
        up = copy(region(chunk, jnp.maximum(up_shard, 0), done), number, step, win + CORES, seq)
        down = copy(
            region(chunk, jnp.minimum(down_shard, chips - 1), done),
            number,
            chip_steps + step,
            win - CORES,
            seq,
        )
        sends_up = (up_shard >= 0) & (here < chips - 1)
        sends_down = (down_shard < chips) & (here > 0)
        gets_up = here >= step + 1
        gets_down = here + step + 1 < chips

        def start():
            guarded(sends_up, up.start)
            guarded(sends_down, down.start)

        def arrive():
            guarded(gets_up, up.wait_recv)
            guarded(gets_down, down.wait_recv)

        def finish():
            guarded(sends_up, up.wait_send)
            guarded(sends_down, down.wait_send)

        return start, arrive, finish

    def bit_stage(chunk, number, step, chip):
        half = chunk[2] // 2
        copies = []
        for part in range(2):
            order = list(range(bits)) if part == 0 else list(reversed(range(bits)))
            ref = region(chunk, chip, frozenset(order[:step]), part * half, half)
            kind = 2 * chip_steps + part * bits + step
            copies.append(copy(ref, number, kind, win, seq ^ (1 << order[step])))

        def start():
            for item in copies:
                item.start()

        def arrive():
            for item in copies:
                item.wait_recv()

        def finish():
            for item in copies:
                item.wait_send()

        return start, arrive, finish

    def core_stage(chunk, number):
        kind = 2 * chip_steps + 2 * bits
        item = copy(region(chunk, slice(None), every_bit), number, kind, win ^ 1, seq)
        return item.start, item.wait_recv, item.wait_send

    def stages(chunk, number):
        if chunk[3]:
            line = [chip_stage(chunk, number, step, frozenset()) for step in range(chip_steps)]
            cube = [bit_stage(chunk, number, step, slice(None)) for step in range(bits)]
            return line + cube + [core_stage(chunk, number)]
        cube = [bit_stage(chunk, number, step, here) for step in range(bits)]
        line = [chip_stage(chunk, number, step, every_bit) for step in range(chip_steps)]
        return cube + line + [core_stage(chunk, number)]

    own = [
        pltpu.make_async_copy(shard, out.at[(here, core) + own_bits], local_sem.at[which])
        for which, (shard, out) in enumerate(zip(shards, outs))
    ]
    return own, [stages(chunk, number) for number, chunk in enumerate(plan)]


def run_turn(work, spacing, turn, last=None):
    for number, stages in enumerate(work):
        at, off = divmod(turn - number, spacing)
        if off == 0 and 0 < at <= len(stages):
            stages[at - 1][1]()
            if at == len(stages) and last is not None:
                last(number)
        if off == 0 and 0 <= at < len(stages):
            stages[at][0]()


def turns_of(work, spacing):
    return len(work) + spacing * len(work[0])


def finish_sends(work):
    for stages in work:
        for stage in stages:
            stage[2]()


def gather_kernel(plan, count, spacing, *refs):
    shards, outs, sems = refs[:count], refs[count : 2 * count], refs[2 * count :]
    own, work = gather_work(plan, shards, outs, *sems)
    for item in own:
        item.start()
    start_together()
    for item in own:
        item.wait()
    for turn in range(turns_of(work, spacing)):
        run_turn(work, spacing, turn)
    finish_sends(work)


def gather_plan(shards, widths, lines_first):
    plan = []
    for which, (shard, width) in enumerate(zip(shards, widths)):
        for col in range(0, shard.shape[1], width):
            plan.append((which, col, width, lines_first(len(plan))))
    return tuple(plan)


def gather_sems(plan, count):
    chips = lax.axis_size("win") // CORES
    bits = lax.axis_size("seq").bit_length() - 1
    kinds = 2 * (chips - 1) + 2 * bits + 1
    return [
        pltpu.SemaphoreType.DMA((len(plan), kinds)),
        pltpu.SemaphoreType.DMA((len(plan), kinds)),
        pltpu.SemaphoreType.DMA((count,)),
    ]


def gathered_shapes(shards):
    chips = lax.axis_size("win") // CORES
    bits = lax.axis_size("seq").bit_length() - 1
    return [jax.ShapeDtypeStruct((chips, CORES) + (2,) * bits + s.shape, s.dtype) for s in shards]


def gather_all(shards, widths, lines_first, spacing, collective_id):
    plan = gather_plan(shards, widths, lines_first)
    return pl.pallas_call(
        functools.partial(gather_kernel, plan, len(shards), spacing),
        in_specs=[pl.BlockSpec(memory_space=pltpu.VMEM)] * len(shards),
        out_specs=[pl.BlockSpec(memory_space=pl.ANY)] * len(shards),
        out_shape=gathered_shapes(shards),
        scratch_shapes=gather_sems(plan, len(shards)),
        compiler_params=pltpu.CompilerParams(collective_id=collective_id, has_side_effects=True),
    )(*shards)


def exchange_work(parts, target, send_sem, recv_sem, local_sem):
    win, seq = lax.axis_index("win"), lax.axis_index("seq")
    items = []
    for peer, part in enumerate(parts):
        sent = pltpu.make_async_remote_copy(
            src_ref=part,
            dst_ref=target(seq),
            send_sem=send_sem.at[peer],
            recv_sem=recv_sem.at[seq],
            device_id=(win, peer),
            device_id_type=pl.DeviceIdType.MESH,
        )
        got = pltpu.make_async_remote_copy(
            src_ref=part,
            dst_ref=target(peer),
            send_sem=send_sem.at[peer],
            recv_sem=recv_sem.at[peer],
            device_id=(win, peer),
            device_id_type=pl.DeviceIdType.MESH,
        )
        own = pltpu.make_async_copy(part, target(peer), local_sem.at[peer])

        def start(peer=peer, sent=sent, own=own):
            pl.when(peer != seq)(sent.start)
            pl.when(peer == seq)(own.start)

        def arrive(peer=peer, got=got, own=own):
            pl.when(peer != seq)(got.wait_recv)
            pl.when(peer == seq)(own.wait)

        def finish(peer=peer, sent=sent):
            pl.when(peer != seq)(sent.wait_send)

        items.append((start, arrive, finish))
    return items


def gelu_parts(v):
    root = math.sqrt(2.0 / math.pi)
    t = jnp.tanh(root * (v + 0.044715 * (v * v * v)))
    cdf = 0.5 * (1.0 + t)
    slope = cdf + 0.5 * v * (1.0 - t * t) * (root * (1.0 + 3 * 0.044715 * (v * v)))
    return v * cdf, slope


def ffn_tasks(plan, gathered, received, ins, outs, scratch):
    source, cot, vectors, bias_in = ins
    attended, hidden_in, normed_two, activation, grad_pre = outs
    grad_act, rings, load_sem = scratch
    peers = received.shape[0]
    last = {chunk[0]: number for number, chunk in enumerate(plan)}
    first = {}
    for number, chunk in enumerate(plan):
        first.setdefault(chunk[0], number)

    def task(number, chunk):
        which, col, cols, _ = chunk
        ring = rings[which]
        held = ring.at[number % 2]
        columns = pl.ds(col, cols)
        lead = (slice(None),) * (len(ring.shape) - 2)
        load = pltpu.make_async_copy(
            gathered[which].at[lead + (columns,)], held, load_sem.at[number]
        )

        def weight():
            return held[...].reshape(math.prod(ring.shape[1:-1]), cols)

        def project():
            if number == first[which]:
                attended[...] = jnp.concatenate([received[peer] for peer in range(peers)], axis=1)
            branch = jnp.dot(attended[...], weight(), preferred_element_type=single)
            hidden_in[:, columns] = (
                source[:, columns].astype(single) + branch + vectors[0:1, columns]
            )
            if number == last[which]:
                normed = layer_norm(hidden_in[...], vectors[1:2, :], vectors[2:3, :])
                normed_two[...] = normed.astype(bfloat)

        def fold():
            term = lax.dot_general(
                cot[:, columns], weight(), (((1,), (1,)), ((), ())), preferred_element_type=single
            )
            grad_act[...] = term if number == first[which] else grad_act[...] + term

        def widen():
            pre = jnp.dot(normed_two[...], weight(), preferred_element_type=single)
            value, derivative = gelu_parts(pre + bias_in[0:1, columns])
            activation[:, columns] = value.astype(bfloat)
            grad_pre[:, columns] = (grad_act[:, columns] * derivative).astype(bfloat)

        return load, (project, fold, widen)[which]

    return [task(number, chunk) for number, chunk in enumerate(plan)]


def attend_kernel(plan, count, spacing, first_turn, dims, *refs):
    hp, vd, bq, ffn = dims
    shards, (outgoing, tab_ref), refs = refs[:count], refs[count : count + 2], refs[count + 2 :]
    if ffn:
        ffn_ins, refs = refs[:4], refs[4:]
    outs, (x_ref, att_out), refs = refs[:count], refs[count : count + 2], refs[count + 2 :]
    if not ffn:
        received, refs = refs[0], refs[1:]
    else:
        ffn_outs, refs = refs[:5], refs[5:]
        (grad_act, *rings, load_sem), refs = refs[: 2 + count], refs[2 + count :]
        received, refs = refs[0], refs[1:]
    att_ref, mixed_ref, *gather_refs = refs[:-7]
    in_send, in_recv, in_local, out_send, out_recv, out_local, att_sem = refs[-7:]
    length = x_ref.shape[0]
    peers, rows = outgoing.shape[0], outgoing.shape[1]
    own, work = gather_work(plan, shards, outs, *gather_refs)
    tasks = []
    if ffn:
        tasks = ffn_tasks(plan, outs, received, ffn_ins, ffn_outs, (grad_act, rings, load_sem))
    incoming = exchange_work(
        [outgoing.at[peer] for peer in range(peers)],
        lambda peer: x_ref.at[pl.ds(peer * rows, rows)],
        in_send,
        in_recv,
        in_local,
    )
    leaving = exchange_work(
        [mixed_ref.at[pl.ds(peer * rows, rows)] for peer in range(peers)],
        lambda peer: received.at[peer],
        out_send,
        out_recv,
        out_local,
    )
    for item in own:
        item.start()
    start_together(True)
    for item in own:
        item.wait()
    for start, _, _ in incoming:
        start()
    blocks = length // bq
    kept = [
        pltpu.make_async_copy(
            att_ref.at[block % 2], att_out.at[:, pl.ds(block * bq, bq)], att_sem.at[block]
        )
        for block in range(blocks)
    ]
    sent = loaded = done = 0
    arrived = set()
    for turn in range(turns_of(work, spacing)):
        run_turn(work, spacing, turn, arrived.add)
        block = turn - first_turn
        if block == 0:
            for _, arrive, _ in incoming:
                arrive()
        if 0 <= block < blocks:
            if block >= 2:
                kept[block - 2].wait()
            attend_block(length, bq, hp, vd, block, x_ref, tab_ref, att_ref.at[block % 2], mixed_ref)
            kept[block].start()
            while sent < peers and (sent + 1) * rows <= (block + 1) * bq:
                leaving[sent][0]()
                sent += 1
        if block >= blocks and done < loaded:
            if done == 0:
                for _, arrive, _ in leaving:
                    arrive()
            tasks[done][0].wait()
            tasks[done][1]()
            done += 1
        while loaded < len(tasks) and loaded in arrived and loaded < done + 2:
            tasks[loaded][0].start()
            loaded += 1
    if done == 0:
        for _, arrive, _ in leaving:
            arrive()
    while done < len(tasks):
        while loaded < len(tasks) and loaded < done + 2:
            tasks[loaded][0].start()
            loaded += 1
        tasks[done][0].wait()
        tasks[done][1]()
        done += 1
    for _, _, finish in incoming + leaving:
        finish()
    for item in kept[-2:]:
        item.wait()
    finish_sends(work)


def gather_and_attend(shards, widths, lines_first, spacing, first_turn, outgoing, tab, ffn_ins, dims):
    hp, vd, bq, ffn = dims
    peers, rows, cols = outgoing.shape
    length = peers * rows
    plan = gather_plan(shards, widths, lines_first)
    count = len(shards)
    anywhere = pl.BlockSpec(memory_space=pl.ANY)
    vmem = pl.BlockSpec(memory_space=pltpu.VMEM)
    dma = pltpu.SemaphoreType.DMA
    gathered = gathered_shapes(shards)
    extra_out, extra_scratch = [], []
    if ffn:
        width, hidden = ffn_ins[0].shape[1], ffn_ins[3].shape[1]
        extra_out = [
            jax.ShapeDtypeStruct((rows, width), bfloat),
            jax.ShapeDtypeStruct((rows, width), single),
            jax.ShapeDtypeStruct((rows, width), bfloat),
            jax.ShapeDtypeStruct((rows, hidden), bfloat),
            jax.ShapeDtypeStruct((rows, hidden), bfloat),
        ]
        extra_scratch = [pltpu.VMEM((rows, hidden), single)]
        for shape, cut in zip(gathered, widths):
            extra_scratch.append(pltpu.VMEM((2,) + shape.shape[:-1] + (cut,), bfloat))
        extra_scratch += [dma((len(plan),)), pltpu.VMEM((peers, rows, hp * vd), bfloat)]
    else:
        ffn_ins = ()
        extra_out = [jax.ShapeDtypeStruct((peers, rows, hp * vd), bfloat)]
    result = pl.pallas_call(
        functools.partial(attend_kernel, plan, count, spacing, first_turn, dims),
        in_specs=[vmem] * count + [anywhere, vmem] + [vmem] * len(ffn_ins),
        out_specs=[anywhere] * count + [vmem, anywhere] + [vmem if ffn else anywhere] * len(extra_out),
        out_shape=gathered
        + [
            jax.ShapeDtypeStruct((length, cols), bfloat),
            jax.ShapeDtypeStruct((hp, length, length), bfloat),
        ]
        + extra_out,
        scratch_shapes=extra_scratch
        + [
            pltpu.VMEM((2, hp, bq, length), bfloat),
            pltpu.VMEM((length, hp * vd), bfloat),
        ]
        + gather_sems(plan, count)
        + [dma((peers,))] * 6
        + [dma((length // bq,))],
        compiler_params=pltpu.CompilerParams(
            collective_id=1, has_side_effects=True, vmem_limit_bytes=VMEM_LIMIT
        ),
    )(*shards, outgoing, tab, *ffn_ins)
    return result[: count + 2], result[count + 2 :]


def scatter_work(plan, arrays, spacing, refs):
    count = len(arrays)
    sources, outs, rest = refs
    win, seq, here, core, chips, bits = partners()
    chip_steps = chips - 1
    ring, kept, rest = rest[:count], rest[count : 2 * count], rest[2 * count :]
    from_bits, rest = rest[: count * bits], rest[count * bits :]
    from_chips, rest = rest[:count], rest[count:]
    send_sem, recv_sem, local_sem = rest
    own_seq = {bit: (seq >> bit) & 1 for bit in range(bits)}

    def add(target, source):
        target[...] = target[...] + source[...]

    def slabs(chunk, chip, bit_index, lead=0, span=None):
        which, slot, _ = chunk
        index = tuple(bit_index.get(bit, slice(None)) for bit in reversed(range(bits)))
        width = arrays[which][1]
        columns = pl.ds(lead, width if span is None else span)
        return kept[which].at[(slot, chip) + index + (slice(None), columns)]

    def copy(src, dst, number, kind, to_win, to_seq):
        return pltpu.make_async_remote_copy(
            src_ref=src,
            dst_ref=dst,
            send_sem=send_sem.at[number, kind],
            recv_sem=recv_sem.at[number, kind],
            device_id=(to_win, to_seq),
            device_id_type=pl.DeviceIdType.MESH,
        )

    def core_stage(chunk, number):
        which, slot, _ = chunk
        width = arrays[which][1]
        product = isinstance(sources[which], tuple)
        held = ring[which].at[slot % spacing]
        columns = (slice(None),) * bits + (slice(None), pl.ds(slot * width, width))
        if product:
            leaving, own = held.at[:, 1 - core], held.at[:, core]
        else:
            leaving, own = sources[which].at[(slice(None), 1 - core) + columns], held
        kind = 2 * chip_steps + 2 * bits
        item = copy(leaving, kept[which].at[slot], number, kind, win ^ 1, seq)
        if not product:
            placed = pltpu.make_async_copy(
                sources[which].at[(slice(None), core) + columns], held, local_sem.at[number]
            )

        def start():
            if product:
                left, right = sources[which]
                grad = lax.dot_general(
                    left[...],
                    right[:, pl.ds(slot * width, width)],
                    (((0,), (0,)), ((), ())),
                    preferred_element_type=single,
                )
                held[...] = grad.astype(bfloat).reshape(held.shape)
            else:
                placed.start()
            item.start()

        def arrive():
            if not product:
                placed.wait()
            item.wait_recv()
            add(kept[which].at[slot], own)
            item.wait_send()

        return start, arrive, lambda: None

    def bit_stage(chunk, number, step, chip):
        which, slot, _ = chunk
        half = arrays[which][1] // 2
        items = []
        for part in range(2):
            order = list(range(bits)) if part else list(reversed(range(bits)))
            bit = order[step]
            done = {b: own_seq[b] for b in order[:step]}
            kind = 2 * chip_steps + part * bits + step
            buffer = from_bits[which * bits + step]
            target = buffer.at[(slot, part) if isinstance(chip, slice) else (slot, part, 0)]
            leaving = slabs(chunk, chip, done | {bit: 1 - own_seq[bit]}, part * half, half)
            staying = slabs(chunk, chip, done | {bit: own_seq[bit]}, part * half, half)
            sent = copy(leaving, target, number, kind, win, seq ^ (1 << bit))
            items.append((sent, staying, target))

        def start():
            for sent, _, _ in items:
                sent.start()

        def arrive():
            for sent, staying, target in items:
                sent.wait_recv()
                add(staying, target)

        def finish():
            for sent, _, _ in items:
                sent.wait_send()

        return start, arrive, finish

    def chip_stage(chunk, number, step, bit_index):
        which, slot, lines_last = chunk
        part = (0,) * bits if lines_last else ()
        up_to, down_to = here + step, here - step
        up_slot = from_chips[which].at[(slot, step - 1) + part]
        down_slot = from_chips[which].at[(slot, chip_steps + step - 1) + part]
        up = copy(
            slabs(chunk, jnp.minimum(up_to, chips - 1), bit_index),
            up_slot,
            number,
            step - 1,
            win + CORES,
            seq,
        )
        down = copy(
            slabs(chunk, jnp.maximum(down_to, 0), bit_index),
            down_slot,
            number,
            chip_steps + step - 1,
            win - CORES,
            seq,
        )
        sends_up, sends_down = up_to < chips, down_to >= 0
        gets_up = (here >= 1) & (here - 1 + step < chips)
        gets_down = (here + 1 < chips) & (here + 1 - step >= 0)

        def start():
            pl.when(sends_up)(up.start)
            pl.when(sends_down)(down.start)

        def arrive():
            @pl.when(gets_up)
            def _():
                up.wait_recv()
                add(slabs(chunk, jnp.minimum(here + step - 1, chips - 1), bit_index), up_slot)

            @pl.when(gets_down)
            def _():
                down.wait_recv()
                add(slabs(chunk, jnp.maximum(here - step + 1, 0), bit_index), down_slot)

        def finish():
            pl.when(sends_up)(up.wait_send)
            pl.when(sends_down)(down.wait_send)

        return start, arrive, finish

    def stages(chunk, number):
        steps = range(chip_steps, 0, -1)
        if chunk[2]:
            cube = [bit_stage(chunk, number, step, slice(None)) for step in range(bits)]
            line = [chip_stage(chunk, number, step, own_seq) for step in steps]
            return [core_stage(chunk, number)] + cube + line
        line = [chip_stage(chunk, number, step, {}) for step in steps]
        cube = [bit_stage(chunk, number, step, here) for step in range(bits)]
        return [core_stage(chunk, number)] + line + cube

    def last(number):
        chunk = plan[number]
        which, slot, _ = chunk
        width = arrays[which][1]
        total = slabs(chunk, here, own_seq)[...].astype(single)
        outs[which][:, pl.ds(slot * width, width)] = total

    return [stages(chunk, number) for number, chunk in enumerate(plan)], last


def scatter_plan(grads, widths, lines_last):
    devices = lax.axis_size("win") * lax.axis_size("seq")
    plan, arrays = [], []
    for which, (grad, width) in enumerate(zip(grads, widths)):
        if isinstance(grad, tuple):
            rows, cols = grad[0].shape[1] // devices, grad[1].shape[1]
        else:
            rows, cols = grad.shape[-2:]
        slots = cols // width
        lasts = [lines_last(len(plan) + slot) for slot in range(slots)]
        plan += [(which, slot, last) for slot, last in enumerate(lasts)]
        arrays.append((rows, width, slots, isinstance(grad, tuple)))
    return tuple(plan), tuple(arrays)


def scatter_scratch(plan, arrays, spacing):
    chips = lax.axis_size("win") // CORES
    bits = lax.axis_size("seq").bit_length() - 1
    cube = (2,) * bits
    ring, kept, from_bits, from_chips = [], [], [], []
    for which, (rows, width, slots, product) in enumerate(arrays):
        halves = (CORES,) if product else ()
        ring.append(pltpu.VMEM((spacing, chips) + halves + cube + (rows, width), bfloat))
        kept.append(pltpu.VMEM((slots, chips) + cube + (rows, width), bfloat))
        for step in range(bits):
            left = (2,) * (bits - 1 - step)
            from_bits.append(pltpu.VMEM((slots, 2, chips) + left + (rows, width // 2), bfloat))
        lone = (1,) * bits if all(c[2] for c in plan if c[0] == which) else cube
        from_chips.append(pltpu.VMEM((slots, 2 * (chips - 1)) + lone + (rows, width), bfloat))
    kinds = 2 * (chips - 1) + 2 * bits + 1
    dma = pltpu.SemaphoreType.DMA
    sems = [dma((len(plan), kinds)), dma((len(plan), kinds)), dma((len(plan),))]
    return ring + kept + from_bits + from_chips + sems


def flat_sources(grads):
    flat, specs = [], []
    for grad in grads:
        whole = isinstance(grad, tuple)
        flat += grad if whole else (grad,)
        specs += [pl.BlockSpec(memory_space=pltpu.VMEM if whole else pl.ANY)] * (2 if whole else 1)
    return flat, specs


def group_sources(arrays, refs):
    sources = []
    for _, _, _, product in arrays:
        sources.append((refs[0], refs[1]) if product else refs[0])
        refs = refs[2 if product else 1 :]
    return sources, refs


def scatter_kernel(plan, arrays, spacing, *refs):
    count = len(arrays)
    sources, refs = group_sources(arrays, refs)
    start_together()
    work, last = scatter_work(plan, arrays, spacing, (sources, refs[:count], refs[count:]))
    for turn in range(turns_of(work, spacing)):
        run_turn(work, spacing, turn, last)
    finish_sends(work)


def scatter_all(grads, widths, lines_last, spacing, collective_id):
    plan, arrays = scatter_plan(grads, widths, lines_last)
    flat, specs = flat_sources(grads)
    return pl.pallas_call(
        functools.partial(scatter_kernel, plan, arrays, spacing),
        in_specs=specs,
        out_specs=[pl.BlockSpec(memory_space=pltpu.VMEM)] * len(grads),
        out_shape=[jax.ShapeDtypeStruct((a[0], a[1] * a[2]), single) for a in arrays],
        scratch_shapes=scatter_scratch(plan, arrays, spacing),
        compiler_params=pltpu.CompilerParams(
            collective_id=collective_id, has_side_effects=True, vmem_limit_bytes=VMEM_LIMIT
        ),
    )(*flat)


def scatter_and_widen_kernel(plan, arrays, spacing, first_turn, cols, *refs):
    count = len(arrays)
    sources, refs = group_sources(arrays, refs)
    (weights, activation, hidden_in, bias), refs = refs[:4], refs[4:]
    outs, layer_out, ring, load_sem, *refs = refs[:count], *refs[count:]
    pieces = layer_out.shape[1] // cols
    lead = (slice(None),) * (len(ring.shape) - 2)
    loads = [
        pltpu.make_async_copy(
            weights.at[lead + (pl.ds(piece * cols, cols),)], ring.at[piece % 2], load_sem.at[piece]
        )
        for piece in range(pieces)
    ]
    for load in loads[:2]:
        load.start()
    start_together()
    work, last = scatter_work(plan, arrays, spacing, (sources, outs, refs))
    for turn in range(turns_of(work, spacing)):
        run_turn(work, spacing, turn, last)
        piece = turn - first_turn
        if 0 <= piece < pieces:
            loads[piece].wait()
            columns = pl.ds(piece * cols, cols)
            w = ring[piece % 2].reshape(activation.shape[1], cols)
            out = jnp.dot(activation[...], w, preferred_element_type=single)
            out = hidden_in[:, columns] + out + bias[:, columns]
            layer_out[:, columns] = out.astype(bfloat)
            if piece + 2 < pieces:
                loads[piece + 2].start()
    finish_sends(work)


def scatter_and_widen(grads, widths, lines_last, spacing, first_turn, layer_ins, collective_id):
    weights, activation, hidden_in, _ = layer_ins
    cols = 256
    plan, arrays = scatter_plan(grads, widths, lines_last)
    flat, specs = flat_sources(grads)
    vmem = pl.BlockSpec(memory_space=pltpu.VMEM)
    return pl.pallas_call(
        functools.partial(scatter_and_widen_kernel, plan, arrays, spacing, first_turn, cols),
        in_specs=specs + [pl.BlockSpec(memory_space=pl.ANY), vmem, vmem, vmem],
        out_specs=[vmem] * (len(arrays) + 1),
        out_shape=[jax.ShapeDtypeStruct((a[0], a[1] * a[2]), single) for a in arrays]
        + [jax.ShapeDtypeStruct(hidden_in.shape, bfloat)],
        scratch_shapes=[
            pltpu.VMEM((2,) + weights.shape[:-1] + (cols,), bfloat),
            pltpu.SemaphoreType.DMA((hidden_in.shape[1] // cols,)),
        ]
        + scatter_scratch(plan, arrays, spacing),
        compiler_params=pltpu.CompilerParams(
            collective_id=collective_id, has_side_effects=True, vmem_limit_bytes=VMEM_LIMIT
        ),
    )(*flat, *layer_ins)


def attend_back_kernel(plan, arrays, spacing, block_turns, dims, *refs):
    hp, vd, bq = dims
    count = len(arrays)
    sources, refs = group_sources(arrays, refs)
    (leaving_ref, x_ref, tab_ref, att_in), refs = refs[:4], refs[4:]
    outs, (returned, dtab_ref, bias_ref), refs = refs[:count], refs[count : count + 3], refs[count + 3 :]
    gm_ref, ret_ref, att_ref, dk_ref, dv_ref, *scatter_refs = refs[:-7]
    in_send, in_recv, in_local, out_send, out_recv, out_local, att_sem = refs[-7:]
    length = x_ref.shape[0]
    hk = hp * KD
    peers, rows = leaving_ref.shape[:2]
    blocks = length // bq
    incoming = exchange_work(
        [leaving_ref.at[peer] for peer in range(peers)],
        lambda peer: gm_ref.at[pl.ds(peer * rows, rows)],
        in_send,
        in_recv,
        in_local,
    )
    leaving = exchange_work(
        [ret_ref.at[pl.ds(peer * rows, rows)] for peer in range(peers)],
        lambda peer: returned.at[peer],
        out_send,
        out_recv,
        out_local,
    )
    loads = [
        pltpu.make_async_copy(
            att_in.at[:, pl.ds(block * bq, bq)], att_ref.at[block % 2], att_sem.at[block]
        )
        for block in range(blocks)
    ]
    for load in loads[:2]:
        load.start()
    start_together(True)
    for start, _, _ in incoming:
        start()
    work, last = scatter_work(plan, arrays, spacing, (sources, outs, scatter_refs))
    dk_ref[...] = jnp.zeros_like(dk_ref)
    dv_ref[...] = jnp.zeros_like(dv_ref)
    dtab_ref[...] = jnp.zeros_like(dtab_ref)
    bias_ref[...] = jnp.zeros_like(bias_ref)
    for turn in range(turns_of(work, spacing)):
        run_turn(work, spacing, turn, last)
        for block in range(blocks):
            if block_turns[block] != turn:
                continue
            if block == 0:
                for _, arrive, _ in incoming:
                    arrive()
            loads[block].wait()
            attend_back(
                length,
                bq,
                hp,
                vd,
                block,
                x_ref,
                tab_ref,
                att_ref.at[block % 2],
                gm_ref,
                ret_ref,
                (dk_ref, dv_ref, dtab_ref, bias_ref),
            )
            if block + 2 < blocks:
                loads[block + 2].start()
            if block == blocks - 1:
                ret_ref[:, hk : 2 * hk] = dk_ref[...].T.astype(bfloat)
                ret_ref[:, 2 * hk :] = dv_ref[...].T.astype(bfloat)
                for start, _, _ in leaving:
                    start()
    for _, arrive, _ in leaving:
        arrive()
    for _, _, finish in incoming + leaving:
        finish()
    finish_sends(work)


def scatter_and_attend_back(
    grads, widths, lines_last, spacing, block_turns, leaving, x, tab, attention, dims
):
    hp, vd, bq = dims
    peers, rows, _ = leaving.shape
    length = peers * rows
    hk = hp * KD
    back = 2 * hk + hp * vd
    plan, arrays = scatter_plan(grads, widths, lines_last)
    flat, specs = flat_sources(grads)
    anywhere = pl.BlockSpec(memory_space=pl.ANY)
    vmem = pl.BlockSpec(memory_space=pltpu.VMEM)
    dma = pltpu.SemaphoreType.DMA
    return pl.pallas_call(
        functools.partial(attend_back_kernel, plan, arrays, spacing, block_turns, dims),
        in_specs=specs + [anywhere, vmem, vmem, anywhere],
        out_specs=[vmem] * len(grads) + [anywhere, vmem, vmem],
        out_shape=[jax.ShapeDtypeStruct((a[0], a[1] * a[2]), single) for a in arrays]
        + [
            jax.ShapeDtypeStruct((peers, rows, back), bfloat),
            jax.ShapeDtypeStruct(tab.shape, single),
            jax.ShapeDtypeStruct((8, hk), single),
        ],
        scratch_shapes=[
            pltpu.VMEM((length, hp * vd), bfloat),
            pltpu.VMEM((length, back), bfloat),
            pltpu.VMEM((2, hp, bq, length), bfloat),
            pltpu.VMEM((hk, length), single),
            pltpu.VMEM((hp * vd, length), single),
        ]
        + scatter_scratch(plan, arrays, spacing)
        + [dma((peers,))] * 6
        + [dma((length // bq,))],
        compiler_params=pltpu.CompilerParams(
            collective_id=2, has_side_effects=True, vmem_limit_bytes=VMEM_LIMIT
        ),
    )(*flat, leaving, x, tab, attention)


def shards(
    inputs,
    cotangent,
    ln1_scale,
    ln1_offset,
    w_query,
    w_key,
    w_value,
    w_rel,
    content_bias,
    position_bias,
    w_out,
    b_out,
    ln2_scale,
    ln2_offset,
    w_in,
    b_in,
    w_mlp_out,
    b_mlp_out,
):
    win_size, seq_size = lax.axis_size("win"), lax.axis_size("seq")
    devices = win_size * seq_size
    seq = lax.axis_index("seq")
    window_count, row_count, width = inputs.shape
    tokens = window_count * row_count
    hk = HEADS * KD
    vd = width // HEADS
    hp = HEADS // seq_size
    hidden = w_in.shape[1]
    scale_factor = KD ** (-0.5)

    wide = (ln1_scale, ln1_offset, b_out, ln2_scale, ln2_offset, b_mlp_out)
    narrow = (content_bias, position_bias)
    packed = jnp.concatenate(wide + (b_in,) + narrow + (w_rel.T.reshape(-1),))
    cuts = [len(wide) * ln1_scale.shape[0]]
    cuts.append(cuts[0] + b_in.shape[0])
    cuts.append(cuts[1] + len(narrow) * content_bias.shape[0])
    packed_size = packed.shape[0]
    small_cols = -(-packed_size // 4096) * 256
    small_size = 16 * small_cols
    packed = jnp.pad(packed, (0, small_size - packed_size)).reshape(16, small_cols)
    packed, whole_qk, whole_v = gather_all(
        (packed, jnp.concatenate([w_query, w_key], axis=1), w_value),
        (256, 512, 512),
        lambda number: number % 3 != 2,
        3,
        0,
    )
    packed = packed.reshape(devices, small_size)
    whole_qk = whole_qk.reshape(width, 2 * hk)
    whole_v = whole_v.reshape(width, width)

    def rows_of(columns, count):
        rows = columns.reshape(devices, count, -1).transpose(1, 0, 2)
        return rows.reshape(count, -1).astype(single)

    wide_rows = rows_of(packed[:, : cuts[0]], len(wide))
    ln1_gain, ln1_shift, bias_out, ln2_gain, ln2_shift, bias_mlp = wide_rows
    bias_in = packed[:, cuts[0] : cuts[1]].reshape(-1).astype(single)
    bias_content, bias_position = rows_of(packed[:, cuts[1] : cuts[2]], len(narrow))
    whole_rel = packed[:, cuts[2] : packed_size].reshape(hk, F)

    features = jnp.pad(rel_features(WLEN, F).astype(bfloat), ((0, 1), (0, 0)))
    own_rel = lax.dynamic_slice_in_dim(whole_rel, seq * hp * KD, hp * KD, 0)
    table = jnp.einsum("cf,tf->ct", own_rel, features, preferred_element_type=single).astype(bfloat)

    source = inputs.reshape(tokens, width).astype(single)
    normed_one_f, norm_one_back = jax.vjp(layer_norm, source, ln1_gain, ln1_shift)
    normed_one = normed_one_f.astype(bfloat)
    proj_qk = jnp.dot(normed_one, whole_qk, preferred_element_type=single)
    query = proj_qk[:, :hk] * scale_factor
    proj_v = jnp.dot(normed_one, whole_v, preferred_element_type=single)
    parts = (
        (query + bias_content).astype(bfloat),
        (query + bias_position).astype(bfloat),
        proj_qk[:, hk:].astype(bfloat),
        proj_v.astype(bfloat),
    )
    outgoing = jnp.concatenate([part.reshape(tokens, seq_size, -1) for part in parts], axis=2)
    outgoing = jnp.transpose(outgoing, (1, 0, 2))
    in_kernel = w_out.shape[0] % 16 == 0 and hp * vd % 128 == 0
    row_vectors = wide_rows[2:]
    cot_rows = cotangent.reshape(tokens, width)
    first_results, ffn_results = gather_and_attend(
        (w_out, w_mlp_out, w_in),
        (512, 256, 512),
        lambda number: number % 3 != 1,
        3,
        FIRST_BLOCK_TURN,
        outgoing,
        table,
        (inputs.reshape(tokens, width), cot_rows, row_vectors, bias_in[None, :]),
        (hp, vd, BLOCK_Q, in_kernel),
    )
    whole_out, gathered_mlp, whole_in, heads_in, attention = first_results
    whole_out = whole_out.reshape(width, width)
    whole_in = whole_in.reshape(width, hidden)
    whole_mlp = gathered_mlp.reshape(hidden, width)
    if in_kernel:
        attended, hidden_in, normed_two, activation, grad_pre = ffn_results
    else:
        attended = jnp.transpose(ffn_results[0], (1, 0, 2)).reshape(tokens, width)
        branch = jnp.dot(attended, whole_out, preferred_element_type=single)
        hidden_in = source + branch + bias_out
        normed_two = layer_norm(hidden_in, ln2_gain, ln2_shift).astype(bfloat)
        pre_act = jnp.dot(normed_two, whole_in, preferred_element_type=single) + bias_in
        gelu_out, gelu_back = jax.vjp(jax.nn.gelu, pre_act)
        activation = gelu_out.astype(bfloat)
        result = hidden_in + jnp.dot(activation, whole_mlp, preferred_element_type=single)
        result = (result + bias_mlp).astype(bfloat)
        grad_act = jnp.einsum("td,fd->tf", cot_rows, whole_mlp, preferred_element_type=single)
        grad_pre = gelu_back(grad_act)[0].astype(bfloat)

    grid = (win_size // CORES, CORES) + (2,) * (seq_size.bit_length() - 1)

    def weight_grad(left, right):
        if left.shape[1] // devices % 16 == 0:
            return left, right
        grad = jnp.einsum("td,te->de", left, right, preferred_element_type=single).astype(bfloat)
        rows, cols = grad.shape
        return grad.reshape(grid + (rows // devices, cols))

    grad_mlp = weight_grad(activation, cot_rows)
    grad_bias_mlp = jnp.sum(cot_rows.astype(single), axis=0)
    grad_in = weight_grad(normed_two, grad_pre)
    grad_bias_in = jnp.sum(grad_pre.astype(single), axis=0)
    grad_normed_two = jnp.einsum("tf,df->td", grad_pre, whole_in, preferred_element_type=single)
    _, norm_two_back = jax.vjp(layer_norm, hidden_in, ln2_gain, ln2_shift)
    hidden_term, grad_ln2_gain, grad_ln2_shift = norm_two_back(grad_normed_two)
    grad_hidden = cot_rows.astype(single) + hidden_term
    grad_branch = grad_hidden.astype(bfloat)
    grad_out = weight_grad(attended, grad_branch)
    grad_bias_out = jnp.sum(grad_branch.astype(single), axis=0)
    grad_mixed = jnp.einsum(
        "te,de->td", grad_branch, whole_out, preferred_element_type=single
    ).astype(bfloat)
    grad_mixed = jnp.transpose(grad_mixed.reshape(tokens, seq_size, hp * vd), (1, 0, 2))
    grad_mlp, grad_in, returned, grad_table, grad_bias = scatter_and_attend_back(
        (grad_mlp, grad_in),
        (256, 512),
        lambda number: number % 4 != 0,
        2,
        BLOCK_TURNS,
        grad_mixed,
        heads_in,
        table,
        attention,
        (hp, vd, BLOCK_Q),
    )
    own = hp * KD
    returned = jnp.transpose(returned, (1, 0, 2))
    grad_qk_rows = jnp.concatenate(
        [
            returned[:, :, :own].reshape(tokens, hk),
            returned[:, :, own : 2 * own].reshape(tokens, hk),
        ],
        axis=1,
    )
    grad_v_rows = returned[:, :, 2 * own :].reshape(tokens, width)
    grad_qk = weight_grad(normed_one, grad_qk_rows)
    grad_v = weight_grad(normed_one, grad_v_rows)
    grad_normed_one = jnp.einsum(
        "tk,dk->td", grad_qk_rows, whole_qk, preferred_element_type=single
    ) + jnp.einsum("tk,dk->td", grad_v_rows, whole_v, preferred_element_type=single)
    source_term, grad_ln1_gain, grad_ln1_shift = norm_one_back(grad_normed_one)
    grad_inputs = (grad_hidden + source_term).reshape(inputs.shape)

    grad_rel = jnp.dot(grad_table, features.astype(single), precision=lax.Precision.HIGHEST)
    whole_grad_rel = lax.dynamic_update_slice_in_dim(
        jnp.zeros((hk, F), single), grad_rel, seq * own, 0
    )

    wide_grads = jnp.stack(
        [
            grad_ln1_gain,
            grad_ln1_shift,
            grad_bias_out,
            grad_ln2_gain,
            grad_ln2_shift,
            grad_bias_mlp,
        ]
    )
    narrow_grads = lax.dynamic_update_slice_in_dim(
        jnp.zeros((len(narrow), hk), single), grad_bias[: len(narrow)], seq * own, 1
    )

    def by_owner(rows):
        count = rows.shape[0]
        return rows.reshape(count, devices, -1).transpose(1, 0, 2).reshape(devices, -1)

    small = jnp.concatenate(
        [
            by_owner(wide_grads),
            grad_bias_in.reshape(devices, -1),
            by_owner(narrow_grads),
            whole_grad_rel.reshape(devices, -1),
        ],
        axis=1,
    )
    small = jnp.pad(small, ((0, 0), (0, small_size - packed_size))).astype(bfloat)
    final = (grad_out, grad_qk, grad_v, small.reshape(grid + (16, small_cols)))
    cuts_of = (512, 512, 512, 256)
    if in_kernel:
        layer_ins = (gathered_mlp, activation, hidden_in, row_vectors[3:4])
        grad_out, grad_qk, grad_v, small, result = scatter_and_widen(
            final, cuts_of, lambda number: number % 4 != 0, 2, 3, layer_ins, 3
        )
    else:
        grad_out, grad_qk, grad_v, small = scatter_all(
            final, cuts_of, lambda number: number % 4 != 0, 2, 3
        )
    layer_out = result.reshape(inputs.shape)
    small = small.reshape(-1)[:packed_size]
    wide_own = small[: cuts[0]].reshape(len(wide), -1)
    narrow_own = small[cuts[1] : cuts[2]].reshape(len(narrow), -1)
    own_grad_rel = small[cuts[2] :].reshape(-1, F).T
    return (
        layer_out,
        grad_inputs,
        wide_own[0],
        wide_own[1],
        grad_qk[:, :hk],
        grad_qk[:, hk:],
        grad_v,
        own_grad_rel,
        narrow_own[0],
        narrow_own[1],
        grad_out,
        wide_own[2],
        wide_own[3],
        wide_own[4],
        grad_in,
        small[cuts[0] : cuts[1]],
        grad_mlp,
        wide_own[5],
    )


def solution(mesh):
    in_specs = (
        P("win", "seq", None),
        P("win", "seq", None),
        P(("win", "seq")),
        P(("win", "seq")),
        P(("win", "seq"), None),
        P(("win", "seq"), None),
        P(("win", "seq"), None),
        P(None, ("win", "seq")),
        P(("win", "seq")),
        P(("win", "seq")),
        P(("win", "seq"), None),
        P(("win", "seq")),
        P(("win", "seq")),
        P(("win", "seq")),
        P(("win", "seq"), None),
        P(("win", "seq")),
        P(("win", "seq"), None),
        P(("win", "seq")),
    )
    out_specs = (
        P("win", "seq", None),
        P("win", "seq", None),
        P(("win", "seq")),
        P(("win", "seq")),
        P(("win", "seq"), None),
        P(("win", "seq"), None),
        P(("win", "seq"), None),
        P(None, ("win", "seq")),
        P(("win", "seq")),
        P(("win", "seq")),
        P(("win", "seq"), None),
        P(("win", "seq")),
        P(("win", "seq")),
        P(("win", "seq")),
        P(("win", "seq"), None),
        P(("win", "seq")),
        P(("win", "seq"), None),
        P(("win", "seq")),
    )
    return jax.shard_map(shards, mesh=mesh, in_specs=in_specs, out_specs=out_specs, check_vma=False)
```
